32 devices in a mesh: feat: 4 (over y, core), node: 8 (over z, x).
Axes of the slice: x: 2, y: 2, z: 4, core: 2. Of those that a mesh axis runs over, the one named last changes fastest.
Arguments:
- node_feats: float32 [256, 32768], P('feat', 'node'), may hold values from -6 to 6
- tiles: float32 [64, 16, 128, 128], P('node'), may hold values from -0.5 to 0.5
- send_col: int32 [64, 16], P('node'), may hold values from 0 to 31
- recv_row: int32 [64, 16], P('node'), may hold values from -1 to 31, as said below
- degree: int32 [32768], P('node'), may hold values from 1 to 8
- w_self: float32 [256, 256], replicated, may hold values from -0.375 to 0.375
- w_neigh: float32 [256, 256], replicated, may hold values from -0.375 to 0.375
- bias: float32 [256], replicated, may hold values from -3 to 3
- cotangent: float32 [32768, 256], P(('node', 'feat')), may hold values from -6 to 6
Outputs:
- activated: float32 [32768, 256], P(('node', 'feat'))
- grad_feats: float32 [256, 32768], P('feat', 'node')
- grad_self: float32 [256, 256], replicated
- grad_neigh: float32 [256, 256], replicated
- grad_bias: float32 [256], replicated
The draws below stay inside these ranges and needn't reach their ends.
Inputs may be any that keep to these rules, and one draw needn't show every extreme that they name: `recv_row`: at most 16 live slots from one sender to one owner; every sender fills all 16 slots to itself, and one owner receives 16 live slots from every sender; -1 marks an empty slot.
All inputs are finite; a program needn't handle non-finite values.
Results may differ from the reference program's by a relative error of at most 0.0003.
Values sent between devices are 32-bit elements; how exact they have to be, the bound alone decides.
No kernel may reach another device: no remote copies, remote signals or barrier semaphores. Data moves between devices by JAX's collectives and lax.ppermute only.
A program may use at most 64 MiB of HBM per device.

```python
import jax
import jax.numpy as jnp
from jax import lax

H = 256
TB = 128
BLK_DEV = 32
CAP = 16
NODES = 32768
N_NODE = 8


def slot_rows(key):
    hot_owner = jax.random.randint(jax.random.fold_in(key, 11), (), 0, N_NODE)
    counts = jax.random.randint(jax.random.fold_in(key, 12), (N_NODE, N_NODE), 0, CAP + 1)
    senders = jnp.arange(N_NODE, dtype=jnp.int32)[:, None]
    owners = jnp.arange(N_NODE, dtype=jnp.int32)[None, :]
    filled = jnp.logical_or(owners == hot_owner, senders == owners)
    counts = jnp.where(filled, CAP, counts)
    live = jnp.arange(CAP, dtype=jnp.int32)[None, None, :] < counts[..., None]
    blocks = jax.random.randint(jax.random.fold_in(key, 13), (N_NODE, N_NODE, CAP), 0, BLK_DEV)
    return jnp.where(live, blocks, -1)


def draw_recv_row(key, part):
    layout = slot_rows(key)
    return layout.transpose(1, 0, 2).reshape(N_NODE * N_NODE, CAP).astype(jnp.int32)


def draw_send_col(key, part):
    key = jax.random.fold_in(key, 5)
    return jax.random.randint(key, (N_NODE * N_NODE, CAP), 0, BLK_DEV).astype(jnp.int32)


def place_ends(result, stream_key, low, high):
    place = [jax.random.randint(jax.random.fold_in(stream_key, axis), (), 0, length) for axis, length in enumerate(result.shape)]
    main_axis = result.shape.index(max(result.shape))
    beside = place[:main_axis] + [(place[main_axis] + 1) % result.shape[main_axis]] + place[main_axis + 1:]
    return result.at[tuple(place)].set(low).at[tuple(beside)].set(high)


def spiked(entries, own_key, source, target, blocks, factor):
    def block_of(position):
        return (jnp.arange(entries.shape[position]) // (entries.shape[position] // blocks)).reshape((-1,) + (1,) * (entries.ndim - 1 - position))

    near = jax.random.permutation(own_key, blocks)[block_of(target)]
    other_side = (block_of(target) + blocks // 2) % blocks
    return jnp.where((block_of(source) == near) | (block_of(source) == other_side), factor * entries, entries)


def level_of(stream_key, extent, cuts, smallest, high):
    factor_of, own = 1.0, jax.random.fold_in(stream_key, 6)
    for dim, blocks in cuts:
        steps = jnp.exp(jax.random.uniform(jax.random.fold_in(own, dim), (blocks,), jnp.float32, smallest / len(cuts), high / len(cuts)))
        factor_of = factor_of * jnp.repeat(steps, extent[dim] // blocks).reshape([-1 if axis == dim else 1 for axis in range(len(extent))])
    return factor_of


def noise(own_key, extent, spread, most, cuts=(), held_as=jnp.bfloat16):
    values = spread * jax.random.normal(own_key, extent, jnp.float32)
    if cuts:
        values = values * level_of(own_key, extent, cuts, -0.22, 0.18)
    return jnp.clip(values, -most, most).astype(held_as)


def gaussian_with(key, extent, width, reach, cuts, heavy, kind=jnp.bfloat16):
    values = width * jax.random.normal(key, extent, jnp.float32)
    if cuts:
        values = values * level_of(key, extent, cuts, -0.22, 0.18)
    return jnp.clip(spiked(values, jax.random.fold_in(key, 3), *heavy), -reach, reach).astype(kind)


def setup_inputs(seed: int = 0) -> dict:
    key_list = jax.random.split(jax.random.key(seed), 10)
    node_feats = noise(key_list[0], (H, NODES), 1.0, 6.0, ((0, 4), (1, 8)), jnp.float32)
    tiles = noise(key_list[1], (N_NODE * N_NODE, CAP, TB, TB), TB ** -0.5, 0.5, ((0, 8),), jnp.float32)
    send_col = draw_send_col(jax.random.fold_in(key_list[9], 71), 0)
    recv_row = draw_recv_row(jax.random.fold_in(key_list[9], 71), 0)
    degree = place_ends(jax.random.randint(key_list[4], (NODES,), 1, 9), jax.random.fold_in(key_list[4], 1), 1, 8).astype(jnp.int32)
    w_self = noise(key_list[5], (H, H), H ** -0.5, 0.375, (), jnp.float32)
    w_neigh = noise(key_list[6], (H, H), H ** -0.5, 0.375, (), jnp.float32)
    bias = noise(key_list[7], (H,), 0.5, 3.0, (), jnp.float32)
    cotangent = gaussian_with(key_list[8], (NODES, H), 1.0, 6.0, ((0, 32),), (0, 1, 32, 2.75), jnp.float32)
    return {"node_feats": node_feats, "tiles": tiles, "send_col": send_col, "recv_row": recv_row, "degree": degree, "w_self": w_self, "w_neigh": w_neigh, "bias": bias, "cotangent": cotangent}


def aggregate(node_feats, tiles, send_col, recv_row, degree):
    feat_blocks = node_feats.reshape(H, N_NODE, BLK_DEV, TB)
    sender_rows = recv_row.reshape(N_NODE, N_NODE, CAP).transpose(1, 0, 2)
    sender_cols = send_col.reshape(N_NODE, N_NODE, CAP)
    tile_grid = tiles.reshape(N_NODE, N_NODE, CAP, TB, TB)
    block_ids = jnp.arange(BLK_DEV, dtype=jnp.int32)

    def sender_step(totals, source):
        local = feat_blocks[:, source]
        col_onehot = (sender_cols[source][..., None] == block_ids).astype(jnp.float32)
        picked = jnp.einsum('dcb,hbj->dchj', col_onehot, local, precision=lax.Precision.HIGHEST)
        partial_value = jnp.einsum('dchj,dcij->dchi', picked, tile_grid[source], precision=lax.Precision.HIGHEST)
        row_onehot = (sender_rows[source][..., None] == block_ids).astype(jnp.float32)
        added = jnp.einsum('dchi,dcb->dhbi', partial_value, row_onehot, precision=lax.Precision.HIGHEST)
        return (totals + added, None)
    start_totals = jnp.zeros((N_NODE, H, BLK_DEV, TB), jnp.float32)
    totals, unused = lax.scan(sender_step, start_totals, jnp.arange(N_NODE, dtype=jnp.int32))
    summed = totals.transpose(1, 0, 2, 3).reshape(H, N_NODE * BLK_DEV * TB)
    return summed / degree.astype(jnp.float32)[None, :]

def reference(node_feats, tiles, send_col, recv_row, degree, w_self, w_neigh, bias, cotangent):

    def forward(feats, wself, wneigh, shift):
        neighbour = aggregate(feats, tiles, send_col, recv_row, degree)
        pre = jnp.dot(feats.T, wself, precision=lax.Precision.HIGHEST)
        pre = pre + jnp.dot(neighbour.T, wneigh, precision=lax.Precision.HIGHEST) + shift
        return jax.nn.silu(pre)
    activated, pullback = jax.vjp(forward, node_feats, w_self, w_neigh, bias)
    grads = pullback(cotangent)
    return (activated, grads[0], grads[1], grads[2], grads[3])
```

```python
import functools

import jax
import jax.numpy as jnp
from jax import lax
from jax.experimental import pallas as pl
from jax.experimental.pallas import tpu as pltpu
from jax.sharding import PartitionSpec as P

TB = 128
F32 = jnp.float32
BF16 = jnp.bfloat16
HIGH = lax.Precision.HIGH
CHUNKS = 2
VMEM_BYTES = 28 * 2**20

FAR_OUTER, FAR_INNER, NEAR, SELF = range(4)


def owner(role, z):
    if role == FAR_OUTER:
        return jnp.where(z < 2, 3, 0)
    if role == FAR_INNER:
        return jnp.where(z < 2, 2, 1)
    if role == NEAR:
        return z + 1 - 2 * (z % 2)
    return z


def owner_dynamic(role, z):
    return jnp.where(
        role == FAR_OUTER,
        owner(FAR_OUTER, z),
        jnp.where(role == FAR_INNER, owner(FAR_INNER, z), jnp.where(role == NEAR, owner(NEAR, z), z)),
    )


def split(value):
    high = value.astype(BF16)
    return high, (value - high.astype(F32)).astype(BF16)


def dot_nn(a, b):
    return lax.dot_general(a, b, (((1,), (0,)), ((), ())), preferred_element_type=F32)


def dot_nt(a, b):
    return lax.dot_general(a, b, (((1,), (1,)), ((), ())), preferred_element_type=F32)


def stacked(value):
    high, low = split(value)
    return jnp.concatenate(
        [jnp.concatenate([high, high], 1), jnp.concatenate([low, jnp.zeros_like(low)], 1)], 0
    )


def times_tile_t(value, tile):
    rows = value.shape[0]
    out = dot_nt(stacked(value), jnp.concatenate(split(tile), 1))
    return out[:rows] + out[rows:]


def times_tile(value, tile):
    rows = value.shape[0]
    out = dot_nn(stacked(value), jnp.concatenate(split(tile), 0))
    return out[:rows] + out[rows:]


def lanes(block):
    return pl.ds(pl.multiple_of(block * TB, TB), TB)


class Layer:
    def __init__(self, slices, owned, cap, parts, width):
        self.slices, self.owned, self.cap, self.parts, self.width = slices, owned, cap, parts, width
        self.blocks = owned // TB
        self.per_part = self.blocks // parts
        self.per_piece = self.per_part // CHUNKS
        self.per_chunk = self.blocks // CHUNKS
        self.piece_rows = self.per_piece * TB

    def spot(self, row):
        row = jnp.maximum(row, 0)
        part, inside = row // self.per_part, row % self.per_part
        return inside // self.per_piece, part * self.per_piece + inside % self.per_piece

    def block(self, chunk, part, inside):
        return part * self.per_part + chunk * self.per_piece + inside

    def full(self, *shape):
        return pl.BlockSpec(shape, lambda i, *_: (0,) * len(shape))

    def tile_spec(self, role, other):
        def where(i, place, *_):
            x = 1 - place[1] if other else place[1]
            return (owner(role, place[0]) * 2 + x, 0, 0, 0)

        return pl.BlockSpec((1, self.cap, TB, TB), where)

    def call(self, body, scalars, grid, in_specs, args, out_specs, out_shape, scratch=(), aliases=None, work=1):
        return pl.pallas_call(
            body,
            grid_spec=pltpu.PrefetchScalarGridSpec(
                num_scalar_prefetch=len(scalars),
                grid=grid,
                in_specs=in_specs,
                out_specs=out_specs,
                scratch_shapes=scratch,
            ),
            out_shape=out_shape,
            input_output_aliases=aliases or {},
            compiler_params=pltpu.CompilerParams(vmem_limit_bytes=VMEM_BYTES),
            cost_estimate=pl.CostEstimate(flops=work * 10**8, bytes_accessed=4 * 2**20, transcendentals=0),
        )(*scalars, *args)

    def slots(self):
        return jax.ShapeDtypeStruct((self.cap, self.slices, TB), F32)

    def dense(self):
        return jax.ShapeDtypeStruct((self.per_chunk, self.slices, TB), F32)

    def partial(self, role, place, cols, feats, tiles):
        def body(place, cols, feats, tile, out):
            owned_by = owner(role, place[0]) * 2 + 1 - place[1]
            for c in range(self.cap):
                out[c] = times_tile_t(feats[:, lanes(cols[owned_by * self.cap + c])], tile[0, c])

        return self.call(
            body, (place, cols), (1,),
            [self.full(self.slices, self.owned), self.tile_spec(role, True)], (feats, tiles),
            self.full(self.cap, self.slices, TB), self.slots(),
        )

    def local(self, place, cols, rows, feats, tiles):
        def where(i, place, *_):
            return (owner_dynamic(i, place[0]) * 2 + place[1], 0, 0, 0)

        def body(place, cols, rows, feats, tile, out):
            owned_by = owner_dynamic(pl.program_id(0), place[0]) * 2 + place[1]
            out[...] = jnp.zeros_like(out)
            for c in range(self.cap):
                row = rows[owned_by * self.cap + c]
                chunk, spot = self.spot(row)
                value = times_tile_t(feats[:, lanes(cols[owned_by * self.cap + c])], tile[0, c])
                out[0, chunk * self.per_chunk + spot] += jnp.where(row >= 0, value, 0.0)

        return self.call(
            body, (place, cols, rows), (4,),
            [self.full(self.slices, self.owned), pl.BlockSpec((1, self.cap, TB, TB), where)], (feats, tiles),
            pl.BlockSpec((1, self.blocks, self.slices, TB), lambda i, *_: (i, 0, 0, 0)),
            jax.ShapeDtypeStruct((4, self.blocks, self.slices, TB), F32), work=4,
        )

    def joined(self, role, place, rows, sums, slots):
        def body(place, rows, sums, slots, *outs):
            z, x = place[0], place[1]
            for k, out in enumerate(outs):
                out[...] = sums[0, k * self.per_chunk : (k + 1) * self.per_chunk]
            for c in range(self.cap):
                row = rows[(owner(role, z) * 2 + 1 - x) * self.cap + c]
                chunk, spot = self.spot(row)
                for k, out in enumerate(outs):
                    out[spot] += jnp.where((row >= 0) & (chunk == k), slots[c], 0.0)

        shape = (self.per_chunk, self.slices, TB)
        return self.call(
            body, (place, rows), (1,),
            [pl.BlockSpec((1, self.blocks, self.slices, TB), lambda i, *_: (role, 0, 0, 0)),
             self.full(self.cap, self.slices, TB)], (sums, slots),
            [self.full(*shape)] * CHUNKS, [self.dense()] * CHUNKS,
        )

    def project(self, k, place, pieces, feats, w_self, w_neigh, inverse):
        def body(place, own, near, inner, outer, feats, w_self, w_neigh, inverse, neighbour, send, keep):
            core = place[3]
            high, low = split(jnp.concatenate([w_self[...], w_neigh[...]], 0))
            twice = jnp.concatenate([high, high], 0)
            for y in range(2):
                for out, side in ((send, 1 - core), (keep, core)):
                    for j in range(self.per_piece):
                        part = 2 * y + side
                        spot, block = part * self.per_piece + j, self.block(k, part, j)
                        mean = (own[spot] + near[spot] + inner[spot] + outer[spot]) * inverse[pl.ds(block, 1), :]
                        neighbour[spot] = mean
                        both = jnp.concatenate([feats[:, lanes(block)], mean], 0).T
                        both_high, both_low = split(both)
                        out[y, j * TB : (j + 1) * TB, :] = dot_nn(
                            jnp.concatenate([both_high, both_low], 1), twice
                        ) + dot_nn(both_high, low)

        dense = self.full(self.per_chunk, self.slices, TB)
        share = jax.ShapeDtypeStruct((2, self.piece_rows, self.width), F32)
        return self.call(
            body, (place,), (1,),
            [dense] * 4 + [self.full(self.slices, self.owned)] + [self.weight_spec()] * 2 + [self.full(self.blocks, TB)],
            (*pieces, feats, w_self, w_neigh, inverse),
            [dense] + [self.full(2, self.piece_rows, self.width)] * 2, [self.dense(), share, share],
        )

    def weight_spec(self):
        return pl.BlockSpec((self.slices, self.width), lambda i, place, *_: (2 * place[2] + place[3], 0))

    def half_spec(self, other):
        return pl.BlockSpec(
            (1, self.piece_rows, self.width),
            lambda i, place, *_: (1 - place[2] if other else place[2], 0, 0),
        )

    def for_other_y(self, place, keep, got):
        def body(place, keep, got, out):
            out[...] = keep[0] + got[0]

        shape = (self.piece_rows, self.width)
        return self.call(
            body, (place,), (1,), [self.half_spec(True)] * 2, (keep, got),
            self.full(*shape), jax.ShapeDtypeStruct(shape, F32),
        )

    def activate(self, k, place, keep, got, far, bias, cotangent, activated):
        def body(place, keep, got, far, bias, cotangent, *rest):
            out, grad = rest[-2:]
            pre = keep[0] + got[0] + far[...] + bias[...]
            sigma = jax.nn.sigmoid(pre)
            out[...] = pre * sigma
            grad[...] = cotangent[...] * (sigma * (1.0 + pre * (1.0 - sigma)))

        shape = (self.piece_rows, self.width)
        rows = pl.BlockSpec(shape, lambda i, *_: (k, 0))
        in_specs = [self.half_spec(False)] * 2 + [self.full(*shape), self.full(1, self.width), rows]
        args = [keep, got, far, bias, cotangent]
        aliases = {}
        if activated is not None:
            aliases = {1 + len(args): 0}
            in_specs.append(pl.BlockSpec(memory_space=pl.ANY))
            args.append(activated)
        return self.call(
            body, (place,), (1,), in_specs, args, [rows, self.full(*shape)],
            [jax.ShapeDtypeStruct(cotangent.shape, F32), jax.ShapeDtypeStruct(shape, F32)], aliases=aliases,
        )

    def back(self, weight, grad):
        rows = weight.shape[0]
        high, low = split(weight)
        grad_high, grad_low = split(grad)
        out = dot_nt(jnp.concatenate([high, low], 0), grad_high)
        return out[:rows] + out[rows:] + dot_nt(high, grad_low)

    def parts_of(self, place, grads):
        y, core = place[2], place[3]
        return (
            (2 * y + core, grads[0]),
            (2 * (1 - y) + core, grads[1]),
            (2 * y + 1 - core, grads[2]),
            (2 * (1 - y) + 1 - core, grads[3]),
        )

    def neighbour_grad(self, k, place, w_neigh, inverse, grads):
        def body(place, w_neigh, inverse, *rest):
            out = rest[-1]
            for part, grad in self.parts_of(place, rest[:-1]):
                value = self.back(w_neigh[...], grad[...])
                for j in range(self.per_piece):
                    block = self.block(k, part, j)
                    out[part * self.per_piece + j] = value[:, j * TB : (j + 1) * TB] * inverse[pl.ds(block, 1), :]

        return self.call(
            body, (place,), (1,),
            [self.weight_spec(), self.full(self.blocks, TB)] + [self.full(self.piece_rows, self.width)] * 4,
            (w_neigh, inverse, *grads),
            self.full(self.per_chunk, self.slices, TB), self.dense(),
        )

    def weight_grad(self, k, place, w_self, feats, neighbour, grads):
        def body(place, w_self, feats, neighbour, *rest):
            self_out, weights_out = rest[-2:]
            total = jnp.zeros((2 * self.slices, self.width), F32)
            bias = jnp.zeros((1, self.width), F32)
            for part, grad in self.parts_of(place, rest[:-2]):
                value = self.back(w_self[...], grad[...])
                first = part * self.per_piece
                for j in range(self.per_piece):
                    self_out[first + j] = value[:, j * TB : (j + 1) * TB]
                start = pl.multiple_of(self.block(k, part, 0) * TB, TB)
                rows = jnp.concatenate(
                    [
                        feats[:, pl.ds(start, self.piece_rows)],
                        jnp.concatenate([neighbour[first + j] for j in range(self.per_piece)], 1),
                    ],
                    0,
                )
                high, low = split(rows)
                grad_high, grad_low = split(grad[...])
                total += (dot_nn(high, grad_high) + dot_nn(low, grad_high)) + dot_nn(high, grad_low)
                bias += jnp.sum(grad[...], axis=0, keepdims=True)
            weights_out[: 2 * self.slices, :] = total
            weights_out[2 * self.slices :, :] = jnp.broadcast_to(bias, (8, self.width))

        dense = self.full(self.per_chunk, self.slices, TB)
        shape = (2 * self.slices + 8, self.width)
        return self.call(
            body, (place,), (1,),
            [self.weight_spec(), self.full(self.slices, self.owned), dense]
            + [self.full(self.piece_rows, self.width)] * 4,
            (w_self, feats, neighbour, *grads),
            [dense, self.full(*shape)], [self.dense(), jax.ShapeDtypeStruct(shape, F32)], work=2,
        )

    def gather(self, place, sources, held):
        z = place[0]
        for k in range(CHUNKS):
            spots = slice(k * self.per_chunk, (k + 1) * self.per_chunk)
            if len(sources) == CHUNKS:
                held[spots] = sources[k][...]
            else:
                outer = (z == 0) | (z == 3)

                @pl.when(outer)
                def _():
                    held[spots] = sources[CHUNKS + k][...]

                @pl.when(jnp.logical_not(outer))
                def _():
                    held[spots] = sources[k][...]

    def held(self):
        return pltpu.VMEM((self.blocks, self.slices, TB), F32)

    def picked(self, role, place, rows, sources):
        def body(place, rows, *rest):
            out, held = rest[-2:]
            self.gather(place, rest[:-2], held)
            first = (owner(role, place[0]) * 2 + 1 - place[1]) * self.cap
            for c in range(self.cap):
                row = rows[first + c]
                chunk, spot = self.spot(row)
                out[c] = jnp.where(row >= 0, held[chunk * self.per_chunk + spot], 0.0)

        return self.call(
            body, (place, rows), (1,), [self.full(self.per_chunk, self.slices, TB)] * len(sources), sources,
            self.full(self.cap, self.slices, TB), self.slots(), scratch=[self.held()],
        )

    def spread_local(self, role, place, cols, rows, tiles, sources, total, through_self=None):
        first_call = through_self is not None

        def body(place, cols, rows, tile, *rest):
            out, held = rest[-2:]
            if first_call:
                self.gather(place, rest[:CHUNKS], held)
                for k, back in enumerate(rest[CHUNKS : 2 * CHUNKS]):
                    for part in range(self.parts):
                        for j in range(self.per_piece):
                            block = self.block(k, part, j)
                            out[:, block * TB : (block + 1) * TB] = back[part * self.per_piece + j]
            else:
                self.gather(place, rest[:-3], held)
                out[...] = rest[-3][...]
            owned_by = owner(role, place[0]) * 2 + place[1]
            for c in range(self.cap):
                row = rows[owned_by * self.cap + c]
                chunk, spot = self.spot(row)
                value = jnp.where(row >= 0, held[chunk * self.per_chunk + spot], 0.0)
                out[:, lanes(cols[owned_by * self.cap + c])] += times_tile(value, tile[0, c])

        whole = self.full(self.slices, self.owned)
        args = [tiles, *sources] + (list(through_self) if first_call else [total])
        dense = self.full(self.per_chunk, self.slices, TB)
        in_specs = [self.tile_spec(role, False)] + [dense] * len(sources)
        in_specs += [dense] * CHUNKS if first_call else [whole]
        return self.call(
            body, (place, cols, rows), (1,), in_specs, args, whole,
            jax.ShapeDtypeStruct((self.slices, self.owned), F32), scratch=[self.held()],
            aliases={} if first_call else {3 + len(args) - 1: 0},
        )

    def spread_slots(self, role, place, cols, tiles, slots, total):
        def body(place, cols, tile, slots, total, out):
            out[...] = total[...]
            owned_by = owner(role, place[0]) * 2 + 1 - place[1]
            for c in range(self.cap):
                out[:, lanes(cols[owned_by * self.cap + c])] += times_tile(slots[c], tile[0, c])

        whole = self.full(self.slices, self.owned)
        return self.call(
            body, (place, cols), (1,),
            [self.tile_spec(role, True), self.full(self.cap, self.slices, TB), whole], (tiles, slots, total),
            whole, jax.ShapeDtypeStruct((self.slices, self.owned), F32), aliases={4: 0},
        )


def pairs_z(steps):
    return [(2 * a + x, 2 * b + x) for a, b in steps for x in range(2)]


INWARD = pairs_z([(0, 1), (3, 2)])
ACROSS = pairs_z([(1, 2), (2, 1)])
OUTWARD = pairs_z([(1, 0), (2, 3)])
NEARBY = pairs_z([(0, 1), (1, 0), (2, 3), (3, 2)])
OTHER_X = [(n, n ^ 1) for n in range(8)]
OTHER_CORE = [(f, f ^ 1) for f in range(4)]
OTHER_Y = [(f, f ^ 2) for f in range(4)]


def chain_shards(node_feats, tiles, send_col, recv_row, degree, w_self, w_neigh, bias, cotangent):
    slices, owned = node_feats.shape
    cap = tiles.shape[1]
    width = w_self.shape[1]
    layer = Layer(slices, owned, cap, 4, width)
    node, feat = lax.axis_index("node"), lax.axis_index("feat")
    z, x = node // 2, node % 2
    place = jnp.stack([z, x, feat // 2, feat % 2]).astype(jnp.int32)
    cols = send_col.reshape(-1)
    every_row = lax.all_gather(recv_row, "node", axis=0, tiled=True)
    rows = every_row.reshape(4, 2, 4, 2, cap)
    rows = lax.dynamic_slice(rows, (0, x, z, 0, 0), (4, 1, 1, 2, cap)).reshape(-1)
    inverse = (1.0 / degree.astype(F32)).reshape(-1, TB)
    bias_row = bias.reshape(1, width)

    slots = []
    for role in range(4):
        part = layer.partial(role, place, cols, node_feats, tiles)
        slots.append(lax.ppermute(part, "node", OTHER_X))
    sums = layer.local(place, cols, rows, node_feats, tiles)
    joined = [layer.joined(role, place, rows, sums, slots[role]) for role in range(4)]

    activated = None
    weights = None
    self_back, own, near = [], [], []
    inner_got, inner_far, outer_got, outer_far = [], [], [], []
    for k in range(CHUNKS):
        far_outer, far_inner, nearby, mine = (joined[role][k] for role in range(4))
        first = lax.ppermute(far_outer, "node", INWARD)
        second = lax.ppermute(far_inner, "node", INWARD)
        third = lax.ppermute(nearby, "node", INWARD)
        for_outer = lax.ppermute(far_outer + first, "node", ACROSS)
        for_inner = lax.ppermute(far_inner + second, "node", ACROSS)
        last = lax.ppermute(nearby + for_outer, "node", OUTWARD)
        neighbour, send, keep = layer.project(
            k, place, (mine, third, for_inner, last), node_feats, w_self, w_neigh, inverse
        )
        got = lax.ppermute(send, "feat", OTHER_CORE)
        far = lax.ppermute(layer.for_other_y(place, keep, got), "feat", OTHER_Y)
        activated, grad = layer.activate(k, place, keep, got, far, bias_row, cotangent, activated)
        grad_y = lax.ppermute(grad, "feat", OTHER_Y)
        grad_core = lax.ppermute(grad, "feat", OTHER_CORE)
        grad_both = lax.ppermute(grad_y, "feat", OTHER_CORE)
        grads = (grad, grad_y, grad_core, grad_both)
        mine_back = layer.neighbour_grad(k, place, w_neigh, inverse, grads)
        own.append(mine_back)
        near.append(lax.ppermute(mine_back, "node", NEARBY))
        inner_got.append(lax.ppermute(mine_back, "node", ACROSS))
        inner_far.append(lax.ppermute(near[k], "node", ACROSS))
        outer_got.append(lax.ppermute(inner_got[k], "node", OUTWARD))
        outer_far.append(lax.ppermute(inner_far[k], "node", OUTWARD))
        back, chunk_weights = layer.weight_grad(k, place, w_self, node_feats, neighbour, grads)
        self_back.append(back)
        weights = chunk_weights if weights is None else weights + chunk_weights

    weights = lax.psum(weights, "node")
    weights = lax.all_gather(weights, "feat", axis=0)
    grad_self = weights[:, :slices].reshape(-1, width)
    grad_neigh = weights[:, slices : 2 * slices].reshape(-1, width)
    grad_bias = weights[0, 2 * slices]

    sources = {
        SELF: own, NEAR: near, FAR_INNER: inner_got + outer_got, FAR_OUTER: inner_far + outer_far,
    }
    order = (SELF, NEAR, FAR_INNER, FAR_OUTER)
    returned = {}
    for role in order:
        returned[role] = lax.ppermute(layer.picked(role, place, rows, sources[role]), "node", OTHER_X)
    total = layer.spread_local(SELF, place, cols, rows, tiles, own, None, self_back)
    total = layer.spread_local(NEAR, place, cols, rows, tiles, near, total)
    total = layer.spread_slots(SELF, place, cols, tiles, returned[SELF], total)
    total = layer.spread_local(FAR_INNER, place, cols, rows, tiles, sources[FAR_INNER], total)
    total = layer.spread_slots(NEAR, place, cols, tiles, returned[NEAR], total)
    total = layer.spread_local(FAR_OUTER, place, cols, rows, tiles, sources[FAR_OUTER], total)
    total = layer.spread_slots(FAR_INNER, place, cols, tiles, returned[FAR_INNER], total)
    total = layer.spread_slots(FAR_OUTER, place, cols, tiles, returned[FAR_OUTER], total)
    return (activated, total, grad_self, grad_neigh, grad_bias)


def slot_shards(node_feats, tiles, send_col, recv_row, degree, w_self, w_neigh, bias, cotangent):
    slices, owned = node_feats.shape
    blocks = owned // TB
    block_ids = jnp.arange(blocks, dtype=jnp.int32)
    scale = degree.astype(F32)[None, :]
    col_onehot = (send_col[..., None] == block_ids).astype(F32)
    row_onehot = (recv_row[..., None] == block_ids).astype(F32)
    feat_blocks = node_feats.reshape(slices, blocks, TB)
    picked = jnp.einsum("dcb,fbj->dcfj", col_onehot, feat_blocks, precision=HIGH)
    partial_value = jnp.einsum("dcfj,dcij->dcfi", picked, tiles, precision=HIGH)
    arrived = lax.all_to_all(partial_value, "node", split_axis=0, concat_axis=0, tiled=True)
    summed = jnp.einsum("scfi,scb->fbi", arrived, row_onehot, precision=HIGH)
    neighbour = summed.reshape(slices, owned) / scale
    offset = lax.axis_index("feat") * slices
    self_rows = lax.dynamic_slice_in_dim(w_self, offset, slices, 0)
    neigh_rows = lax.dynamic_slice_in_dim(w_neigh, offset, slices, 0)
    dims = (((0,), (0,)), ((), ()))
    first = lax.dot_general(node_feats, self_rows, dims, precision=HIGH)
    second = lax.dot_general(neighbour, neigh_rows, dims, precision=HIGH)
    pre = lax.psum_scatter(first + second, "feat", scatter_dimension=0, tiled=True) + bias
    sigma = jax.nn.sigmoid(pre)
    activated = pre * sigma
    gpre = cotangent * sigma * (1.0 + pre * (1.0 - sigma))
    piece = lax.all_gather(gpre, "feat", axis=0, tiled=True)
    dims = (((1,), (1,)), ((), ()))
    self_back = lax.dot_general(self_rows, piece, dims, precision=HIGH)
    neigh_back = lax.dot_general(neigh_rows, piece, dims, precision=HIGH)
    slice_self = jnp.dot(node_feats, piece, precision=HIGH)
    slice_neigh = jnp.dot(neighbour, piece, precision=HIGH)
    sums = lax.psum((slice_self, slice_neigh, jnp.sum(piece, axis=0)), "node")
    grad_self, grad_neigh = (lax.all_gather(part, "feat", axis=0, tiled=True) for part in sums[:2])
    gneigh = (neigh_back / scale).reshape(slices, blocks, TB)
    outgoing = jnp.einsum("scb,fbi->scfi", row_onehot, gneigh, precision=HIGH)
    returned = lax.all_to_all(outgoing, "node", split_axis=0, concat_axis=0, tiled=True)
    spread = jnp.einsum("dcfi,dcij->dcfj", returned, tiles, precision=HIGH)
    placed = jnp.einsum("dcfj,dcb->fbj", spread, col_onehot, precision=HIGH)
    grad_feats = self_back + placed.reshape(slices, owned)
    return (activated, grad_feats, grad_self, grad_neigh, sums[2])


def solution(mesh):
    chain = mesh.shape["node"] == 8 and mesh.shape["feat"] == 4
    return jax.shard_map(
        chain_shards if chain else slot_shards,
        mesh=mesh,
        in_specs=(
            P("feat", "node"),
            P("node", None, None, None),
            P("node", None),
            P("node", None),
            P("node"),
            P(),
            P(),
            P(),
            P(("node", "feat"), None),
        ),
        out_specs=(P(("node", "feat"), None), P("feat", "node"), P(), P(), P()),
        check_vma=False,
    )
```

```python
import jax
import jax.numpy as jnp
from jax import lax
from jax.experimental import pallas as pl
from jax.experimental.pallas import tpu as pltpu
from jax.sharding import PartitionSpec as P

TB = 128
F32 = jnp.float32
BF16 = jnp.bfloat16
HIGH = lax.Precision.HIGH
CHUNKS = 2
VMEM_BYTES = 28 * 2**20

FAR_OUTER, FAR_INNER, NEAR, SELF = range(4)


def owner(role, z):
    if role == FAR_OUTER:
        return jnp.where(z < 2, 3, 0)
    if role == FAR_INNER:
        return jnp.where(z < 2, 2, 1)
    if role == NEAR:
        return z + 1 - 2 * (z % 2)
    return z


def split(value):
    high = value.astype(BF16)
    return high, (value - high.astype(F32)).astype(BF16)


def dot_nn(a, b):
    return lax.dot_general(a, b, (((1,), (0,)), ((), ())), preferred_element_type=F32)


def dot_nt(a, b):
    return lax.dot_general(a, b, (((1,), (1,)), ((), ())), preferred_element_type=F32)


def stacked(value):
    high, low = split(value)
    return jnp.concatenate(
        [jnp.concatenate([high, high], 1), jnp.concatenate([low, jnp.zeros_like(low)], 1)], 0
    )


def times_tile_t(value, tile):
    rows = value.shape[0]
    out = dot_nt(stacked(value), jnp.concatenate(split(tile), 1))
    return out[:rows] + out[rows:]


def times_tile(value, tile):
    rows = value.shape[0]
    out = dot_nn(stacked(value), jnp.concatenate(split(tile), 0))
    return out[:rows] + out[rows:]


def lanes(block):
    return pl.ds(pl.multiple_of(block * TB, TB), TB)


class Layer:
    def __init__(self, slices, owned, cap, parts, width):
        self.slices, self.owned, self.cap, self.parts, self.width = slices, owned, cap, parts, width
        self.blocks = owned // TB
        self.per_part = self.blocks // parts
        self.per_piece = self.per_part // CHUNKS
        self.per_chunk = self.blocks // CHUNKS
        self.piece = self.per_piece * TB
        self.span = self.per_chunk * TB

    def spot(self, row):
        row = jnp.maximum(row, 0)
        part, inside = row // self.per_part, row % self.per_part
        return inside // self.per_piece, part * self.per_piece + inside % self.per_piece

    def block(self, chunk, part, inside):
        return part * self.per_part + chunk * self.per_piece + inside

    def full(self, *shape):
        return pl.BlockSpec(shape, lambda *_: (0,) * len(shape))

    def dense_spec(self):
        return self.full(self.per_chunk, self.slices, TB)

    def slots_spec(self):
        return self.full(self.cap, self.slices, TB)

    def slots(self):
        return jax.ShapeDtypeStruct((self.cap, self.slices, TB), F32)

    def dense(self):
        return jax.ShapeDtypeStruct((self.per_chunk, self.slices, TB), F32)

    def call(self, body, scalars, grid, in_specs, args, out_specs, out_shape, scratch=(), aliases=None, after=()):
        given = len(scalars) + len(args)

        def ordered(*refs):
            body(*refs[:given], *refs[given + len(after) :])

        return pl.pallas_call(
            ordered,
            grid_spec=pltpu.PrefetchScalarGridSpec(
                num_scalar_prefetch=len(scalars),
                grid=grid,
                in_specs=list(in_specs) + [pl.BlockSpec(memory_space=pl.ANY)] * len(after),
                out_specs=out_specs,
                scratch_shapes=scratch,
            ),
            out_shape=out_shape,
            input_output_aliases=aliases or {},
            compiler_params=pltpu.CompilerParams(vmem_limit_bytes=VMEM_BYTES),
            cost_estimate=pl.CostEstimate(flops=10**8, bytes_accessed=4 * 2**20, transcendentals=0),
        )(*scalars, *args, *after)

    def fetched(self, count):
        return [pltpu.VMEM((count, self.cap, TB, TB), F32), pltpu.SemaphoreType.DMA((count,))]

    def fetch(self, tiles, buffer, sems, index, slot):
        return pltpu.make_async_copy(tiles.at[index], buffer.at[slot], sems.at[slot])

    def tiles_spec(self):
        return pl.BlockSpec(memory_space=pltpu.HBM)

    def partial(self, role, place, cols, feats, tiles, after=()):
        def body(place, cols, feats, tiles, out, buffer, sems):
            owned_by = owner(role, place[0]) * 2 + 1 - place[1]
            copy = self.fetch(tiles, buffer, sems, owned_by, 0)
            copy.start()
            copy.wait()
            for c in range(self.cap):
                out[c] = times_tile_t(feats[:, lanes(cols[owned_by * self.cap + c])], buffer[0, c])

        return self.call(
            body, (place, cols), (1,),
            [self.full(self.slices, self.owned), self.tiles_spec()], (feats, tiles),
            self.slots_spec(), self.slots(), scratch=self.fetched(1), after=after,
        )

    def local(self, place, cols, rows, feats, tiles, after=()):
        def body(place, cols, rows, feats, tiles, out, buffer, sems):
            z, x = place[0], place[1]
            copies = [self.fetch(tiles, buffer, sems, owner(role, z) * 2 + x, role) for role in range(4)]
            for copy in copies:
                copy.start()
            for role in range(4):
                out[role] = jnp.zeros(out.shape[1:], F32)
                copies[role].wait()
                first = (owner(role, z) * 2 + x) * self.cap
                for c in range(self.cap):
                    row = rows[self.row_index(role, z, x) + c]
                    chunk, spot = self.spot(row)
                    value = times_tile_t(feats[:, lanes(cols[first + c])], buffer[role, c])
                    out[role, chunk * self.per_chunk + spot] += jnp.where(row >= 0, value, 0.0)

        shape = (4, self.blocks, self.slices, TB)
        return self.call(
            body, (place, cols, rows), (1,),
            [self.full(self.slices, self.owned), self.tiles_spec()], (feats, tiles),
            self.full(*shape), jax.ShapeDtypeStruct(shape, F32), scratch=self.fetched(4), after=after,
        )

    def row_index(self, role, z, sender_x):
        return ((owner(role, z) ^ z) * 2 + sender_x) * self.cap

    def joined(self, role, k, place, rows, sums, slots, after=()):
        def body(place, rows, sums, slots, out):
            out[...] = sums[0]
            first = self.row_index(role, place[0], 1 - place[1])
            for c in range(self.cap):
                row = rows[first + c]
                chunk, spot = self.spot(row)
                out[spot] += jnp.where((row >= 0) & (chunk == k), slots[c], 0.0)

        return self.call(
            body, (place, rows), (1,),
            [pl.BlockSpec((1, self.per_chunk, self.slices, TB), lambda *_: (role, k, 0, 0)), self.slots_spec()],
            (sums, slots), self.dense_spec(), self.dense(), after=after,
        )

    def means(self, k, pieces, inverse):
        def body(own, near, inner, outer, inverse, out):
            for part in range(self.parts):
                for j in range(self.per_piece):
                    spot, block = part * self.per_piece + j, self.block(k, part, j)
                    total = own[spot] + near[spot] + inner[spot] + outer[spot]
                    out[spot] = total * inverse[block : block + 1, :]

        return self.call(
            body, (), (1,), [self.dense_spec()] * 4 + [self.full(self.blocks, TB)], (*pieces, inverse),
            self.dense_spec(), self.dense(),
        )

    def transposed(self, value, after=()):
        def body(value, out):
            out[...] = value[...].T

        rows, cols = value.shape
        return self.call(
            body, (), (1,), [self.full(rows, cols)], (value,), self.full(cols, rows),
            jax.ShapeDtypeStruct((cols, rows), F32), after=after,
        )

    def feats_of(self, place):
        y, core = place[2], place[3]
        return (2 * y + core, 2 * (1 - y) + core, 2 * y + 1 - core, 2 * (1 - y) + 1 - core)

    def times_weight(self, weight_t, high, low):
        rows = weight_t.shape[0]
        weight_high, weight_low = split(weight_t)
        out = dot_nn(jnp.concatenate([weight_high, weight_low], 0), high)
        return out[:rows] + out[rows:] + dot_nn(weight_high, low)

    def self_part(self, place, slices, w_self, bias, after=()):
        def body(place, own, far, core, both, w_self, bias, out, held):
            for index, piece in zip(self.feats_of(place), (own, far, core, both)):
                held[pl.ds(pl.multiple_of(index * self.slices, self.slices), self.slices), :] = piece[...]
            column = jnp.broadcast_to(bias[...], (TB, self.width)).T
            value = self.times_weight(w_self[...].T, *split(held[...]))
            out[0] = value + jnp.concatenate([column] * self.per_piece, 1)

        columns = pl.BlockSpec((self.slices, self.piece), lambda k, part, *_: (0, part * CHUNKS + k))
        return self.call(
            body, (place,), (CHUNKS, self.parts),
            [columns] * 4 + [self.full(self.width, self.width), self.full(1, self.width)], (*slices, w_self, bias),
            pl.BlockSpec((1, self.width, self.piece), lambda k, part, *_: (k, 0, part)),
            jax.ShapeDtypeStruct((CHUNKS, self.width, self.span), F32),
            scratch=[pltpu.VMEM((self.width, self.piece), F32)], after=after,
        )

    def activate(self, k, place, means, w_neigh, self_part, cotangents, inverse, activated):
        rows = pl.BlockSpec((self.piece, self.width), lambda *_: (k, 0))

        def body(place, m0, m1, m2, m3, weight, self_part, c0, c1, c2, c3, inverse, *rest):
            out, grad, back, high, low = rest[-5:]
            feats = self.feats_of(place)
            for index, piece in zip(feats, (m0, m1, m2, m3)):
                at = pl.ds(pl.multiple_of(index * self.slices, self.slices), self.slices)
                for spot in range(self.per_chunk):
                    columns = slice(spot * TB, (spot + 1) * TB)
                    high[at, columns], low[at, columns] = split(piece[spot])
            weight_t = weight[...].T
            own_rows = weight[pl.ds(pl.multiple_of(feats[0] * self.slices, self.slices), self.slices), :]
            for part, cotangent in zip(feats, (c0, c1, c2, c3)):
                at = pl.ds(pl.multiple_of(part * self.piece, self.piece), self.piece)
                pre = self.times_weight(weight_t, high[:, at], low[:, at]) + self_part[0, :, at]
                sigma = jax.nn.sigmoid(pre)
                if cotangent is c0:
                    out[...] = (pre * sigma).T
                slope = cotangent[...] * (sigma * (1.0 + pre * (1.0 - sigma)))
                grad[:, at] = slope
                value = self.times_weight(own_rows, *split(slope))
                for j in range(self.per_piece):
                    scale = inverse[pl.ds(self.block(k, part, j), 1), :]
                    back[part * self.per_piece + j] = value[:, j * TB : (j + 1) * TB] * scale

        in_specs = (
            [self.dense_spec()] * 4
            + [self.full(self.width, self.width)]
            + [pl.BlockSpec((1, self.width, self.span), lambda *_: (k, 0, 0))]
            + [pl.BlockSpec((self.width, self.piece), lambda *_: (0, k))] * 4
            + [self.full(self.blocks, TB)]
        )
        args = [*means, w_neigh, self_part, *cotangents, inverse]
        aliases = {}
        if activated is not None:
            aliases = {1 + len(args): 0}
            in_specs.append(pl.BlockSpec(memory_space=pl.ANY))
            args.append(activated)
        return self.call(
            body, (place,), (1,), in_specs, args,
            [rows, self.full(self.width, self.span), self.dense_spec()],
            [jax.ShapeDtypeStruct((self.per_part * TB, self.width), F32),
             jax.ShapeDtypeStruct((self.width, self.span), F32), self.dense()],
            scratch=[pltpu.VMEM((self.width, self.span), BF16)] * 2, aliases=aliases,
        )

    def weight_grad(self, k, place, w_self, feats, means, grad, before):
        shape = (2 * self.slices + 16, self.width)

        def body(place, w_self, feats, means, grad, *rest):
            self_out, weights_out = rest[-2:]
            total = rest[0][...] if before is not None else jnp.zeros(shape, F32)
            for part in range(self.parts):
                first = part * self.per_piece
                at = slice(part * self.piece, (part + 1) * self.piece)
                high, low = split(grad[:, at])
                value = self.times_weight(w_self[...], high, low)
                for j in range(self.per_piece):
                    self_out[first + j] = value[:, j * TB : (j + 1) * TB]
                start = self.block(k, part, 0) * TB
                rows = jnp.concatenate(
                    [
                        feats[:, start : start + self.piece],
                        jnp.concatenate([means[first + j] for j in range(self.per_piece)], 1),
                        jnp.ones((16, self.piece), F32),
                    ],
                    0,
                )
                rows_high, rows_low = split(rows)
                total += (dot_nt(rows_high, high) + dot_nt(rows_low, high)) + dot_nt(rows_high, low)
            weights_out[...] = total

        own_rows = pl.BlockSpec((self.slices, self.width), lambda i, place, *_: (2 * place[2] + place[3], 0))
        args = [w_self, feats, means, grad] + ([] if before is None else [before])
        return self.call(
            body, (place,), (1,),
            [own_rows, self.full(self.slices, self.owned), self.dense_spec(), self.full(self.width, self.span)]
            + [self.full(*shape)] * (before is not None),
            args, [self.dense_spec(), self.full(*shape)], [self.dense(), jax.ShapeDtypeStruct(shape, F32)],
        )

    def gather(self, place, sources, held):
        outer = (place[0] == 0) | (place[0] == 3)
        for k in range(CHUNKS):
            spots = slice(k * self.per_chunk, (k + 1) * self.per_chunk)
            if len(sources) == CHUNKS:
                held[spots] = sources[k][...]
            else:

                @pl.when(outer)
                def _():
                    held[spots] = sources[CHUNKS + k][...]

                @pl.when(jnp.logical_not(outer))
                def _():
                    held[spots] = sources[k][...]

    def held(self):
        return pltpu.VMEM((self.blocks, self.slices, TB), F32)

    def pick(self, row, held):
        chunk, spot = self.spot(row)
        return jnp.where(row >= 0, held[chunk * self.per_chunk + spot], 0.0)

    def picked(self, role, place, rows, sources):
        def body(place, rows, *rest):
            out, held = rest[-2:]
            self.gather(place, rest[:-2], held)
            first = self.row_index(role, place[0], 1 - place[1])
            for c in range(self.cap):
                out[c] = self.pick(rows[first + c], held)

        return self.call(
            body, (place, rows), (1,), [self.dense_spec()] * len(sources), sources,
            self.slots_spec(), self.slots(), scratch=[self.held()],
        )

    def spread(self, place, cols, rows, tiles, jobs, total=None, self_back=None):
        counts = [len(sources) for _, sources in jobs]
        extra = [total] if self_back is None else list(self_back)

        def body(place, cols, rows, tiles, *rest):
            arrays, more = rest[: sum(counts)], rest[sum(counts) : sum(counts) + len(extra)]
            out, held, buffer, sems = rest[sum(counts) + len(extra) :]
            z, x = place[0], place[1]
            owners = [owner(role, z) * 2 + (1 - x if n == 1 else x) for (role, _), n in zip(jobs, counts)]
            copies = [self.fetch(tiles, buffer, sems, owned_by, i) for i, owned_by in enumerate(owners)]
            for copy in copies:
                copy.start()
            if self_back is None:
                out[...] = more[0][...]
            else:
                for k, back in enumerate(more):
                    for part in range(self.parts):
                        for j in range(self.per_piece):
                            block = self.block(k, part, j)
                            out[:, block * TB : (block + 1) * TB] = back[part * self.per_piece + j]
            for i, (role, _) in enumerate(jobs):
                sources = arrays[sum(counts[:i]) : sum(counts[: i + 1])]
                if counts[i] > 1:
                    self.gather(place, sources, held)
                copies[i].wait()
                for c in range(self.cap):
                    if counts[i] > 1:
                        value = self.pick(rows[self.row_index(role, z, x) + c], held)
                    else:
                        value = sources[0][c]
                    out[:, lanes(cols[owners[i] * self.cap + c])] += times_tile(value, buffer[i, c])

        whole = self.full(self.slices, self.owned)
        in_specs, args = [self.tiles_spec()], [tiles]
        for _, sources in jobs:
            in_specs += [self.slots_spec() if len(sources) == 1 else self.dense_spec()] * len(sources)
            args += sources
        in_specs += [whole] if self_back is None else [self.dense_spec()] * CHUNKS
        args += extra
        return self.call(
            body, (place, cols, rows), (1,), in_specs, args, whole,
            jax.ShapeDtypeStruct((self.slices, self.owned), F32),
            scratch=[self.held(), *self.fetched(len(jobs))],
            aliases={3 + len(args) - 1: 0} if self_back is None else {},
        )


def pairs_z(steps):
    return [(2 * a + x, 2 * b + x) for a, b in steps for x in range(2)]


INWARD = pairs_z([(0, 1), (3, 2)])
ACROSS = pairs_z([(1, 2), (2, 1)])
OUTWARD = pairs_z([(1, 0), (2, 3)])
OTHER_X = [(n, n ^ 1) for n in range(8)]
OTHER_CORE = [(f, f ^ 1) for f in range(4)]
OTHER_Y = [(f, f ^ 2) for f in range(4)]


def along_z(distance):
    return pairs_z([(z, z ^ distance) for z in range(4)])


def node_swap(value, pairs):
    return lax.ppermute(value, "node", pairs)


def over_feat(value):
    far = lax.ppermute(value, "feat", OTHER_Y)
    core = lax.ppermute(value, "feat", OTHER_CORE)
    return value, far, core, lax.ppermute(far, "feat", OTHER_CORE)


def pair(mine, other, place):
    return jnp.where(place == 0, jnp.stack([mine, other]), jnp.stack([other, mine]))


def spread_weights(weights, x, y, core):
    halves = weights.reshape(2, -1, weights.shape[1])
    keep = lax.dynamic_index_in_dim(halves, x, 0, keepdims=False)
    send = lax.dynamic_index_in_dim(halves, 1 - x, 0, keepdims=False)
    total = keep + node_swap(send, OTHER_X)
    total = total + node_swap(total, along_z(1))
    total = total + node_swap(total, along_z(3))
    whole = pair(total, node_swap(total, OTHER_X), x).reshape(weights.shape)
    cores = pair(whole, lax.ppermute(whole, "feat", OTHER_CORE), core)
    return pair(cores, lax.ppermute(cores, "feat", OTHER_Y), y).reshape(4, *weights.shape)


def chain_shards(node_feats, tiles, send_col, recv_row, degree, w_self, w_neigh, bias, cotangent):
    slices, owned = node_feats.shape
    cap = tiles.shape[1]
    width = w_self.shape[1]
    layer = Layer(slices, owned, cap, 4, width)
    node, feat = lax.axis_index("node"), lax.axis_index("feat")
    z, x, y, core = node // 2, node % 2, feat // 2, feat % 2
    place = jnp.stack([z, x, y, core]).astype(jnp.int32)
    cols = send_col.reshape(-1)

    slots = []
    for role in range(4):
        part = layer.partial(role, place, cols, node_feats, tiles, after=slots[-1:])
        slots.append(node_swap(part, OTHER_X))
    every_row = jnp.stack([recv_row] + [node_swap(recv_row, along_z(d)) for d in (1, 2, 3)])
    rows = lax.dynamic_slice(every_row, (0, 2 * z, 0), (4, 2, cap)).reshape(-1)
    inverse = (1.0 / degree.astype(F32)).reshape(-1, TB)
    feat_slices = over_feat(node_feats)
    cotangents = over_feat(layer.transposed(cotangent))
    self_part = layer.self_part(place, feat_slices, w_self, bias.reshape(1, width))
    sums = layer.local(place, cols, rows, node_feats, tiles)

    activated = None
    weights = None
    order = []
    self_back, own, near = [], [], []
    inner_got, inner_far, outer_got, outer_far = [], [], [], []
    for k in range(CHUNKS):
        parts = []
        for role in range(3):
            part = layer.joined(role, k, place, rows, sums, slots[role], after=order[-2:-1])
            parts.append(part)
            order.append(node_swap(part, INWARD))
        mine = layer.joined(SELF, k, place, rows, sums, slots[SELF])
        first, second, third = order[-3:]
        for_outer = node_swap(parts[FAR_OUTER] + first, ACROSS)
        for_inner = node_swap(parts[FAR_INNER] + second, ACROSS)
        last = node_swap(parts[NEAR] + for_outer, OUTWARD)
        means = layer.means(k, (mine, third, for_inner, last), inverse)
        activated, grad, mine_back = layer.activate(
            k, place, over_feat(means), w_neigh, self_part, cotangents, inverse, activated
        )
        own.append(mine_back)
        near.append(node_swap(mine_back, along_z(1)))
        inner_got.append(node_swap(mine_back, ACROSS))
        inner_far.append(node_swap(near[k], ACROSS))
        outer_got.append(node_swap(inner_got[k], OUTWARD))
        outer_far.append(node_swap(inner_far[k], OUTWARD))
        back, weights = layer.weight_grad(k, place, w_self, node_feats, means, grad, weights)
        self_back.append(back)

    weights = spread_weights(weights, x, y, core)
    grad_self = weights[:, :slices].reshape(-1, width)
    grad_neigh = weights[:, slices : 2 * slices].reshape(-1, width)
    grad_bias = weights[0, 2 * slices]

    sources = {
        SELF: own, NEAR: near, FAR_INNER: inner_got + outer_got, FAR_OUTER: inner_far + outer_far,
    }
    returned = {}
    for role in (SELF, NEAR, FAR_INNER, FAR_OUTER):
        returned[role] = [node_swap(layer.picked(role, place, rows, sources[role]), OTHER_X)]
    local = {role: (role, sources[role]) for role in sources}
    other = {role: (role, returned[role]) for role in sources}
    total = layer.spread(place, cols, rows, tiles, [local[SELF]], self_back=self_back)
    total = layer.spread(place, cols, rows, tiles, [local[NEAR], other[SELF]], total)
    total = layer.spread(place, cols, rows, tiles, [local[FAR_INNER], other[NEAR]], total)
    total = layer.spread(place, cols, rows, tiles, [local[FAR_OUTER], other[FAR_INNER]], total)
    total = layer.spread(place, cols, rows, tiles, [other[FAR_OUTER]], total)
    return (activated, total, grad_self, grad_neigh, grad_bias)


def slot_shards(node_feats, tiles, send_col, recv_row, degree, w_self, w_neigh, bias, cotangent):
    slices, owned = node_feats.shape
    blocks = owned // TB
    block_ids = jnp.arange(blocks, dtype=jnp.int32)
    scale = degree.astype(F32)[None, :]
    col_onehot = (send_col[..., None] == block_ids).astype(F32)
    row_onehot = (recv_row[..., None] == block_ids).astype(F32)
    feat_blocks = node_feats.reshape(slices, blocks, TB)
    picked = jnp.einsum("dcb,fbj->dcfj", col_onehot, feat_blocks, precision=HIGH)
    partial_value = jnp.einsum("dcfj,dcij->dcfi", picked, tiles, precision=HIGH)
    arrived = lax.all_to_all(partial_value, "node", split_axis=0, concat_axis=0, tiled=True)
    summed = jnp.einsum("scfi,scb->fbi", arrived, row_onehot, precision=HIGH)
    neighbour = summed.reshape(slices, owned) / scale
    offset = lax.axis_index("feat") * slices
    self_rows = lax.dynamic_slice_in_dim(w_self, offset, slices, 0)
    neigh_rows = lax.dynamic_slice_in_dim(w_neigh, offset, slices, 0)
    dims = (((0,), (0,)), ((), ()))
    first = lax.dot_general(node_feats, self_rows, dims, precision=HIGH)
    second = lax.dot_general(neighbour, neigh_rows, dims, precision=HIGH)
    pre = lax.psum_scatter(first + second, "feat", scatter_dimension=0, tiled=True) + bias
    sigma = jax.nn.sigmoid(pre)
    activated = pre * sigma
    gpre = cotangent * sigma * (1.0 + pre * (1.0 - sigma))
    piece = lax.all_gather(gpre, "feat", axis=0, tiled=True)
    dims = (((1,), (1,)), ((), ()))
    self_back = lax.dot_general(self_rows, piece, dims, precision=HIGH)
    neigh_back = lax.dot_general(neigh_rows, piece, dims, precision=HIGH)
    slice_self = jnp.dot(node_feats, piece, precision=HIGH)
    slice_neigh = jnp.dot(neighbour, piece, precision=HIGH)
    sums = lax.psum((slice_self, slice_neigh, jnp.sum(piece, axis=0)), "node")
    grad_self, grad_neigh = (lax.all_gather(part, "feat", axis=0, tiled=True) for part in sums[:2])
    gneigh = (neigh_back / scale).reshape(slices, blocks, TB)
    outgoing = jnp.einsum("scb,fbi->scfi", row_onehot, gneigh, precision=HIGH)
    returned = lax.all_to_all(outgoing, "node", split_axis=0, concat_axis=0, tiled=True)
    spread = jnp.einsum("dcfi,dcij->dcfj", returned, tiles, precision=HIGH)
    placed = jnp.einsum("dcfj,dcb->fbj", spread, col_onehot, precision=HIGH)
    grad_feats = self_back + placed.reshape(slices, owned)
    return (activated, grad_feats, grad_self, grad_neigh, sums[2])


def solution(mesh):
    chain = mesh.shape["node"] == 8 and mesh.shape["feat"] == 4
    return jax.shard_map(
        chain_shards if chain else slot_shards,
        mesh=mesh,
        in_specs=(
            P("feat", "node"),
            P("node", None, None, None),
            P("node", None),
            P("node", None),
            P("node"),
            P(),
            P(),
            P(),
            P(("node", "feat"), None),
        ),
        out_specs=(P(("node", "feat"), None), P("feat", "node"), P(), P(), P()),
        check_vma=False,
    )
```

```python
import jax
import jax.numpy as jnp
from jax import lax
from jax.experimental import pallas as pl
from jax.experimental.pallas import tpu as pltpu
from jax.sharding import PartitionSpec as P

TB = 128
F32 = jnp.float32
BF16 = jnp.bfloat16
HIGH = lax.Precision.HIGH
CHUNKS = 2
VMEM_BYTES = 28 * 2**20
TILE_VMEM_BYTES = 57 * 2**20

FAR_OUTER, FAR_INNER, NEAR, SELF = range(4)


def owner(role, z):
    if role == FAR_OUTER:
        return jnp.where(z < 2, 3, 0)
    if role == FAR_INNER:
        return jnp.where(z < 2, 2, 1)
    if role == NEAR:
        return z + 1 - 2 * (z % 2)
    return z


def split(value):
    high = value.astype(BF16)
    return high, (value - high.astype(F32)).astype(BF16)


def dot_nn(a, b):
    return lax.dot_general(a, b, (((1,), (0,)), ((), ())), preferred_element_type=F32)


def dot_nt(a, b):
    return lax.dot_general(a, b, (((1,), (1,)), ((), ())), preferred_element_type=F32)


def stacked(value):
    high, low = split(value)
    return jnp.concatenate(
        [jnp.concatenate([high, high], 1), jnp.concatenate([low, jnp.zeros_like(low)], 1)], 0
    )


def times_tile_t(value, tile):
    rows = value.shape[0]
    out = dot_nt(stacked(value), jnp.concatenate(split(tile), 1))
    return out[:rows] + out[rows:]


def times_tile(value, tile):
    rows = value.shape[0]
    out = dot_nn(stacked(value), jnp.concatenate(split(tile), 0))
    return out[:rows] + out[rows:]


def lanes(block):
    return pl.ds(pl.multiple_of(block * TB, TB), TB)


class Layer:
    def __init__(self, slices, owned, cap, parts, width):
        self.slices, self.owned, self.cap, self.parts, self.width = slices, owned, cap, parts, width
        self.blocks = owned // TB
        self.per_part = self.blocks // parts
        self.per_piece = self.per_part // CHUNKS
        self.per_chunk = self.blocks // CHUNKS
        self.piece = self.per_piece * TB
        self.span = self.per_chunk * TB
        self.token = None

    def spot(self, row):
        row = jnp.maximum(row, 0)
        part, inside = row // self.per_part, row % self.per_part
        return inside // self.per_piece, part * self.per_piece + inside % self.per_piece

    def block(self, chunk, part, inside):
        return part * self.per_part + chunk * self.per_piece + inside

    def full(self, *shape):
        return pl.BlockSpec(shape, lambda *_: (0,) * len(shape))

    def dense_spec(self):
        return self.full(self.per_chunk, self.slices, TB)

    def slots_spec(self):
        return self.full(self.cap, self.slices, TB)

    def slots(self):
        return jax.ShapeDtypeStruct((self.cap, self.slices, TB), F32)

    def dense(self):
        return jax.ShapeDtypeStruct((self.per_chunk, self.slices, TB), F32)

    def call(self, body, scalars, grid, in_specs, args, out_specs, out_shape, scratch=(), aliases=None, after=(), vmem=VMEM_BYTES):
        given = len(scalars) + len(args)
        waits = list(after) + ([] if self.token is None else [self.token])

        def ordered(*refs):
            body(*refs[:given], *refs[given + len(waits) :])

        out = pl.pallas_call(
            ordered,
            grid_spec=pltpu.PrefetchScalarGridSpec(
                num_scalar_prefetch=len(scalars),
                grid=grid,
                in_specs=list(in_specs) + [pl.BlockSpec(memory_space=pl.ANY)] * len(waits),
                out_specs=out_specs,
                scratch_shapes=scratch,
            ),
            out_shape=out_shape,
            input_output_aliases=aliases or {},
            compiler_params=pltpu.CompilerParams(vmem_limit_bytes=vmem),
            cost_estimate=pl.CostEstimate(flops=1, bytes_accessed=1, transcendentals=0),
        )(*scalars, *args, *waits)
        self.token = jax.tree.leaves(out)[-1]
        return out

    def relay(self, value):
        def body(value, out):
            pass

        anywhere = pl.BlockSpec(memory_space=pl.ANY)
        return self.call(
            body, (), (1,), [anywhere], (value,), anywhere, jax.ShapeDtypeStruct(value.shape, value.dtype),
            aliases={0: 0},
        )

    def added(self, a, b):
        def body(a, b, out):
            out[...] = a[...] + b[...]

        spec = self.full(*a.shape)
        return self.call(body, (), (1,), [spec] * 2, (a, b), spec, jax.ShapeDtypeStruct(a.shape, F32))

    def fetched(self, count):
        return [pltpu.VMEM((count, self.cap, TB, TB), F32), pltpu.SemaphoreType.DMA((count,))]

    def fetch(self, tiles, buffer, sems, index, slot):
        return pltpu.make_async_copy(tiles.at[index], buffer.at[slot], sems.at[slot])

    def tiles_spec(self):
        return pl.BlockSpec(memory_space=pltpu.HBM)

    def partial(self, role, place, cols, feats, tiles, after=()):
        def body(place, cols, feats, tiles, out, buffer, sems):
            owned_by = owner(role, place[0]) * 2 + 1 - place[1]
            copy = self.fetch(tiles, buffer, sems, owned_by, 0)
            copy.start()
            copy.wait()
            for c in range(self.cap):
                out[c] = times_tile_t(feats[:, lanes(cols[owned_by, c])], buffer[0, c])

        return self.call(
            body, (place, cols), (1,),
            [self.full(self.slices, self.owned), self.tiles_spec()], (feats, tiles),
            self.slots_spec(), self.slots(), scratch=self.fetched(1), after=after, vmem=TILE_VMEM_BYTES,
        )

    def local(self, place, cols, rows, feats, tiles):
        def body(place, cols, rows, feats, tiles, out, buffer, sems):
            z, x = place[0], place[1]
            copies = [self.fetch(tiles, buffer, sems, owner(role, z) * 2 + x, role) for role in range(4)]
            for copy in copies:
                copy.start()
            for role in range(4):
                out[role] = jnp.zeros(out.shape[1:], F32)
                copies[role].wait()
                owned_by, row_of = owner(role, z) * 2 + x, self.row_index(role, z, x)
                for c in range(self.cap):
                    row = rows[row_of, c]
                    chunk, spot = self.spot(row)
                    value = times_tile_t(feats[:, lanes(cols[owned_by, c])], buffer[role, c])
                    out[role, chunk * self.per_chunk + spot] += jnp.where(row >= 0, value, 0.0)

        shape = (4, self.blocks, self.slices, TB)
        return self.call(
            body, (place, cols, rows), (1,),
            [self.full(self.slices, self.owned), self.tiles_spec()], (feats, tiles),
            self.full(*shape), jax.ShapeDtypeStruct(shape, F32), scratch=self.fetched(4), vmem=TILE_VMEM_BYTES,
        )

    def own_rows(self, place, tables):
        def body(place, *refs):
            for distance, table in enumerate(refs[:4]):
                refs[4][2 * distance : 2 * distance + 2, :] = table[pl.ds(2 * place[0], 2), :]

        spec = self.full(*tables[0].shape)
        return self.call(
            body, (place,), (1,), [spec] * 4, tables, spec, jax.ShapeDtypeStruct(tables[0].shape, jnp.int32)
        )

    def row_index(self, role, z, sender_x):
        return (owner(role, z) ^ z) * 2 + sender_x

    def joined(self, role, k, place, rows, sums, slots, after=()):
        def body(place, rows, sums, slots, out):
            out[...] = sums[0]
            row_of = self.row_index(role, place[0], 1 - place[1])
            for c in range(self.cap):
                row = rows[row_of, c]
                chunk, spot = self.spot(row)
                out[spot] += jnp.where((row >= 0) & (chunk == k), slots[c], 0.0)

        return self.call(
            body, (place, rows), (1,),
            [pl.BlockSpec((1, self.per_chunk, self.slices, TB), lambda *_: (role, k, 0, 0)), self.slots_spec()],
            (sums, slots), self.dense_spec(), self.dense(), after=after,
        )

    def means(self, k, pieces, inverse):
        def body(own, near, inner, outer, inverse, out):
            for part in range(self.parts):
                for j in range(self.per_piece):
                    spot, block = part * self.per_piece + j, self.block(k, part, j)
                    total = own[spot] + near[spot] + inner[spot] + outer[spot]
                    out[spot] = total * inverse[block : block + 1, :]

        return self.call(
            body, (), (1,), [self.dense_spec()] * 4 + [self.full(self.blocks, TB)], (*pieces, inverse),
            self.dense_spec(), self.dense(),
        )

    def turned(self, feats, cotangent):
        def body(feats, cotangent, feats_out, cotangent_out):
            feats_out[...] = feats[...]
            cotangent_out[...] = cotangent[...].T

        rows, cols = cotangent.shape
        whole, turned = self.full(*feats.shape), self.full(cols, rows)
        return self.call(
            body, (), (1,), [whole, self.full(rows, cols)], (feats, cotangent), [whole, turned],
            [jax.ShapeDtypeStruct(feats.shape, F32), jax.ShapeDtypeStruct((cols, rows), F32)],
        )

    def copied(self, table):
        def body(table, out):
            out[...] = table[...]

        spec = self.full(*table.shape)
        return self.call(body, (), (1,), [spec], (table,), spec, jax.ShapeDtypeStruct(table.shape, table.dtype))

    def feats_of(self, place):
        y, core = place[2], place[3]
        return (2 * y + core, 2 * (1 - y) + core, 2 * y + 1 - core, 2 * (1 - y) + 1 - core)

    def times_weight(self, weight_t, high, low):
        rows = weight_t.shape[0]
        weight_high, weight_low = split(weight_t)
        out = dot_nn(jnp.concatenate([weight_high, weight_low], 0), high)
        return out[:rows] + out[rows:] + dot_nn(weight_high, low)

    def self_part(self, place, slices, w_self, bias):
        def body(place, own, far, core, both, w_self, bias, out, held):
            for index, piece in zip(self.feats_of(place), (own, far, core, both)):
                held[pl.ds(pl.multiple_of(index * self.slices, self.slices), self.slices), :] = piece[...]
            column = jnp.broadcast_to(bias[...], (TB, self.width)).T
            value = self.times_weight(w_self[...].T, *split(held[...]))
            out[0] = value + jnp.concatenate([column] * self.per_piece, 1)

        columns = pl.BlockSpec((self.slices, self.piece), lambda k, part, *_: (0, part * CHUNKS + k))
        return self.call(
            body, (place,), (CHUNKS, self.parts),
            [columns] * 4 + [self.full(self.width, self.width), self.full(1, self.width)], (*slices, w_self, bias),
            pl.BlockSpec((1, self.width, self.piece), lambda k, part, *_: (k, 0, part)),
            jax.ShapeDtypeStruct((CHUNKS, self.width, self.span), F32),
            scratch=[pltpu.VMEM((self.width, self.piece), F32)],
        )

    def activate(self, k, place, means, w_neigh, self_part, cotangents, inverse, activated):
        rows = pl.BlockSpec((self.piece, self.width), lambda *_: (k, 0))

        def body(place, m0, m1, m2, m3, weight, self_part, c0, c1, c2, c3, inverse, *rest):
            out, grad, back, high, low = rest[-5:]
            feats = self.feats_of(place)
            for index, piece in zip(feats, (m0, m1, m2, m3)):
                at = pl.ds(pl.multiple_of(index * self.slices, self.slices), self.slices)
                for spot in range(self.per_chunk):
                    columns = slice(spot * TB, (spot + 1) * TB)
                    high[at, columns], low[at, columns] = split(piece[spot])
            weight_t = weight[...].T
            own_rows = weight[pl.ds(pl.multiple_of(feats[0] * self.slices, self.slices), self.slices), :]
            for part, cotangent in zip(feats, (c0, c1, c2, c3)):
                at = pl.ds(pl.multiple_of(part * self.piece, self.piece), self.piece)
                pre = self.times_weight(weight_t, high[:, at], low[:, at]) + self_part[0, :, at]
                sigma = jax.nn.sigmoid(pre)
                if cotangent is c0:
                    out[...] = (pre * sigma).T
                slope = cotangent[...] * (sigma * (1.0 + pre * (1.0 - sigma)))
                grad[:, at] = slope
                value = self.times_weight(own_rows, *split(slope))
                for j in range(self.per_piece):
                    scale = inverse[pl.ds(self.block(k, part, j), 1), :]
                    back[part * self.per_piece + j] = value[:, j * TB : (j + 1) * TB] * scale

        in_specs = (
            [self.dense_spec()] * 4
            + [self.full(self.width, self.width)]
            + [pl.BlockSpec((1, self.width, self.span), lambda *_: (k, 0, 0))]
            + [pl.BlockSpec((self.width, self.piece), lambda *_: (0, k))] * 4
            + [self.full(self.blocks, TB)]
        )
        args = [*means, w_neigh, self_part, *cotangents, inverse]
        aliases = {}
        if activated is not None:
            aliases = {1 + len(args): 0}
            in_specs.append(pl.BlockSpec(memory_space=pl.ANY))
            args.append(activated)
        return self.call(
            body, (place,), (1,), in_specs, args,
            [rows, self.full(self.width, self.span), self.dense_spec()],
            [jax.ShapeDtypeStruct((self.per_part * TB, self.width), F32),
             jax.ShapeDtypeStruct((self.width, self.span), F32), self.dense()],
            scratch=[pltpu.VMEM((self.width, self.span), BF16)] * 2, aliases=aliases,
        )

    def weight_grad(self, k, place, w_self, feats, means, grad, before):
        last = k == CHUNKS - 1
        rows_all = 2 * self.slices + 16
        shapes = [(rows_all // 2, self.width)] * 2 if last else [(rows_all, self.width)]

        def body(place, w_self, feats, means, grad, *rest):
            total = rest[0][...] if before is not None else jnp.zeros((rows_all, self.width), F32)
            self_out, outs = rest[before is not None], rest[1 + (before is not None) :]
            for part in range(self.parts):
                first = part * self.per_piece
                at = slice(part * self.piece, (part + 1) * self.piece)
                high, low = split(grad[:, at])
                value = self.times_weight(w_self[...], high, low)
                for j in range(self.per_piece):
                    self_out[first + j] = value[:, j * TB : (j + 1) * TB]
                start = self.block(k, part, 0) * TB
                rows = jnp.concatenate(
                    [
                        feats[:, start : start + self.piece],
                        jnp.concatenate([means[first + j] for j in range(self.per_piece)], 1),
                        jnp.ones((16, self.piece), F32),
                    ],
                    0,
                )
                rows_high, rows_low = split(rows)
                total += (dot_nt(rows_high, high) + dot_nt(rows_low, high)) + dot_nt(rows_high, low)
            if last:
                x0 = place[1] == 0
                lower, upper = total[: rows_all // 2], total[rows_all // 2 :]
                outs[0][...] = jnp.where(x0, upper, lower)
                outs[1][...] = jnp.where(x0, lower, upper)
            else:
                outs[0][...] = total

        weight_rows = pl.BlockSpec((self.slices, self.width), lambda i, place, *_: (2 * place[2] + place[3], 0))
        args = [w_self, feats, means, grad] + ([] if before is None else [before])
        return self.call(
            body, (place,), (1,),
            [weight_rows, self.full(self.slices, self.owned), self.dense_spec(), self.full(self.width, self.span)]
            + [self.full(rows_all, self.width)] * (before is not None),
            args, [self.dense_spec()] + [self.full(*shape) for shape in shapes],
            [self.dense()] + [jax.ShapeDtypeStruct(shape, F32) for shape in shapes],
        )

    def both_halves(self, place, mine, other):
        half = mine.shape[0]

        def body(place, mine, other, out):
            out[pl.ds(pl.multiple_of(place[1] * half, 8), half), :] = mine[...]
            out[pl.ds(pl.multiple_of((1 - place[1]) * half, 8), half), :] = other[...]

        shape = (2 * half, self.width)
        return self.call(
            body, (place,), (1,), [self.full(*mine.shape)] * 2, (mine, other), self.full(*shape),
            jax.ShapeDtypeStruct(shape, F32),
        )

    def both_cores(self, place, mine, other):
        def body(place, mine, other, out):
            out[place[3]] = mine[...]
            out[1 - place[3]] = other[...]

        shape = (2, *mine.shape)
        return self.call(
            body, (place,), (1,), [self.full(*mine.shape)] * 2, (mine, other), self.full(*shape),
            jax.ShapeDtypeStruct(shape, F32),
        )

    def whole_weights(self, place, mine, other):
        def body(place, mine, other, w_self, w_neigh, bias):
            for y, block in ((place[2], mine), (1 - place[2], other)):
                for core in range(2):
                    at = pl.ds(pl.multiple_of((2 * y + core) * self.slices, self.slices), self.slices)
                    w_self[at, :] = block[core, : self.slices, :]
                    w_neigh[at, :] = block[core, self.slices : 2 * self.slices, :]
            bias[...] = mine[0, 2 * self.slices : 2 * self.slices + 1, :]

        square, row = (self.width, self.width), (1, self.width)
        return self.call(
            body, (place,), (1,), [self.full(*mine.shape)] * 2, (mine, other),
            [self.full(*square), self.full(*square), self.full(*row)],
            [jax.ShapeDtypeStruct(shape, F32) for shape in (square, square, row)],
        )

    def gather(self, place, sources, held):
        outer = (place[0] == 0) | (place[0] == 3)
        for k in range(CHUNKS):
            spots = slice(k * self.per_chunk, (k + 1) * self.per_chunk)
            if len(sources) == CHUNKS:
                held[spots] = sources[k][...]
            else:

                @pl.when(outer)
                def _():
                    held[spots] = sources[CHUNKS + k][...]

                @pl.when(jnp.logical_not(outer))
                def _():
                    held[spots] = sources[k][...]

    def held(self):
        return pltpu.VMEM((self.blocks, self.slices, TB), F32)

    def pick(self, row, held):
        chunk, spot = self.spot(row)
        return jnp.where(row >= 0, held[chunk * self.per_chunk + spot], 0.0)

    def picked(self, role, place, rows, sources):
        def body(place, rows, *rest):
            out, held = rest[-2:]
            self.gather(place, rest[:-2], held)
            row_of = self.row_index(role, place[0], 1 - place[1])
            for c in range(self.cap):
                out[c] = self.pick(rows[row_of, c], held)

        return self.call(
            body, (place, rows), (1,), [self.dense_spec()] * len(sources), sources,
            self.slots_spec(), self.slots(), scratch=[self.held()],
        )

    def spread(self, place, cols, rows, tiles, jobs, total=None, self_back=None):
        counts = [len(sources) for _, sources in jobs]
        extra = [total] if self_back is None else list(self_back)

        def body(place, cols, rows, tiles, *rest):
            arrays, more = rest[: sum(counts)], rest[sum(counts) : sum(counts) + len(extra)]
            out, held, buffer, sems = rest[sum(counts) + len(extra) :]
            z, x = place[0], place[1]
            owners = [owner(role, z) * 2 + (1 - x if n == 1 else x) for (role, _), n in zip(jobs, counts)]
            copies = [self.fetch(tiles, buffer, sems, owned_by, i) for i, owned_by in enumerate(owners)]
            for copy in copies:
                copy.start()
            if self_back is None:
                out[...] = more[0][...]
            else:
                for k, back in enumerate(more):
                    for part in range(self.parts):
                        for j in range(self.per_piece):
                            block = self.block(k, part, j)
                            out[:, block * TB : (block + 1) * TB] = back[part * self.per_piece + j]
            for i, (role, _) in enumerate(jobs):
                sources = arrays[sum(counts[:i]) : sum(counts[: i + 1])]
                if counts[i] > 1:
                    self.gather(place, sources, held)
                copies[i].wait()
                for c in range(self.cap):
                    if counts[i] > 1:
                        value = self.pick(rows[self.row_index(role, z, x), c], held)
                    else:
                        value = sources[0][c]
                    out[:, lanes(cols[owners[i], c])] += times_tile(value, buffer[i, c])

        whole = self.full(self.slices, self.owned)
        in_specs, args = [self.tiles_spec()], [tiles]
        for _, sources in jobs:
            in_specs += [self.slots_spec() if len(sources) == 1 else self.dense_spec()] * len(sources)
            args += sources
        in_specs += [whole] if self_back is None else [self.dense_spec()] * CHUNKS
        args += extra
        return self.call(
            body, (place, cols, rows), (1,), in_specs, args, whole,
            jax.ShapeDtypeStruct((self.slices, self.owned), F32),
            scratch=[self.held(), *self.fetched(len(jobs))],
            aliases={3 + len(args) - 1: 0} if self_back is None else {}, vmem=TILE_VMEM_BYTES,
        )


def pairs_z(steps):
    return [(2 * a + x, 2 * b + x) for a, b in steps for x in range(2)]


INWARD = pairs_z([(0, 1), (3, 2)])
ACROSS = pairs_z([(1, 2), (2, 1)])
OUTWARD = pairs_z([(1, 0), (2, 3)])
OTHER_X = [(n, n ^ 1) for n in range(8)]
OTHER_CORE = [(f, f ^ 1) for f in range(4)]
OTHER_Y = [(f, f ^ 2) for f in range(4)]


def along_z(distance):
    return pairs_z([(z, z ^ distance) for z in range(4)])


def node_swap(value, pairs):
    return lax.ppermute(value, "node", pairs)


def feat_swap(value, pairs):
    return lax.ppermute(value, "feat", pairs)


ORDER = [
    ("slots", FAR_OUTER),
    ("table_out",),
    ("turn",),
    ("rows_in",),
    ("local",),
    ("slots", FAR_INNER),
    ("join", FAR_OUTER, 0),
    ("join", FAR_INNER, 0),
    ("slots", NEAR),
    ("pass_on", FAR_OUTER, 0),
    ("feats_on",),
    ("join", FAR_OUTER, 1),
    ("join", NEAR, 0),
    ("pass_on", FAR_INNER, 0),
    ("slots", SELF),
    ("pass_on", NEAR, 0),
    ("self_part",),
    ("pass_on", FAR_OUTER, 1),
    ("join", SELF, 0),
    ("join", FAR_INNER, 1),
    ("mean", 0),
    ("cotangents_on",),
    ("join", SELF, 1),
    ("join", NEAR, 1),
    ("pass_on", NEAR, 1),
    ("pass_on", FAR_INNER, 1),
    ("means_on", 0),
    ("activate", 0),
    ("mean", 1),
    ("inner_on", 0),
    ("means_on", 1),
    ("near_on", 0),
    ("weight", 0),
    ("activate", 1),
    ("weight", 1),
    ("weight_x",),
    ("outer_on", 0),
    ("pick", SELF),
    ("inner_on", 1),
    ("weight_near",),
    ("near_on", 1),
    ("weight_far",),
    ("pick", NEAR),
    ("spread", SELF, None),
    ("spread", NEAR, SELF),
    ("outer_on", 1),
    ("pick", FAR_INNER),
    ("weight_halves",),
    ("pick", FAR_OUTER),
    ("weight_cores",),
    ("spread", FAR_INNER, NEAR),
    ("spread", FAR_OUTER, FAR_INNER),
    ("weight_whole",),
    ("spread", None, FAR_OUTER),
]


class Steps:
    def __init__(self, layer, place, node_feats, tiles, send_col, recv_row, inverse, w_self, w_neigh, bias, cotangent):
        self.layer, self.place, self.feats, self.tiles = layer, place, node_feats, tiles
        self.cols, self.table, self.inverse = send_col, recv_row, inverse
        self.w_self, self.w_neigh, self.bias, self.cotangent = w_self, w_neigh, bias, cotangent
        self.slots_in, self.joined, self.inward, self.returned = {}, {}, {}, {}
        self.sent = []
        self.across, self.outward, self.means, self.mean_parts = {}, {}, {}, {}
        self.grads, self.own, self.near, self.inner, self.outer = {}, {}, {}, {}, {}
        self.self_back, self.activated, self.weights, self.total = {}, None, None, None

    def slots(self, role):
        after = [self.slots_in[role - 1]] if role else []
        part = self.layer.partial(role, self.place, self.cols, self.feats, self.tiles, after=after)
        self.slots_in[role] = node_swap(part, OTHER_X)

    def table_out(self):
        table = self.layer.copied(self.table)
        self.tables = [self.table] + [node_swap(table, along_z(distance)) for distance in (1, 2, 3)]

    def rows_in(self):
        self.rows = self.layer.own_rows(self.place, self.tables)

    def local(self):
        self.sums = self.layer.local(self.place, self.cols, self.rows, self.feats, self.tiles)

    def turn(self):
        feats, cotangent = self.layer.turned(self.feats, self.cotangent)
        self.feat_parts = [self.feats, feat_swap(feats, OTHER_Y), feat_swap(feats, OTHER_CORE)]
        self.cotangents = [cotangent, feat_swap(cotangent, OTHER_Y), feat_swap(cotangent, OTHER_CORE)]

    def on(self, parts):
        parts[1] = self.layer.relay(parts[1])
        parts.append(feat_swap(parts[1], OTHER_CORE))

    def feats_on(self):
        self.on(self.feat_parts)

    def cotangents_on(self):
        self.on(self.cotangents)

    def self_part(self):
        self.self_parts = self.layer.self_part(self.place, self.feat_parts, self.w_self, self.bias)

    def join(self, role, k):
        after = [] if role == SELF else self.sent[-2:-1]
        part = self.layer.joined(role, k, self.place, self.rows, self.sums, self.slots_in[role], after=after)
        self.joined[role, k] = part
        if role != SELF:
            self.inward[role, k] = node_swap(part, INWARD)
            self.sent.append(self.inward[role, k])

    def pass_on(self, role, k):
        if role == NEAR:
            part = self.layer.added(self.joined[NEAR, k], self.across[FAR_OUTER, k])
            self.outward[k] = node_swap(part, OUTWARD)
        else:
            part = self.layer.added(self.joined[role, k], self.inward[role, k])
            self.across[role, k] = node_swap(part, ACROSS)

    def mean(self, k):
        pieces = (self.joined[SELF, k], self.inward[NEAR, k], self.across[FAR_INNER, k], self.outward[k])
        means = self.layer.means(k, pieces, self.inverse)
        self.means[k] = means
        self.mean_parts[k] = [means, feat_swap(means, OTHER_Y), feat_swap(means, OTHER_CORE)]

    def means_on(self, k):
        self.on(self.mean_parts[k])

    def activate(self, k):
        self.activated, self.grads[k], back = self.layer.activate(
            k, self.place, self.mean_parts[k], self.w_neigh, self.self_parts, self.cotangents, self.inverse, self.activated
        )
        self.own[k] = back
        self.near[k] = node_swap(back, along_z(1))
        self.inner[k] = [node_swap(back, ACROSS)]

    def near_on(self, k):
        self.near[k] = self.layer.relay(self.near[k])
        self.outer[k] = [node_swap(self.near[k], ACROSS)]

    def inner_on(self, k):
        self.inner[k][0] = self.layer.relay(self.inner[k][0])
        self.inner[k].append(node_swap(self.inner[k][0], OUTWARD))

    def outer_on(self, k):
        self.outer[k][0] = self.layer.relay(self.outer[k][0])
        self.outer[k].append(node_swap(self.outer[k][0], OUTWARD))

    def weight(self, k):
        back, *weights = self.layer.weight_grad(
            k, self.place, self.w_self, self.feats, self.means[k], self.grads[k], self.weights
        )
        self.self_back[k] = back
        if k == CHUNKS - 1:
            send, self.weights = weights
            self.weights_in = node_swap(send, OTHER_X)
        else:
            self.weights = weights[0]

    def weight_x(self):
        self.weights = self.layer.added(self.weights, self.weights_in)
        self.weights_in = node_swap(self.weights, along_z(1))

    def weight_near(self):
        self.weights = self.layer.added(self.weights, self.weights_in)
        self.weights_in = node_swap(self.weights, along_z(3))

    def weight_far(self):
        self.weights = self.layer.added(self.weights, self.weights_in)
        self.weights_in = node_swap(self.weights, OTHER_X)

    def weight_halves(self):
        self.weights = self.layer.both_halves(self.place, self.weights, self.weights_in)
        self.weights_in = feat_swap(self.weights, OTHER_CORE)

    def weight_cores(self):
        self.weights = self.layer.both_cores(self.place, self.weights, self.weights_in)
        self.weights_in = feat_swap(self.weights, OTHER_Y)

    def weight_whole(self):
        self.weights = self.layer.whole_weights(self.place, self.weights, self.weights_in)

    def sources(self, role):
        if role in (SELF, NEAR):
            return [(self.own if role == SELF else self.near)[k] for k in range(CHUNKS)]
        held = self.inner if role == FAR_INNER else self.outer
        return [held[k][0] for k in range(CHUNKS)] + [held[k][1] for k in range(CHUNKS)]

    def pick(self, role):
        self.returned[role] = node_swap(self.layer.picked(role, self.place, self.rows, self.sources(role)), OTHER_X)

    def spread(self, local, slots):
        jobs = [] if local is None else [(local, self.sources(local))]
        jobs += [] if slots is None else [(slots, [self.returned[slots]])]
        first = self.total is None
        back = [self.self_back[k] for k in range(CHUNKS)] if first else None
        self.total = self.layer.spread(self.place, self.cols, self.rows, self.tiles, jobs, self.total, back)


def chain_shards(node_feats, tiles, send_col, recv_row, degree, w_self, w_neigh, bias, cotangent):
    slices, owned = node_feats.shape
    width = w_self.shape[1]
    layer = Layer(slices, owned, tiles.shape[1], 4, width)
    node, feat = lax.axis_index("node"), lax.axis_index("feat")
    place = jnp.stack([node // 2, node % 2, feat // 2, feat % 2]).astype(jnp.int32)
    inverse = (1.0 / degree.astype(F32)).reshape(-1, TB)
    steps = Steps(
        layer, place, node_feats, tiles, send_col, recv_row, inverse, w_self, w_neigh, bias.reshape(1, width), cotangent
    )
    for name, *arguments in ORDER:
        getattr(steps, name)(*arguments)
    grad_self, grad_neigh, grad_bias = steps.weights
    return (steps.activated, steps.total, grad_self, grad_neigh, grad_bias.reshape(width))


def slot_shards(node_feats, tiles, send_col, recv_row, degree, w_self, w_neigh, bias, cotangent):
    slices, owned = node_feats.shape
    blocks = owned // TB
    block_ids = jnp.arange(blocks, dtype=jnp.int32)
    scale = degree.astype(F32)[None, :]
    col_onehot = (send_col[..., None] == block_ids).astype(F32)
    row_onehot = (recv_row[..., None] == block_ids).astype(F32)
    feat_blocks = node_feats.reshape(slices, blocks, TB)
    picked = jnp.einsum("dcb,fbj->dcfj", col_onehot, feat_blocks, precision=HIGH)
    partial_value = jnp.einsum("dcfj,dcij->dcfi", picked, tiles, precision=HIGH)
    arrived = lax.all_to_all(partial_value, "node", split_axis=0, concat_axis=0, tiled=True)
    summed = jnp.einsum("scfi,scb->fbi", arrived, row_onehot, precision=HIGH)
    neighbour = summed.reshape(slices, owned) / scale
    offset = lax.axis_index("feat") * slices
    self_rows = lax.dynamic_slice_in_dim(w_self, offset, slices, 0)
    neigh_rows = lax.dynamic_slice_in_dim(w_neigh, offset, slices, 0)
    dims = (((0,), (0,)), ((), ()))
    first = lax.dot_general(node_feats, self_rows, dims, precision=HIGH)
    second = lax.dot_general(neighbour, neigh_rows, dims, precision=HIGH)
    pre = lax.psum_scatter(first + second, "feat", scatter_dimension=0, tiled=True) + bias
    sigma = jax.nn.sigmoid(pre)
    activated = pre * sigma
    gpre = cotangent * sigma * (1.0 + pre * (1.0 - sigma))
    piece = lax.all_gather(gpre, "feat", axis=0, tiled=True)
    dims = (((1,), (1,)), ((), ()))
    self_back = lax.dot_general(self_rows, piece, dims, precision=HIGH)
    neigh_back = lax.dot_general(neigh_rows, piece, dims, precision=HIGH)
    slice_self = jnp.dot(node_feats, piece, precision=HIGH)
    slice_neigh = jnp.dot(neighbour, piece, precision=HIGH)
    sums = lax.psum((slice_self, slice_neigh, jnp.sum(piece, axis=0)), "node")
    grad_self, grad_neigh = (lax.all_gather(part, "feat", axis=0, tiled=True) for part in sums[:2])
    gneigh = (neigh_back / scale).reshape(slices, blocks, TB)
    outgoing = jnp.einsum("scb,fbi->scfi", row_onehot, gneigh, precision=HIGH)
    returned = lax.all_to_all(outgoing, "node", split_axis=0, concat_axis=0, tiled=True)
    spread = jnp.einsum("dcfi,dcij->dcfj", returned, tiles, precision=HIGH)
    placed = jnp.einsum("dcfj,dcb->fbj", spread, col_onehot, precision=HIGH)
    grad_feats = self_back + placed.reshape(slices, owned)
    return (activated, grad_feats, grad_self, grad_neigh, sums[2])


def solution(mesh):
    chain = mesh.shape["node"] == 8 and mesh.shape["feat"] == 4
    return jax.shard_map(
        chain_shards if chain else slot_shards,
        mesh=mesh,
        in_specs=(
            P("feat", "node"),
            P("node", None, None, None),
            P("node", None),
            P("node", None),
            P("node"),
            P(),
            P(),
            P(),
            P(("node", "feat"), None),
        ),
        out_specs=(P(("node", "feat"), None), P("feat", "node"), P(), P(), P()),
        check_vma=False,
    )
```

```python
import jax
import jax.numpy as jnp
from jax import lax
from jax.experimental import pallas as pl
from jax.experimental.pallas import tpu as pltpu
from jax.sharding import PartitionSpec as P

TB = 128
F32 = jnp.float32
BF16 = jnp.bfloat16
HIGH = lax.Precision.HIGH
CHUNKS = 2
VMEM_BYTES = 28 * 2**20

FAR_OUTER, FAR_INNER, NEAR, SELF = range(4)


def owner(role, z):
    if role == FAR_OUTER:
        return jnp.where(z < 2, 3, 0)
    if role == FAR_INNER:
        return jnp.where(z < 2, 2, 1)
    if role == NEAR:
        return z + 1 - 2 * (z % 2)
    return z


def split(value):
    high = value.astype(BF16)
    return high, (value - high.astype(F32)).astype(BF16)


def dot_nn(a, b):
    return lax.dot_general(a, b, (((1,), (0,)), ((), ())), preferred_element_type=F32)


def dot_nt(a, b):
    return lax.dot_general(a, b, (((1,), (1,)), ((), ())), preferred_element_type=F32)


def stacked(value):
    high, low = split(value)
    return jnp.concatenate(
        [jnp.concatenate([high, high], 1), jnp.concatenate([low, jnp.zeros_like(low)], 1)], 0
    )


def times_tile_t(value, tile):
    rows = value.shape[0]
    out = dot_nt(stacked(value), jnp.concatenate(split(tile), 1))
    return out[:rows] + out[rows:]


def times_tile(value, tile):
    rows = value.shape[0]
    out = dot_nn(stacked(value), jnp.concatenate(split(tile), 0))
    return out[:rows] + out[rows:]


def lanes(block):
    return pl.ds(pl.multiple_of(block * TB, TB), TB)


class Layer:
    def __init__(self, slices, owned, cap, parts, width):
        self.slices, self.owned, self.cap, self.parts, self.width = slices, owned, cap, parts, width
        self.blocks = owned // TB
        self.per_part = self.blocks // parts
        self.per_piece = self.per_part // CHUNKS
        self.per_chunk = self.blocks // CHUNKS
        self.piece = self.per_piece * TB
        self.span = self.per_chunk * TB
        self.token = None
        self.pending = []

    def spot(self, row):
        row = jnp.maximum(row, 0)
        part, inside = row // self.per_part, row % self.per_part
        return inside // self.per_piece, part * self.per_piece + inside % self.per_piece

    def block(self, chunk, part, inside):
        return part * self.per_part + chunk * self.per_piece + inside

    def full(self, *shape):
        return pl.BlockSpec(shape, lambda *_: (0,) * len(shape))

    def dense_spec(self):
        return self.full(self.per_chunk, self.slices, TB)

    def slots_spec(self):
        return self.full(self.cap, self.slices, TB)

    def slots(self):
        return jax.ShapeDtypeStruct((self.cap, self.slices, TB), F32)

    def dense(self):
        return jax.ShapeDtypeStruct((self.per_chunk, self.slices, TB), F32)

    def call(self, body, scalars, grid, in_specs, args, out_specs, out_shape, scratch=(), aliases=None, after=()):
        given = len(scalars) + len(args)
        waits = list(after) + self.pending + ([] if self.token is None else [self.token])
        self.pending = []

        def ordered(*refs):
            body(*refs[:given], *refs[given + len(waits) :])

        out = pl.pallas_call(
            ordered,
            grid_spec=pltpu.PrefetchScalarGridSpec(
                num_scalar_prefetch=len(scalars),
                grid=grid,
                in_specs=list(in_specs) + [pl.BlockSpec(memory_space=pl.ANY)] * len(waits),
                out_specs=out_specs,
                scratch_shapes=scratch,
            ),
            out_shape=out_shape,
            input_output_aliases=aliases or {},
            compiler_params=pltpu.CompilerParams(vmem_limit_bytes=VMEM_BYTES),
            cost_estimate=pl.CostEstimate(flops=1, bytes_accessed=1, transcendentals=0),
        )(*scalars, *args, *waits)
        self.token = jax.tree.leaves(out)[-1]
        return out

    def relay(self, value):
        def body(value, out):
            pass

        anywhere = pl.BlockSpec(memory_space=pl.ANY)
        return self.call(
            body, (), (1,), [anywhere], (value,), anywhere, jax.ShapeDtypeStruct(value.shape, value.dtype),
            aliases={0: 0},
        )

    def added(self, a, b):
        def body(a, b, out):
            out[...] = a[...] + b[...]

        spec = self.full(*a.shape)
        return self.call(body, (), (1,), [spec] * 2, (a, b), spec, jax.ShapeDtypeStruct(a.shape, F32))

    def fetched(self, count):
        return [pltpu.VMEM((count, self.cap, TB, TB), F32), pltpu.SemaphoreType.DMA((count,))]

    def fetch(self, tiles, buffer, sems, index, slot):
        return pltpu.make_async_copy(tiles.at[index], buffer.at[slot], sems.at[slot])

    def tiles_spec(self):
        return pl.BlockSpec(memory_space=pl.ANY)

    def partial(self, role, place, cols, feats, tiles, after=()):
        def body(place, cols, feats, tiles, out, buffer, sems):
            owned_by = owner(role, place[0]) * 2 + 1 - place[1]
            copy = self.fetch(tiles, buffer, sems, owned_by, 0)
            copy.start()
            copy.wait()
            for c in range(self.cap):
                out[c] = times_tile_t(feats[:, lanes(cols[owned_by, c])], buffer[0, c])

        return self.call(
            body, (place, cols), (1,),
            [self.full(self.slices, self.owned), self.tiles_spec()], (feats, tiles),
            self.slots_spec(), self.slots(), scratch=self.fetched(1), after=after,
        )

    def local(self, place, cols, rows, feats, tiles):
        def body(place, cols, rows, feats, tiles, out, buffer, sems):
            z, x = place[0], place[1]
            copies = [self.fetch(tiles, buffer, sems, owner(role, z) * 2 + x, role) for role in range(4)]
            for copy in copies:
                copy.start()
            for role in range(4):
                out[role] = jnp.zeros(out.shape[1:], F32)
                copies[role].wait()
                owned_by, row_of = owner(role, z) * 2 + x, self.row_index(role, z, x)
                for c in range(self.cap):
                    row = rows[row_of, c]
                    chunk, spot = self.spot(row)
                    value = times_tile_t(feats[:, lanes(cols[owned_by, c])], buffer[role, c])
                    out[role, chunk * self.per_chunk + spot] += jnp.where(row >= 0, value, 0.0)

        shape = (4, self.blocks, self.slices, TB)
        return self.call(
            body, (place, cols, rows), (1,),
            [self.full(self.slices, self.owned), self.tiles_spec()], (feats, tiles),
            self.full(*shape), jax.ShapeDtypeStruct(shape, F32), scratch=self.fetched(4),
        )

    def own_rows(self, place, tables):
        def body(place, *refs):
            for distance, table in enumerate(refs[:4]):
                refs[4][2 * distance : 2 * distance + 2, :] = table[pl.ds(2 * place[0], 2), :]

        spec = self.full(*tables[0].shape)
        return self.call(
            body, (place,), (1,), [spec] * 4, tables, spec, jax.ShapeDtypeStruct(tables[0].shape, jnp.int32)
        )

    def row_index(self, role, z, sender_x):
        return (owner(role, z) ^ z) * 2 + sender_x

    def joined(self, role, k, place, rows, sums, slots, after=()):
        def body(place, rows, sums, slots, out):
            out[...] = sums[0]
            row_of = self.row_index(role, place[0], 1 - place[1])
            for c in range(self.cap):
                row = rows[row_of, c]
                chunk, spot = self.spot(row)
                out[spot] += jnp.where((row >= 0) & (chunk == k), slots[c], 0.0)

        return self.call(
            body, (place, rows), (1,),
            [pl.BlockSpec((1, self.per_chunk, self.slices, TB), lambda *_: (role, k, 0, 0)), self.slots_spec()],
            (sums, slots), self.dense_spec(), self.dense(), after=after,
        )

    def means(self, k, pieces, inverse):
        def body(own, near, inner, outer, inverse, out):
            for part in range(self.parts):
                for j in range(self.per_piece):
                    spot, block = part * self.per_piece + j, self.block(k, part, j)
                    total = own[spot] + near[spot] + inner[spot] + outer[spot]
                    out[spot] = total * inverse[block : block + 1, :]

        return self.call(
            body, (), (1,), [self.dense_spec()] * 4 + [self.full(self.blocks, TB)], (*pieces, inverse),
            self.dense_spec(), self.dense(),
        )

    def loaded(self, feats, tiles, cotangent):
        def body(feats, tiles, cotangent, feats_out, tiles_out, cotangent_out, sems):
            copies = [
                pltpu.make_async_copy(feats, feats_out, sems.at[0]),
                pltpu.make_async_copy(tiles, tiles_out, sems.at[1]),
            ]
            for copy in copies:
                copy.start()
            cotangent_out[...] = cotangent[...].T
            for copy in copies:
                copy.wait()

        rows, cols = cotangent.shape
        anywhere = pl.BlockSpec(memory_space=pl.ANY)
        return self.call(
            body, (), (1,), [anywhere, anywhere, self.full(rows, cols)], (feats, tiles, cotangent),
            [anywhere, anywhere, self.full(cols, rows)],
            [pltpu.VMEM(feats.shape, F32), pltpu.VMEM(tiles.shape, F32), jax.ShapeDtypeStruct((cols, rows), F32)],
            scratch=[pltpu.SemaphoreType.DMA((2,))],
        )

    def copied(self, table):
        def body(table, out):
            out[...] = table[...]

        spec = self.full(*table.shape)
        return self.call(body, (), (1,), [spec], (table,), spec, jax.ShapeDtypeStruct(table.shape, table.dtype))

    def feats_of(self, place):
        y, core = place[2], place[3]
        return (2 * y + core, 2 * (1 - y) + core, 2 * y + 1 - core, 2 * (1 - y) + 1 - core)

    def times_weight(self, weight_t, high, low):
        rows = weight_t.shape[0]
        weight_high, weight_low = split(weight_t)
        out = dot_nn(jnp.concatenate([weight_high, weight_low], 0), high)
        return out[:rows] + out[rows:] + dot_nn(weight_high, low)

    def self_part(self, place, slices, w_self, bias):
        def body(place, own, far, core, both, w_self, bias, out, held):
            for index, piece in zip(self.feats_of(place), (own, far, core, both)):
                held[pl.ds(pl.multiple_of(index * self.slices, self.slices), self.slices), :] = piece[...]
            column = jnp.broadcast_to(bias[...], (TB, self.width)).T
            value = self.times_weight(w_self[...].T, *split(held[...]))
            out[0] = value + jnp.concatenate([column] * self.per_piece, 1)

        columns = pl.BlockSpec((self.slices, self.piece), lambda k, part, *_: (0, part * CHUNKS + k))
        return self.call(
            body, (place,), (CHUNKS, self.parts),
            [columns] * 4 + [self.full(self.width, self.width), self.full(1, self.width)], (*slices, w_self, bias),
            pl.BlockSpec((1, self.width, self.piece), lambda k, part, *_: (k, 0, part)),
            jax.ShapeDtypeStruct((CHUNKS, self.width, self.span), F32),
            scratch=[pltpu.VMEM((self.width, self.piece), F32)],
        )

    def activate(self, k, place, means, w_neigh, self_part, cotangents, inverse, activated):
        rows = pl.BlockSpec((self.piece, self.width), lambda *_: (k, 0))

        def body(place, m0, m1, m2, m3, weight, self_part, c0, c1, c2, c3, inverse, *rest):
            out, grad, back, high, low = rest[-5:]
            feats = self.feats_of(place)
            for index, piece in zip(feats, (m0, m1, m2, m3)):
                at = pl.ds(pl.multiple_of(index * self.slices, self.slices), self.slices)
                for spot in range(self.per_chunk):
                    columns = slice(spot * TB, (spot + 1) * TB)
                    high[at, columns], low[at, columns] = split(piece[spot])
            weight_t = weight[...].T
            own_rows = weight[pl.ds(pl.multiple_of(feats[0] * self.slices, self.slices), self.slices), :]
            for part, cotangent in zip(feats, (c0, c1, c2, c3)):
                at = pl.ds(pl.multiple_of(part * self.piece, self.piece), self.piece)
                pre = self.times_weight(weight_t, high[:, at], low[:, at]) + self_part[0, :, at]
                sigma = jax.nn.sigmoid(pre)
                if cotangent is c0:
                    out[...] = (pre * sigma).T
                slope = cotangent[...] * (sigma * (1.0 + pre * (1.0 - sigma)))
                grad[:, at] = slope
                value = self.times_weight(own_rows, *split(slope))
                for j in range(self.per_piece):
                    scale = inverse[pl.ds(self.block(k, part, j), 1), :]
                    back[part * self.per_piece + j] = value[:, j * TB : (j + 1) * TB] * scale

        in_specs = (
            [self.dense_spec()] * 4
            + [self.full(self.width, self.width)]
            + [pl.BlockSpec((1, self.width, self.span), lambda *_: (k, 0, 0))]
            + [pl.BlockSpec((self.width, self.piece), lambda *_: (0, k))] * 4
            + [self.full(self.blocks, TB)]
        )
        args = [*means, w_neigh, self_part, *cotangents, inverse]
        aliases = {}
        if activated is not None:
            aliases = {1 + len(args): 0}
            in_specs.append(pl.BlockSpec(memory_space=pl.ANY))
            args.append(activated)
        return self.call(
            body, (place,), (1,), in_specs, args,
            [rows, self.full(self.width, self.span), self.dense_spec()],
            [jax.ShapeDtypeStruct((self.per_part * TB, self.width), F32),
             jax.ShapeDtypeStruct((self.width, self.span), F32), self.dense()],
            scratch=[pltpu.VMEM((self.width, self.span), BF16)] * 2, aliases=aliases,
        )

    def weight_grad(self, k, place, w_self, feats, means, grad, before):
        last = k == CHUNKS - 1
        rows_all = 2 * self.slices + 16
        shapes = [(rows_all // 2, self.width)] * 2 if last else [(rows_all, self.width)]

        def body(place, w_self, feats, means, grad, *rest):
            total = rest[0][...] if before is not None else jnp.zeros((rows_all, self.width), F32)
            self_out, outs = rest[before is not None], rest[1 + (before is not None) :]
            for part in range(self.parts):
                first = part * self.per_piece
                at = slice(part * self.piece, (part + 1) * self.piece)
                high, low = split(grad[:, at])
                value = self.times_weight(w_self[...], high, low)
                for j in range(self.per_piece):
                    self_out[first + j] = value[:, j * TB : (j + 1) * TB]
                start = self.block(k, part, 0) * TB
                rows = jnp.concatenate(
                    [
                        feats[:, start : start + self.piece],
                        jnp.concatenate([means[first + j] for j in range(self.per_piece)], 1),
                        jnp.ones((16, self.piece), F32),
                    ],
                    0,
                )
                rows_high, rows_low = split(rows)
                total += (dot_nt(rows_high, high) + dot_nt(rows_low, high)) + dot_nt(rows_high, low)
            if last:
                x0 = place[1] == 0
                lower, upper = total[: rows_all // 2], total[rows_all // 2 :]
                outs[0][...] = jnp.where(x0, upper, lower)
                outs[1][...] = jnp.where(x0, lower, upper)
            else:
                outs[0][...] = total

        weight_rows = pl.BlockSpec((self.slices, self.width), lambda i, place, *_: (2 * place[2] + place[3], 0))
        args = [w_self, feats, means, grad] + ([] if before is None else [before])
        return self.call(
            body, (place,), (1,),
            [weight_rows, self.full(self.slices, self.owned), self.dense_spec(), self.full(self.width, self.span)]
            + [self.full(rows_all, self.width)] * (before is not None),
            args, [self.dense_spec()] + [self.full(*shape) for shape in shapes],
            [self.dense()] + [jax.ShapeDtypeStruct(shape, F32) for shape in shapes],
        )

    def both_halves(self, place, mine, other):
        half = mine.shape[0]

        def body(place, mine, other, out):
            out[pl.ds(pl.multiple_of(place[1] * half, 8), half), :] = mine[...]
            out[pl.ds(pl.multiple_of((1 - place[1]) * half, 8), half), :] = other[...]

        shape = (2 * half, self.width)
        return self.call(
            body, (place,), (1,), [self.full(*mine.shape)] * 2, (mine, other), self.full(*shape),
            jax.ShapeDtypeStruct(shape, F32),
        )

    def both_cores(self, place, mine, other):
        def body(place, mine, other, out):
            out[place[3]] = mine[...]
            out[1 - place[3]] = other[...]

        shape = (2, *mine.shape)
        return self.call(
            body, (place,), (1,), [self.full(*mine.shape)] * 2, (mine, other), self.full(*shape),
            jax.ShapeDtypeStruct(shape, F32),
        )

    def whole_weights(self, place, mine, other):
        def body(place, mine, other, w_self, w_neigh, bias):
            for y, block in ((place[2], mine), (1 - place[2], other)):
                for core in range(2):
                    at = pl.ds(pl.multiple_of((2 * y + core) * self.slices, self.slices), self.slices)
                    w_self[at, :] = block[core, : self.slices, :]
                    w_neigh[at, :] = block[core, self.slices : 2 * self.slices, :]
            bias[...] = mine[0, 2 * self.slices : 2 * self.slices + 1, :]

        square, row = (self.width, self.width), (1, self.width)
        return self.call(
            body, (place,), (1,), [self.full(*mine.shape)] * 2, (mine, other),
            [self.full(*square), self.full(*square), self.full(*row)],
            [jax.ShapeDtypeStruct(shape, F32) for shape in (square, square, row)],
        )

    def gather(self, place, sources, held):
        outer = (place[0] == 0) | (place[0] == 3)
        for k in range(CHUNKS):
            spots = slice(k * self.per_chunk, (k + 1) * self.per_chunk)
            if len(sources) == CHUNKS:
                held[spots] = sources[k][...]
            else:

                @pl.when(outer)
                def _():
                    held[spots] = sources[CHUNKS + k][...]

                @pl.when(jnp.logical_not(outer))
                def _():
                    held[spots] = sources[k][...]

    def held(self):
        return pltpu.VMEM((self.blocks, self.slices, TB), F32)

    def pick(self, row, held):
        chunk, spot = self.spot(row)
        return jnp.where(row >= 0, held[chunk * self.per_chunk + spot], 0.0)

    def picked(self, role, place, rows, sources):
        def body(place, rows, *rest):
            out, held = rest[-2:]
            self.gather(place, rest[:-2], held)
            row_of = self.row_index(role, place[0], 1 - place[1])
            for c in range(self.cap):
                out[c] = self.pick(rows[row_of, c], held)

        return self.call(
            body, (place, rows), (1,), [self.dense_spec()] * len(sources), sources,
            self.slots_spec(), self.slots(), scratch=[self.held()],
        )

    def spread(self, place, cols, rows, tiles, jobs, total=None, self_back=None):
        counts = [len(sources) for _, sources in jobs]
        extra = [total] if self_back is None else list(self_back)

        def body(place, cols, rows, tiles, *rest):
            arrays, more = rest[: sum(counts)], rest[sum(counts) : sum(counts) + len(extra)]
            out, done, held, buffer, sems = rest[sum(counts) + len(extra) :]
            done[...] = jnp.zeros_like(done)
            z, x = place[0], place[1]
            owners = [owner(role, z) * 2 + (1 - x if n == 1 else x) for (role, _), n in zip(jobs, counts)]
            copies = [self.fetch(tiles, buffer, sems, owned_by, i) for i, owned_by in enumerate(owners)]
            for copy in copies:
                copy.start()
            if self_back is None:
                out[...] = more[0][...]
            else:
                for k, back in enumerate(more):
                    for part in range(self.parts):
                        for j in range(self.per_piece):
                            block = self.block(k, part, j)
                            out[:, block * TB : (block + 1) * TB] = back[part * self.per_piece + j]
            for i, (role, _) in enumerate(jobs):
                sources = arrays[sum(counts[:i]) : sum(counts[: i + 1])]
                if counts[i] > 1:
                    self.gather(place, sources, held)
                copies[i].wait()
                for c in range(self.cap):
                    if counts[i] > 1:
                        value = self.pick(rows[self.row_index(role, z, x), c], held)
                    else:
                        value = sources[0][c]
                    out[:, lanes(cols[owners[i], c])] += times_tile(value, buffer[i, c])

        whole = self.full(self.slices, self.owned)
        in_specs, args = [self.tiles_spec()], [tiles]
        for _, sources in jobs:
            in_specs += [self.slots_spec() if len(sources) == 1 else self.dense_spec()] * len(sources)
            args += sources
        in_specs += [whole] if self_back is None else [self.dense_spec()] * CHUNKS
        args += extra
        return self.call(
            body, (place, cols, rows), (1,), in_specs, args, [whole, self.full(8, TB)],
            [jax.ShapeDtypeStruct((self.slices, self.owned), F32), jax.ShapeDtypeStruct((8, TB), F32)],
            scratch=[self.held(), *self.fetched(len(jobs))],
            aliases={3 + len(args) - 1: 0} if self_back is None else {},
        )[0]


def pairs_z(steps):
    return [(2 * a + x, 2 * b + x) for a, b in steps for x in range(2)]


INWARD = pairs_z([(0, 1), (3, 2)])
ACROSS = pairs_z([(1, 2), (2, 1)])
OUTWARD = pairs_z([(1, 0), (2, 3)])
OTHER_X = [(n, n ^ 1) for n in range(8)]
OTHER_CORE = [(f, f ^ 1) for f in range(4)]
OTHER_Y = [(f, f ^ 2) for f in range(4)]


def along_z(distance):
    return pairs_z([(z, z ^ distance) for z in range(4)])


def node_swap(value, pairs):
    return lax.ppermute(value, "node", pairs)


def feat_swap(value, pairs):
    return lax.ppermute(value, "feat", pairs)


ORDER = [
    ("load",),
    ("slots", FAR_OUTER),
    ("table_out",),
    ("rows_in",),
    ("local",),
    ("slots", FAR_INNER),
    ("join", FAR_OUTER, 0),
    ("join", FAR_INNER, 0),
    ("pass_on", FAR_OUTER, 0),
    ("slots", NEAR),
    ("join", FAR_OUTER, 1),
    ("join", NEAR, 0),
    ("feats_on",),
    ("slots", SELF),
    ("pass_on", NEAR, 0),
    ("pass_on", FAR_INNER, 0),
    ("join", SELF, 1),
    ("join", SELF, 0),
    ("pass_on", FAR_OUTER, 1),
    ("join", NEAR, 1),
    ("join", FAR_INNER, 1),
    ("mean", 0),
    ("cotangents_on",),
    ("self_part",),
    ("pass_on", NEAR, 1),
    ("pass_on", FAR_INNER, 1),
    ("means_on", 0),
    ("activate", 0),
    ("mean", 1),
    ("near_on", 0),
    ("inner_on", 0),
    ("means_on", 1),
    ("weight", 0),
    ("activate", 1),
    ("outer_on", 0),
    ("wait", "inner", 0, 1),
    ("pick", SELF),
    ("weight", 1),
    ("spread", SELF, None),
    ("wait", "returned", SELF),
    ("wait", "inner", 1, 0),
    ("wait", "near", 1),
    ("near_on", 1),
    ("weight_x",),
    ("inner_on", 1),
    ("pick", NEAR),
    ("wait", "outer", 0, 1),
    ("weight_near",),
    ("outer_on", 1),
    ("spread", NEAR, SELF),
    ("weight_far",),
    ("pick", FAR_INNER),
    ("spread", FAR_INNER, NEAR),
    ("weight_halves",),
    ("pick", FAR_OUTER),
    ("weight_cores",),
    ("wait", "returned", FAR_INNER),
    ("spread", FAR_OUTER, FAR_INNER),
    ("weight_whole",),
    ("spread", None, FAR_OUTER),
]


class Steps:
    def __init__(self, layer, place, node_feats, tiles, send_col, recv_row, inverse, w_self, w_neigh, bias, cotangent):
        self.layer, self.place, self.feats, self.tiles = layer, place, node_feats, tiles
        self.cols, self.table, self.inverse = send_col, recv_row, inverse
        self.w_self, self.w_neigh, self.bias, self.cotangent = w_self, w_neigh, bias, cotangent
        self.slots_in, self.joined, self.inward, self.returned = {}, {}, {}, {}
        self.across, self.outward, self.means, self.mean_parts = {}, {}, {}, {}
        self.grads, self.own, self.near, self.inner, self.outer = {}, {}, {}, {}, {}
        self.self_back, self.activated, self.weights, self.total = {}, None, None, None

    def wait(self, name, *key):
        held = getattr(self, name)
        for index in key:
            held = held[index]
        self.layer.pending.append(held)

    def slots(self, role):
        after = [self.slots_in[role - 1]] if role else []
        part = self.layer.partial(role, self.place, self.cols, self.feats, self.tiles, after=after)
        self.slots_in[role] = node_swap(part, OTHER_X)

    def table_out(self):
        table = self.layer.copied(self.table)
        self.tables = [self.table] + [node_swap(table, along_z(distance)) for distance in (1, 2, 3)]

    def rows_in(self):
        self.rows = self.layer.own_rows(self.place, self.tables)

    def local(self):
        self.sums = self.layer.local(self.place, self.cols, self.rows, self.feats, self.tiles)

    def load(self):
        feats, self.tiles, cotangent = self.layer.loaded(self.feats, self.tiles, self.cotangent)
        self.feats = feats
        self.feat_parts = [feats, feat_swap(feats, OTHER_Y), feat_swap(feats, OTHER_CORE)]
        self.cotangents = [cotangent, feat_swap(cotangent, OTHER_Y), feat_swap(cotangent, OTHER_CORE)]

    def on(self, parts):
        parts[1] = self.layer.relay(parts[1])
        parts.append(feat_swap(parts[1], OTHER_CORE))

    def feats_on(self):
        self.on(self.feat_parts)

    def cotangents_on(self):
        self.on(self.cotangents)

    def self_part(self):
        self.self_parts = self.layer.self_part(self.place, self.feat_parts, self.w_self, self.bias)

    def join(self, role, k):
        early = 3 * k + role - 2
        after = [] if role == SELF or early < 0 else [self.inward[early % 3, early // 3]]
        part = self.layer.joined(role, k, self.place, self.rows, self.sums, self.slots_in[role], after=after)
        self.joined[role, k] = part
        if role != SELF:
            self.inward[role, k] = node_swap(part, INWARD)

    def pass_on(self, role, k):
        if role == NEAR:
            part = self.layer.added(self.joined[NEAR, k], self.across[FAR_OUTER, k])
            self.outward[k] = node_swap(part, OUTWARD)
        else:
            part = self.layer.added(self.joined[role, k], self.inward[role, k])
            self.across[role, k] = node_swap(part, ACROSS)

    def mean(self, k):
        pieces = (self.joined[SELF, k], self.inward[NEAR, k], self.across[FAR_INNER, k], self.outward[k])
        means = self.layer.means(k, pieces, self.inverse)
        self.means[k] = means
        self.mean_parts[k] = [means, feat_swap(means, OTHER_Y), feat_swap(means, OTHER_CORE)]

    def means_on(self, k):
        self.on(self.mean_parts[k])

    def activate(self, k):
        self.activated, self.grads[k], back = self.layer.activate(
            k, self.place, self.mean_parts[k], self.w_neigh, self.self_parts, self.cotangents, self.inverse, self.activated
        )
        self.own[k] = back
        self.near[k] = node_swap(back, along_z(1))
        self.inner[k] = [node_swap(back, ACROSS)]

    def near_on(self, k):
        self.near[k] = self.layer.relay(self.near[k])
        self.outer[k] = [node_swap(self.near[k], ACROSS)]

    def inner_on(self, k):
        self.inner[k][0] = self.layer.relay(self.inner[k][0])
        self.inner[k].append(node_swap(self.inner[k][0], OUTWARD))

    def outer_on(self, k):
        self.outer[k][0] = self.layer.relay(self.outer[k][0])
        self.outer[k].append(node_swap(self.outer[k][0], OUTWARD))

    def weight(self, k):
        back, *weights = self.layer.weight_grad(
            k, self.place, self.w_self, self.feats, self.means[k], self.grads[k], self.weights
        )
        self.self_back[k] = back
        if k == CHUNKS - 1:
            send, self.weights = weights
            self.weights_in = node_swap(send, OTHER_X)
        else:
            self.weights = weights[0]

    def weight_x(self):
        self.weights = self.layer.added(self.weights, self.weights_in)
        self.weights_in = node_swap(self.weights, along_z(1))

    def weight_near(self):
        self.weights = self.layer.added(self.weights, self.weights_in)
        self.weights_in = node_swap(self.weights, along_z(3))

    def weight_far(self):
        self.weights = self.layer.added(self.weights, self.weights_in)
        self.weights_in = node_swap(self.weights, OTHER_X)

    def weight_halves(self):
        self.weights = self.layer.both_halves(self.place, self.weights, self.weights_in)
        self.weights_in = feat_swap(self.weights, OTHER_CORE)

    def weight_cores(self):
        self.weights = self.layer.both_cores(self.place, self.weights, self.weights_in)
        self.weights_in = feat_swap(self.weights, OTHER_Y)

    def weight_whole(self):
        self.weights = self.layer.whole_weights(self.place, self.weights, self.weights_in)

    def sources(self, role):
        if role in (SELF, NEAR):
            return [(self.own if role == SELF else self.near)[k] for k in range(CHUNKS)]
        held = self.inner if role == FAR_INNER else self.outer
        return [held[k][0] for k in range(CHUNKS)] + [held[k][1] for k in range(CHUNKS)]

    def pick(self, role):
        self.returned[role] = node_swap(self.layer.picked(role, self.place, self.rows, self.sources(role)), OTHER_X)

    def spread(self, local, slots):
        jobs = [] if local is None else [(local, self.sources(local))]
        jobs += [] if slots is None else [(slots, [self.returned[slots]])]
        first = self.total is None
        back = [self.self_back[k] for k in range(CHUNKS)] if first else None
        self.total = self.layer.spread(self.place, self.cols, self.rows, self.tiles, jobs, self.total, back)


def chain_shards(node_feats, tiles, send_col, recv_row, degree, w_self, w_neigh, bias, cotangent):
    slices, owned = node_feats.shape
    width = w_self.shape[1]
    layer = Layer(slices, owned, tiles.shape[1], 4, width)
    node, feat = lax.axis_index("node"), lax.axis_index("feat")
    place = jnp.stack([node // 2, node % 2, feat // 2, feat % 2]).astype(jnp.int32)
    inverse = (1.0 / degree.astype(F32)).reshape(-1, TB)
    steps = Steps(
        layer, place, node_feats, tiles, send_col, recv_row, inverse, w_self, w_neigh, bias.reshape(1, width), cotangent
    )
    for name, *arguments in ORDER:
        getattr(steps, name)(*arguments)
    grad_self, grad_neigh, grad_bias = steps.weights
    return (steps.activated, steps.total, grad_self, grad_neigh, grad_bias.reshape(width))


def slot_shards(node_feats, tiles, send_col, recv_row, degree, w_self, w_neigh, bias, cotangent):
    slices, owned = node_feats.shape
    blocks = owned // TB
    block_ids = jnp.arange(blocks, dtype=jnp.int32)
    scale = degree.astype(F32)[None, :]
    col_onehot = (send_col[..., None] == block_ids).astype(F32)
    row_onehot = (recv_row[..., None] == block_ids).astype(F32)
    feat_blocks = node_feats.reshape(slices, blocks, TB)
    picked = jnp.einsum("dcb,fbj->dcfj", col_onehot, feat_blocks, precision=HIGH)
    partial_value = jnp.einsum("dcfj,dcij->dcfi", picked, tiles, precision=HIGH)
    arrived = lax.all_to_all(partial_value, "node", split_axis=0, concat_axis=0, tiled=True)
    summed = jnp.einsum("scfi,scb->fbi", arrived, row_onehot, precision=HIGH)
    neighbour = summed.reshape(slices, owned) / scale
    offset = lax.axis_index("feat") * slices
    self_rows = lax.dynamic_slice_in_dim(w_self, offset, slices, 0)
    neigh_rows = lax.dynamic_slice_in_dim(w_neigh, offset, slices, 0)
    dims = (((0,), (0,)), ((), ()))
    first = lax.dot_general(node_feats, self_rows, dims, precision=HIGH)
    second = lax.dot_general(neighbour, neigh_rows, dims, precision=HIGH)
    pre = lax.psum_scatter(first + second, "feat", scatter_dimension=0, tiled=True) + bias
    sigma = jax.nn.sigmoid(pre)
    activated = pre * sigma
    gpre = cotangent * sigma * (1.0 + pre * (1.0 - sigma))
    piece = lax.all_gather(gpre, "feat", axis=0, tiled=True)
    dims = (((1,), (1,)), ((), ()))
    self_back = lax.dot_general(self_rows, piece, dims, precision=HIGH)
    neigh_back = lax.dot_general(neigh_rows, piece, dims, precision=HIGH)
    slice_self = jnp.dot(node_feats, piece, precision=HIGH)
    slice_neigh = jnp.dot(neighbour, piece, precision=HIGH)
    sums = lax.psum((slice_self, slice_neigh, jnp.sum(piece, axis=0)), "node")
    grad_self, grad_neigh = (lax.all_gather(part, "feat", axis=0, tiled=True) for part in sums[:2])
    gneigh = (neigh_back / scale).reshape(slices, blocks, TB)
    outgoing = jnp.einsum("scb,fbi->scfi", row_onehot, gneigh, precision=HIGH)
    returned = lax.all_to_all(outgoing, "node", split_axis=0, concat_axis=0, tiled=True)
    spread = jnp.einsum("dcfi,dcij->dcfj", returned, tiles, precision=HIGH)
    placed = jnp.einsum("dcfj,dcb->fbj", spread, col_onehot, precision=HIGH)
    grad_feats = self_back + placed.reshape(slices, owned)
    return (activated, grad_feats, grad_self, grad_neigh, sums[2])


def solution(mesh):
    chain = mesh.shape["node"] == 8 and mesh.shape["feat"] == 4
    return jax.shard_map(
        chain_shards if chain else slot_shards,
        mesh=mesh,
        in_specs=(
            P("feat", "node"),
            P("node", None, None, None),
            P("node", None),
            P("node", None),
            P("node"),
            P(),
            P(),
            P(),
            P(("node", "feat"), None),
        ),
        out_specs=(P(("node", "feat"), None), P("feat", "node"), P(), P(), P()),
        check_vma=False,
    )
```

```python
import jax
import jax.numpy as jnp
from jax import lax
from jax.experimental import pallas as pl
from jax.experimental.pallas import tpu as pltpu
from jax.sharding import PartitionSpec as P

TB = 128
F32 = jnp.float32
BF16 = jnp.bfloat16
HIGH = lax.Precision.HIGH
CHUNKS = 2
VMEM_BYTES = 28 * 2**20
FIRST_VMEM_BYTES = 57 * 2**20

FAR_OUTER, FAR_INNER, NEAR, SELF = range(4)


def owner(role, z):
    if role == FAR_OUTER:
        return jnp.where(z < 2, 3, 0)
    if role == FAR_INNER:
        return jnp.where(z < 2, 2, 1)
    if role == NEAR:
        return z + 1 - 2 * (z % 2)
    return z


def split(value):
    high = value.astype(BF16)
    return high, (value - high.astype(F32)).astype(BF16)


def dot_nn(a, b):
    return lax.dot_general(a, b, (((1,), (0,)), ((), ())), preferred_element_type=F32)


def dot_nt(a, b):
    return lax.dot_general(a, b, (((1,), (1,)), ((), ())), preferred_element_type=F32)


def stacked(value):
    high, low = split(value)
    return jnp.concatenate(
        [jnp.concatenate([high, high], 1), jnp.concatenate([low, jnp.zeros_like(low)], 1)], 0
    )


def times_tile_t(value, tile):
    rows = value.shape[0]
    out = dot_nt(stacked(value), jnp.concatenate(split(tile), 1))
    return out[:rows] + out[rows:]


def times_tile(value, tile):
    rows = value.shape[0]
    out = dot_nn(stacked(value), jnp.concatenate(split(tile), 0))
    return out[:rows] + out[rows:]


def lanes(block):
    return pl.ds(pl.multiple_of(block * TB, TB), TB)


class Layer:
    def __init__(self, slices, owned, cap, parts, width):
        self.slices, self.owned, self.cap, self.parts, self.width = slices, owned, cap, parts, width
        self.blocks = owned // TB
        self.per_part = self.blocks // parts
        self.per_piece = self.per_part // CHUNKS
        self.per_chunk = self.blocks // CHUNKS
        self.piece = self.per_piece * TB
        self.span = self.per_chunk * TB
        self.token = None
        self.pending = []

    def spot(self, row):
        row = jnp.maximum(row, 0)
        part, inside = row // self.per_part, row % self.per_part
        return inside // self.per_piece, part * self.per_piece + inside % self.per_piece

    def block(self, chunk, part, inside):
        return part * self.per_part + chunk * self.per_piece + inside

    def full(self, *shape):
        return pl.BlockSpec(shape, lambda *_: (0,) * len(shape))

    def dense_spec(self):
        return self.full(self.per_chunk, self.slices, TB)

    def slots_spec(self):
        return self.full(self.cap, self.slices, TB)

    def slots(self):
        return jax.ShapeDtypeStruct((self.cap, self.slices, TB), F32)

    def dense(self):
        return jax.ShapeDtypeStruct((self.per_chunk, self.slices, TB), F32)

    def call(self, body, scalars, grid, in_specs, args, out_specs, out_shape, scratch=(), aliases=None, after=(), vmem=VMEM_BYTES):
        given = len(scalars) + len(args)
        waits = list(after) + self.pending + ([] if self.token is None else [self.token])
        self.pending = []

        def ordered(*refs):
            body(*refs[:given], *refs[given + len(waits) :])

        out = pl.pallas_call(
            ordered,
            grid_spec=pltpu.PrefetchScalarGridSpec(
                num_scalar_prefetch=len(scalars),
                grid=grid,
                in_specs=list(in_specs) + [pl.BlockSpec(memory_space=pl.ANY)] * len(waits),
                out_specs=out_specs,
                scratch_shapes=scratch,
            ),
            out_shape=out_shape,
            input_output_aliases=aliases or {},
            compiler_params=pltpu.CompilerParams(vmem_limit_bytes=vmem),
            cost_estimate=pl.CostEstimate(flops=1, bytes_accessed=1, transcendentals=0),
        )(*scalars, *args, *waits)
        self.token = jax.tree.leaves(out)[-1]
        return out

    def relay(self, value, after=()):
        def body(value, out):
            pass

        anywhere = pl.BlockSpec(memory_space=pl.ANY)
        return self.call(
            body, (), (1,), [anywhere], (value,), anywhere, jax.ShapeDtypeStruct(value.shape, value.dtype),
            aliases={0: 0}, after=after,
        )

    def added(self, a, b):
        def body(a, b, out):
            out[...] = a[...] + b[...]

        spec = self.full(*a.shape)
        return self.call(body, (), (1,), [spec] * 2, (a, b), spec, jax.ShapeDtypeStruct(a.shape, F32))

    def fetched(self, count):
        return [pltpu.VMEM((count, self.cap, TB, TB), F32), pltpu.SemaphoreType.DMA((count,))]

    def fetch(self, tiles, buffer, sems, index, slot):
        return pltpu.make_async_copy(tiles.at[index], buffer.at[slot], sems.at[slot])

    def tiles_spec(self):
        return pl.BlockSpec(memory_space=pl.ANY)

    def first_slots(self, role, place, cols, feats, tiles):
        groups = 4
        per_group = self.cap // groups

        def body(place, cols, feats, tiles, out, held, buffer, sems):
            owned_by = owner(role, place[0]) * 2 + 1 - place[1]
            copies = [pltpu.make_async_copy(feats, held, sems.at[groups])]
            for g in range(groups):
                some = pl.ds(g * per_group, per_group)
                copies.append(pltpu.make_async_copy(tiles.at[owned_by, some], buffer.at[some], sems.at[g]))
            for copy in copies:
                copy.start()
            for g in range(groups):
                if g == 0:
                    copies[0].wait()
                copies[1 + g].wait()
                for c in range(g * per_group, (g + 1) * per_group):
                    out[c] = times_tile_t(held[:, lanes(cols[owned_by, c])], buffer[c])

        return self.call(
            body, (place, cols), (1,), [self.tiles_spec()] * 2, (feats, tiles), self.slots_spec(), self.slots(),
            scratch=[
                pltpu.VMEM((self.slices, self.owned), F32),
                pltpu.VMEM((self.cap, TB, TB), F32),
                pltpu.SemaphoreType.DMA((groups + 1,)),
            ],
            vmem=FIRST_VMEM_BYTES,
        )

    def later_slots(self, roles, place, cols, feats, tiles):
        def body(place, cols, feats, tiles, *rest):
            outs, (buffer, sems) = rest[: len(roles)], rest[len(roles) :]
            owners = [owner(role, place[0]) * 2 + 1 - place[1] for role in roles]
            copies = [self.fetch(tiles, buffer, sems, owned_by, i) for i, owned_by in enumerate(owners)]
            for copy in copies:
                copy.start()
            for i, owned_by in enumerate(owners):
                copies[i].wait()
                for c in range(self.cap):
                    outs[i][c] = times_tile_t(feats[:, lanes(cols[owned_by, c])], buffer[i, c])

        return self.call(
            body, (place, cols), (1,), [self.full(self.slices, self.owned), self.tiles_spec()], (feats, tiles),
            [self.slots_spec()] * len(roles), [self.slots()] * len(roles), scratch=self.fetched(len(roles)),
        )

    def dense_sums(self, role, place, cols, rows, feats, tiles, slots):
        def body(place, cols, rows, feats, tiles, slots, *rest):
            outs, (buffer, sems) = rest[:CHUNKS], rest[CHUNKS:]
            z, x = place[0], place[1]
            owned_by = owner(role, z) * 2 + x
            copy = self.fetch(tiles, buffer, sems, owned_by, 0)
            copy.start()
            for out in outs:
                out[...] = jnp.zeros_like(out)

            def add(row, value):
                chunk, spot = self.spot(row)
                for k, out in enumerate(outs):
                    out[spot] += jnp.where((row >= 0) & (chunk == k), value, 0.0)

            for c in range(self.cap):
                add(rows[self.row_index(role, z, 1 - x), c], slots[c])
            copy.wait()
            for c in range(self.cap):
                value = times_tile_t(feats[:, lanes(cols[owned_by, c])], buffer[0, c])
                add(rows[self.row_index(role, z, x), c], value)

        return self.call(
            body, (place, cols, rows), (1,),
            [self.full(self.slices, self.owned), self.tiles_spec(), self.slots_spec()], (feats, tiles, slots),
            [self.dense_spec()] * CHUNKS, [self.dense()] * CHUNKS, scratch=self.fetched(1),
        )

    def stacked_tables(self, first, second):
        def body(first, second, out):
            out[: first.shape[0], :] = first[...]
            out[first.shape[0] :, :] = second[...]

        shape = (2 * first.shape[0], first.shape[1])
        return self.call(
            body, (), (1,), [self.full(*first.shape)] * 2, (first, second), self.full(*shape),
            jax.ShapeDtypeStruct(shape, first.dtype),
        )

    def own_rows(self, place, pair, other_pair):
        half = pair.shape[0] // 2

        def body(place, pair, other, out):
            for distance in range(4):
                table = (pair, other)[distance // 2]
                start = half * (distance % 2) + 2 * place[0]
                out[2 * distance : 2 * distance + 2, :] = table[pl.ds(start, 2), :]

        shape = (half, pair.shape[1])
        return self.call(
            body, (place,), (1,), [self.full(*pair.shape)] * 2, (pair, other_pair), self.full(*shape),
            jax.ShapeDtypeStruct(shape, pair.dtype),
        )

    def row_index(self, role, z, sender_x):
        return (owner(role, z) ^ z) * 2 + sender_x

    def means(self, k, pieces, inverse):
        def body(own, near, inner, inverse, out):
            for part in range(self.parts):
                for j in range(self.per_piece):
                    spot, block = part * self.per_piece + j, self.block(k, part, j)
                    total = own[spot] + near[spot] + inner[spot]
                    out[spot] = total * inverse[block : block + 1, :]

        return self.call(
            body, (), (1,), [self.dense_spec()] * 3 + [self.full(self.blocks, TB)], (*pieces, inverse),
            self.dense_spec(), self.dense(),
        )

    def loaded(self, feats, tiles, cotangent):
        def body(feats, tiles, cotangent, feats_out, tiles_out, cotangent_out, sems):
            copies = [
                pltpu.make_async_copy(feats, feats_out, sems.at[0]),
                pltpu.make_async_copy(tiles, tiles_out, sems.at[1]),
            ]
            for copy in copies:
                copy.start()
            cotangent_out[...] = cotangent[...].T
            for copy in copies:
                copy.wait()

        rows, cols = cotangent.shape
        anywhere = pl.BlockSpec(memory_space=pl.ANY)
        return self.call(
            body, (), (1,), [anywhere, anywhere, self.full(rows, cols)], (feats, tiles, cotangent),
            [anywhere, anywhere, self.full(cols, rows)],
            [pltpu.VMEM(feats.shape, F32), pltpu.VMEM(tiles.shape, F32), jax.ShapeDtypeStruct((cols, rows), F32)],
            scratch=[pltpu.SemaphoreType.DMA((2,))],
        )

    def copied(self, table):
        def body(table, out):
            out[...] = table[...]

        spec = self.full(*table.shape)
        return self.call(body, (), (1,), [spec], (table,), spec, jax.ShapeDtypeStruct(table.shape, table.dtype))

    def feats_of(self, place):
        y, core = place[2], place[3]
        return (2 * y + core, 2 * (1 - y) + core, 2 * y + 1 - core, 2 * (1 - y) + 1 - core)

    def times_weight(self, weight_t, high, low):
        rows = weight_t.shape[0]
        weight_high, weight_low = split(weight_t)
        out = dot_nn(jnp.concatenate([weight_high, weight_low], 0), high)
        return out[:rows] + out[rows:] + dot_nn(weight_high, low)

    def self_part(self, place, slices, w_self, bias):
        def body(place, own, far, core, both, w_self, bias, out, held):
            for index, piece in zip(self.feats_of(place), (own, far, core, both)):
                held[pl.ds(pl.multiple_of(index * self.slices, self.slices), self.slices), :] = piece[...]
            column = jnp.broadcast_to(bias[...], (TB, self.width)).T
            value = self.times_weight(w_self[...].T, *split(held[...]))
            out[0] = value + jnp.concatenate([column] * self.per_piece, 1)

        columns = pl.BlockSpec((self.slices, self.piece), lambda k, part, *_: (0, part * CHUNKS + k))
        return self.call(
            body, (place,), (CHUNKS, self.parts),
            [columns] * 4 + [self.full(self.width, self.width), self.full(1, self.width)], (*slices, w_self, bias),
            pl.BlockSpec((1, self.width, self.piece), lambda k, part, *_: (k, 0, part)),
            jax.ShapeDtypeStruct((CHUNKS, self.width, self.span), F32),
            scratch=[pltpu.VMEM((self.width, self.piece), F32)],
        )

    def activate(self, k, place, means, w_neigh, self_part, cotangents, inverse, activated):
        rows = pl.BlockSpec((self.piece, self.width), lambda *_: (k, 0))

        def body(place, m0, m1, m2, m3, weight, self_part, c0, c1, c2, c3, inverse, *rest):
            out, grad, back, high, low = rest[-5:]
            feats = self.feats_of(place)
            for index, piece in zip(feats, (m0, m1, m2, m3)):
                at = pl.ds(pl.multiple_of(index * self.slices, self.slices), self.slices)
                for spot in range(self.per_chunk):
                    columns = slice(spot * TB, (spot + 1) * TB)
                    high[at, columns], low[at, columns] = split(piece[spot])
            weight_t = weight[...].T
            own_rows = weight[pl.ds(pl.multiple_of(feats[0] * self.slices, self.slices), self.slices), :]
            for part, cotangent in zip(feats, (c0, c1, c2, c3)):
                at = pl.ds(pl.multiple_of(part * self.piece, self.piece), self.piece)
                pre = self.times_weight(weight_t, high[:, at], low[:, at]) + self_part[0, :, at]
                sigma = jax.nn.sigmoid(pre)
                if cotangent is c0:
                    out[...] = (pre * sigma).T
                slope = cotangent[...] * (sigma * (1.0 + pre * (1.0 - sigma)))
                grad[:, at] = slope
                value = self.times_weight(own_rows, *split(slope))
                for j in range(self.per_piece):
                    scale = inverse[pl.ds(self.block(k, part, j), 1), :]
                    back[part * self.per_piece + j] = value[:, j * TB : (j + 1) * TB] * scale

        in_specs = (
            [self.dense_spec()] * 4
            + [self.full(self.width, self.width)]
            + [pl.BlockSpec((1, self.width, self.span), lambda *_: (k, 0, 0))]
            + [pl.BlockSpec((self.width, self.piece), lambda *_: (0, k))] * 4
            + [self.full(self.blocks, TB)]
        )
        args = [*means, w_neigh, self_part, *cotangents, inverse]
        aliases = {}
        if activated is not None:
            aliases = {1 + len(args): 0}
            in_specs.append(pl.BlockSpec(memory_space=pl.ANY))
            args.append(activated)
        return self.call(
            body, (place,), (1,), in_specs, args,
            [rows, self.full(self.width, self.span), self.dense_spec()],
            [jax.ShapeDtypeStruct((self.per_part * TB, self.width), F32),
             jax.ShapeDtypeStruct((self.width, self.span), F32), self.dense()],
            scratch=[pltpu.VMEM((self.width, self.span), BF16)] * 2, aliases=aliases,
        )

    def weight_grad(self, k, place, w_self, feats, means, grad, before):
        shape = (2 * self.slices + 16, self.width)

        def body(place, w_self, feats, means, grad, *rest):
            self_out, weights_out = rest[-2:]
            total = rest[0][...] if before is not None else jnp.zeros(shape, F32)
            for part in range(self.parts):
                first = part * self.per_piece
                at = slice(part * self.piece, (part + 1) * self.piece)
                high, low = split(grad[:, at])
                value = self.times_weight(w_self[...], high, low)
                for j in range(self.per_piece):
                    self_out[first + j] = value[:, j * TB : (j + 1) * TB]
                start = self.block(k, part, 0) * TB
                rows = jnp.concatenate(
                    [
                        feats[:, start : start + self.piece],
                        jnp.concatenate([means[first + j] for j in range(self.per_piece)], 1),
                        jnp.ones((16, self.piece), F32),
                    ],
                    0,
                )
                rows_high, rows_low = split(rows)
                total += (dot_nt(rows_high, high) + dot_nt(rows_low, high)) + dot_nt(rows_high, low)
            weights_out[...] = total

        weight_rows = pl.BlockSpec((self.slices, self.width), lambda i, place, *_: (2 * place[2] + place[3], 0))
        args = [w_self, feats, means, grad] + ([] if before is None else [before])
        return self.call(
            body, (place,), (1,),
            [weight_rows, self.full(self.slices, self.owned), self.dense_spec(), self.full(self.width, self.span)]
            + [self.full(*shape)] * (before is not None),
            args, [self.dense_spec(), self.full(*shape)], [self.dense(), jax.ShapeDtypeStruct(shape, F32)],
        )

    def both_cores(self, place, mine, other):
        def body(place, mine, other, out):
            out[place[3]] = mine[...]
            out[1 - place[3]] = other[...]

        shape = (2, *mine.shape)
        return self.call(
            body, (place,), (1,), [self.full(*mine.shape)] * 2, (mine, other), self.full(*shape),
            jax.ShapeDtypeStruct(shape, F32),
        )

    def whole_weights(self, place, mine, other):
        def body(place, mine, other, w_self, w_neigh, bias):
            for y, block in ((place[2], mine), (1 - place[2], other)):
                for core in range(2):
                    at = pl.ds(pl.multiple_of((2 * y + core) * self.slices, self.slices), self.slices)
                    w_self[at, :] = block[core, : self.slices, :]
                    w_neigh[at, :] = block[core, self.slices : 2 * self.slices, :]
            bias[...] = mine[0, 2 * self.slices : 2 * self.slices + 1, :]

        square, row = (self.width, self.width), (1, self.width)
        return self.call(
            body, (place,), (1,), [self.full(*mine.shape)] * 2, (mine, other),
            [self.full(*square), self.full(*square), self.full(*row)],
            [jax.ShapeDtypeStruct(shape, F32) for shape in (square, square, row)],
        )

    def gather(self, place, sources, held):
        outer = (place[0] == 0) | (place[0] == 3)
        for k in range(CHUNKS):
            spots = slice(k * self.per_chunk, (k + 1) * self.per_chunk)
            if len(sources) == CHUNKS:
                held[spots] = sources[k][...]
            else:

                @pl.when(outer)
                def _():
                    held[spots] = sources[CHUNKS + k][...]

                @pl.when(jnp.logical_not(outer))
                def _():
                    held[spots] = sources[k][...]

    def held(self):
        return pltpu.VMEM((self.blocks, self.slices, TB), F32)

    def pick(self, row, held):
        chunk, spot = self.spot(row)
        return jnp.where(row >= 0, held[chunk * self.per_chunk + spot], 0.0)

    def picked(self, role, place, rows, sources):
        def body(place, rows, *rest):
            out, held = rest[-2:]
            self.gather(place, rest[:-2], held)
            row_of = self.row_index(role, place[0], 1 - place[1])
            for c in range(self.cap):
                out[c] = self.pick(rows[row_of, c], held)

        return self.call(
            body, (place, rows), (1,), [self.dense_spec()] * len(sources), sources,
            self.slots_spec(), self.slots(), scratch=[self.held()],
        )

    def spread(self, place, cols, rows, tiles, jobs, total=None, self_back=None):
        counts = [len(sources) for _, sources in jobs]
        extra = [total] if self_back is None else list(self_back)

        def body(place, cols, rows, tiles, *rest):
            arrays, more = rest[: sum(counts)], rest[sum(counts) : sum(counts) + len(extra)]
            out, done, held, buffer, sems = rest[sum(counts) + len(extra) :]
            done[...] = jnp.zeros_like(done)
            z, x = place[0], place[1]
            owners = [owner(role, z) * 2 + (1 - x if n == 1 else x) for (role, _), n in zip(jobs, counts)]
            copies = [self.fetch(tiles, buffer, sems, owned_by, i) for i, owned_by in enumerate(owners)]
            for copy in copies:
                copy.start()
            if self_back is None:
                out[...] = more[0][...]
            else:
                for k, back in enumerate(more):
                    for part in range(self.parts):
                        for j in range(self.per_piece):
                            block = self.block(k, part, j)
                            out[:, block * TB : (block + 1) * TB] = back[part * self.per_piece + j]
            for i, (role, _) in enumerate(jobs):
                sources = arrays[sum(counts[:i]) : sum(counts[: i + 1])]
                if counts[i] > 1:
                    self.gather(place, sources, held)
                copies[i].wait()
                for c in range(self.cap):
                    if counts[i] > 1:
                        value = self.pick(rows[self.row_index(role, z, x), c], held)
                    else:
                        value = sources[0][c]
                    out[:, lanes(cols[owners[i], c])] += times_tile(value, buffer[i, c])

        whole = self.full(self.slices, self.owned)
        in_specs, args = [self.tiles_spec()], [tiles]
        for _, sources in jobs:
            in_specs += [self.slots_spec() if len(sources) == 1 else self.dense_spec()] * len(sources)
            args += sources
        in_specs += [whole] if self_back is None else [self.dense_spec()] * CHUNKS
        args += extra
        return self.call(
            body, (place, cols, rows), (1,), in_specs, args, [whole, self.full(8, TB)],
            [jax.ShapeDtypeStruct((self.slices, self.owned), F32), jax.ShapeDtypeStruct((8, TB), F32)],
            scratch=[self.held(), *self.fetched(len(jobs))],
            aliases={3 + len(args) - 1: 0} if self_back is None else {},
        )[0]


def pairs_z(steps):
    return [(2 * a + x, 2 * b + x) for a, b in steps for x in range(2)]


INWARD = pairs_z([(0, 1), (3, 2)])
ACROSS = pairs_z([(1, 2), (2, 1)])
OUTWARD = pairs_z([(1, 0), (2, 3)])
OTHER_X = [(n, n ^ 1) for n in range(8)]
OTHER_CORE = [(f, f ^ 1) for f in range(4)]
OTHER_Y = [(f, f ^ 2) for f in range(4)]


def along_z(distance):
    return pairs_z([(z, z ^ distance) for z in range(4)])


def node_swap(value, pairs):
    return lax.ppermute(value, "node", pairs)


def feat_swap(value, pairs):
    return lax.ppermute(value, "feat", pairs)


ORDER = [
    ("slots_first",),
    ("table_out",),
    ("load",),
    ("tables_out",),
    ("slots_later",),
    ("rows_in",),
    ("dense", FAR_OUTER),
    ("slots", FAR_INNER),
    ("send_in", FAR_OUTER, 1),
    ("pass_on", FAR_OUTER, 0),
    ("dense", FAR_INNER),
    ("slots", NEAR),
    ("send_in", FAR_INNER, 1),
    ("pass_on", FAR_OUTER, 1),
    ("slots", SELF),
    ("dense", NEAR),
    ("pass_on", FAR_INNER, 0),
    ("feats_on",),
    ("pass_on", NEAR, 0),
    ("pass_on", NEAR, 1),
    ("pass_on", FAR_INNER, 1),
    ("dense", SELF),
    ("mean", 0),
    ("cotangents_on",),
    ("self_part",),
    ("means_on", 0),
    ("mean", 1),
    ("activate", 0),
    ("means_on", 1),
    ("weight", 0),
    ("activate", 1),
    ("weight", 1),
    ("near_on", 0),
    ("inner_on", 0),
    ("weight_sum", along_z(1)),
    ("near_on", 1),
    ("pick", SELF),
    ("wait", "inner", 0, 1),
    ("inner_on", 1),
    ("spread", SELF, None),
    ("pick", NEAR),
    ("weight_sum", along_z(3)),
    ("outer_on", 0),
    ("spread", NEAR, SELF),
    ("pick", FAR_INNER),
    ("weight_sum", None),
    ("outer_on", 1),
    ("wait", "outer", 0, 1),
    ("weight_cores",),
    ("spread", FAR_INNER, NEAR),
    ("pick", FAR_OUTER),
    ("wait", "returned", FAR_INNER),
    ("spread", FAR_OUTER, FAR_INNER),
    ("weight_whole",),
    ("spread", None, FAR_OUTER),
]


class Steps:
    def __init__(self, layer, place, node_feats, tiles, send_col, recv_row, inverse, w_self, w_neigh, bias, cotangent):
        self.layer, self.place, self.feats, self.tiles = layer, place, node_feats, tiles
        self.cols, self.table, self.inverse = send_col, recv_row, inverse
        self.w_self, self.w_neigh, self.bias, self.cotangent = w_self, w_neigh, bias, cotangent
        self.slots_in, self.joined, self.inward, self.returned = {}, {}, {}, {}
        self.across, self.nearby, self.means, self.mean_parts = {}, {}, {}, {}
        self.grads, self.own, self.near, self.inner, self.outer = {}, {}, {}, {}, {}
        self.self_back, self.activated, self.weights, self.total = {}, None, None, None

    def wait(self, name, *key):
        held = getattr(self, name)
        for index in key:
            held = held[index]
        self.layer.pending.append(held)

    def slots_first(self):
        part = self.layer.first_slots(FAR_OUTER, self.place, self.cols, self.feats, self.tiles)
        self.slots_in[FAR_OUTER] = node_swap(part, OTHER_X)

    def slots_later(self):
        self.parts = self.layer.later_slots((FAR_INNER, NEAR, SELF), self.place, self.cols, self.feats, self.tiles)

    def slots(self, role):
        part = self.layer.relay(self.parts[role - 1], after=[self.slots_in[role - 1]])
        self.slots_in[role] = node_swap(part, OTHER_X)

    def table_out(self):
        self.table = self.layer.copied(self.table)
        self.table_in = node_swap(self.table, along_z(1))

    def tables_out(self):
        self.tables = self.layer.stacked_tables(self.table, self.table_in)
        self.tables_in = node_swap(self.tables, along_z(2))

    def rows_in(self):
        self.rows = self.layer.own_rows(self.place, self.tables, self.tables_in)

    def load(self):
        feats, self.tiles, cotangent = self.layer.loaded(self.feats, self.tiles, self.cotangent)
        self.feats = feats
        self.feat_parts = [feats, feat_swap(feats, OTHER_Y), feat_swap(feats, OTHER_CORE)]
        self.cotangents = [cotangent, feat_swap(cotangent, OTHER_Y), feat_swap(cotangent, OTHER_CORE)]

    def on(self, parts):
        parts[1] = self.layer.relay(parts[1])
        parts.append(feat_swap(parts[1], OTHER_CORE))

    def feats_on(self):
        self.on(self.feat_parts)

    def cotangents_on(self):
        self.on(self.cotangents)

    def self_part(self):
        self.self_parts = self.layer.self_part(self.place, self.feat_parts, self.w_self, self.bias)

    def dense(self, role):
        sums = self.layer.dense_sums(
            role, self.place, self.cols, self.rows, self.feats, self.tiles, self.slots_in[role]
        )
        for k in range(CHUNKS):
            self.joined[role, k] = sums[k]
        if role in (FAR_OUTER, FAR_INNER):
            self.inward[role, 0] = node_swap(sums[0], INWARD)

    def send_in(self, role, k):
        self.joined[role, k] = self.layer.relay(self.joined[role, k])
        self.inward[role, k] = node_swap(self.joined[role, k], INWARD)

    def pass_on(self, role, k):
        if role == NEAR:
            part = self.layer.added(self.joined[NEAR, k], self.across[FAR_OUTER, k])
            self.nearby[k] = node_swap(part, along_z(1))
        else:
            part = self.layer.added(self.joined[role, k], self.inward[role, k])
            self.across[role, k] = node_swap(part, ACROSS)

    def mean(self, k):
        pieces = (self.joined[SELF, k], self.nearby[k], self.across[FAR_INNER, k])
        means = self.layer.means(k, pieces, self.inverse)
        self.means[k] = means
        self.mean_parts[k] = [means, feat_swap(means, OTHER_Y), feat_swap(means, OTHER_CORE)]

    def means_on(self, k):
        self.on(self.mean_parts[k])

    def activate(self, k):
        self.activated, self.grads[k], back = self.layer.activate(
            k, self.place, self.mean_parts[k], self.w_neigh, self.self_parts, self.cotangents, self.inverse, self.activated
        )
        self.own[k] = back
        self.near[k] = node_swap(back, along_z(1))
        self.inner[k] = [node_swap(back, ACROSS)]

    def near_on(self, k):
        self.near[k] = self.layer.relay(self.near[k])
        self.outer[k] = [node_swap(self.near[k], ACROSS)]

    def inner_on(self, k):
        self.inner[k][0] = self.layer.relay(self.inner[k][0])
        self.inner[k].append(node_swap(self.inner[k][0], OUTWARD))

    def outer_on(self, k):
        self.outer[k][0] = self.layer.relay(self.outer[k][0])
        self.outer[k].append(node_swap(self.outer[k][0], OUTWARD))

    def weight(self, k):
        back, weights = self.layer.weight_grad(
            k, self.place, self.w_self, self.feats, self.means[k], self.grads[k], self.weights
        )
        self.self_back[k] = back
        self.weights = weights
        if k == CHUNKS - 1:
            self.weights_in = node_swap(weights, OTHER_X)

    def weight_sum(self, pairs):
        self.weights = self.layer.added(self.weights, self.weights_in)
        if pairs is None:
            self.weights_in = feat_swap(self.weights, OTHER_CORE)
        else:
            self.weights_in = node_swap(self.weights, pairs)

    def weight_cores(self):
        self.weights = self.layer.both_cores(self.place, self.weights, self.weights_in)
        self.weights_in = feat_swap(self.weights, OTHER_Y)

    def weight_whole(self):
        self.weights = self.layer.whole_weights(self.place, self.weights, self.weights_in)

    def sources(self, role):
        if role in (SELF, NEAR):
            return [(self.own if role == SELF else self.near)[k] for k in range(CHUNKS)]
        held = self.inner if role == FAR_INNER else self.outer
        return [held[k][0] for k in range(CHUNKS)] + [held[k][1] for k in range(CHUNKS)]

    def pick(self, role):
        self.returned[role] = node_swap(self.layer.picked(role, self.place, self.rows, self.sources(role)), OTHER_X)

    def spread(self, local, slots):
        jobs = [] if local is None else [(local, self.sources(local))]
        jobs += [] if slots is None else [(slots, [self.returned[slots]])]
        first = self.total is None
        back = [self.self_back[k] for k in range(CHUNKS)] if first else None
        self.total = self.layer.spread(self.place, self.cols, self.rows, self.tiles, jobs, self.total, back)


def chain_shards(node_feats, tiles, send_col, recv_row, degree, w_self, w_neigh, bias, cotangent):
    slices, owned = node_feats.shape
    width = w_self.shape[1]
    layer = Layer(slices, owned, tiles.shape[1], 4, width)
    node, feat = lax.axis_index("node"), lax.axis_index("feat")
    place = jnp.stack([node // 2, node % 2, feat // 2, feat % 2]).astype(jnp.int32)
    inverse = (1.0 / degree.astype(F32)).reshape(-1, TB)
    steps = Steps(
        layer, place, node_feats, tiles, send_col, recv_row, inverse, w_self, w_neigh, bias.reshape(1, width), cotangent
    )
    for name, *arguments in ORDER:
        getattr(steps, name)(*arguments)
    grad_self, grad_neigh, grad_bias = steps.weights
    return (steps.activated, steps.total, grad_self, grad_neigh, grad_bias.reshape(width))


def slot_shards(node_feats, tiles, send_col, recv_row, degree, w_self, w_neigh, bias, cotangent):
    slices, owned = node_feats.shape
    blocks = owned // TB
    block_ids = jnp.arange(blocks, dtype=jnp.int32)
    scale = degree.astype(F32)[None, :]
    col_onehot = (send_col[..., None] == block_ids).astype(F32)
    row_onehot = (recv_row[..., None] == block_ids).astype(F32)
    feat_blocks = node_feats.reshape(slices, blocks, TB)
    picked = jnp.einsum("dcb,fbj->dcfj", col_onehot, feat_blocks, precision=HIGH)
    partial_value = jnp.einsum("dcfj,dcij->dcfi", picked, tiles, precision=HIGH)
    arrived = lax.all_to_all(partial_value, "node", split_axis=0, concat_axis=0, tiled=True)
    summed = jnp.einsum("scfi,scb->fbi", arrived, row_onehot, precision=HIGH)
    neighbour = summed.reshape(slices, owned) / scale
    offset = lax.axis_index("feat") * slices
    self_rows = lax.dynamic_slice_in_dim(w_self, offset, slices, 0)
    neigh_rows = lax.dynamic_slice_in_dim(w_neigh, offset, slices, 0)
    dims = (((0,), (0,)), ((), ()))
    first = lax.dot_general(node_feats, self_rows, dims, precision=HIGH)
    second = lax.dot_general(neighbour, neigh_rows, dims, precision=HIGH)
    pre = lax.psum_scatter(first + second, "feat", scatter_dimension=0, tiled=True) + bias
    sigma = jax.nn.sigmoid(pre)
    activated = pre * sigma
    gpre = cotangent * sigma * (1.0 + pre * (1.0 - sigma))
    piece = lax.all_gather(gpre, "feat", axis=0, tiled=True)
    dims = (((1,), (1,)), ((), ()))
    self_back = lax.dot_general(self_rows, piece, dims, precision=HIGH)
    neigh_back = lax.dot_general(neigh_rows, piece, dims, precision=HIGH)
    slice_self = jnp.dot(node_feats, piece, precision=HIGH)
    slice_neigh = jnp.dot(neighbour, piece, precision=HIGH)
    sums = lax.psum((slice_self, slice_neigh, jnp.sum(piece, axis=0)), "node")
    grad_self, grad_neigh = (lax.all_gather(part, "feat", axis=0, tiled=True) for part in sums[:2])
    gneigh = (neigh_back / scale).reshape(slices, blocks, TB)
    outgoing = jnp.einsum("scb,fbi->scfi", row_onehot, gneigh, precision=HIGH)
    returned = lax.all_to_all(outgoing, "node", split_axis=0, concat_axis=0, tiled=True)
    spread = jnp.einsum("dcfi,dcij->dcfj", returned, tiles, precision=HIGH)
    placed = jnp.einsum("dcfj,dcb->fbj", spread, col_onehot, precision=HIGH)
    grad_feats = self_back + placed.reshape(slices, owned)
    return (activated, grad_feats, grad_self, grad_neigh, sums[2])


def solution(mesh):
    chain = mesh.shape["node"] == 8 and mesh.shape["feat"] == 4
    return jax.shard_map(
        chain_shards if chain else slot_shards,
        mesh=mesh,
        in_specs=(
            P("feat", "node"),
            P("node", None, None, None),
            P("node", None),
            P("node", None),
            P("node"),
            P(),
            P(),
            P(),
            P(("node", "feat"), None),
        ),
        out_specs=(P(("node", "feat"), None), P("feat", "node"), P(), P(), P()),
        check_vma=False,
    )
```

```python
import jax
import jax.numpy as jnp
from jax import lax
from jax.experimental import pallas as pl
from jax.experimental.pallas import tpu as pltpu
from jax.sharding import PartitionSpec as P

TB = 128
F32 = jnp.float32
BF16 = jnp.bfloat16
HIGH = lax.Precision.HIGH
CHUNKS = 2
VMEM_BYTES = 28 * 2**20
FIRST_VMEM_BYTES = 57 * 2**20

FAR_OUTER, FAR_INNER, NEAR, SELF = range(4)


def owner(role, z):
    if role == FAR_OUTER:
        return jnp.where(z < 2, 3, 0)
    if role == FAR_INNER:
        return jnp.where(z < 2, 2, 1)
    if role == NEAR:
        return z + 1 - 2 * (z % 2)
    return z


def inner_place(place):
    return (place[0] == 1) | (place[0] == 2)


def split(value):
    high = value.astype(BF16)
    return high, (value - high.astype(F32)).astype(BF16)


def dot_nn(a, b):
    return lax.dot_general(a, b, (((1,), (0,)), ((), ())), preferred_element_type=F32)


def dot_nt(a, b):
    return lax.dot_general(a, b, (((1,), (1,)), ((), ())), preferred_element_type=F32)


def stacked(value):
    high, low = split(value)
    return jnp.concatenate(
        [jnp.concatenate([high, high], 1), jnp.concatenate([low, jnp.zeros_like(low)], 1)], 0
    )


def times_tile_t(value, tile):
    rows = value.shape[0]
    out = dot_nt(stacked(value), jnp.concatenate(split(tile), 1))
    return out[:rows] + out[rows:]


def times_tile(value, tile):
    rows = value.shape[0]
    out = dot_nn(stacked(value), jnp.concatenate(split(tile), 0))
    return out[:rows] + out[rows:]


def lanes(block):
    return pl.ds(pl.multiple_of(block * TB, TB), TB)


class Layer:
    def __init__(self, slices, owned, cap, parts, width):
        self.slices, self.owned, self.cap, self.parts, self.width = slices, owned, cap, parts, width
        self.blocks = owned // TB
        self.per_part = self.blocks // parts
        self.per_piece = self.per_part // CHUNKS
        self.per_chunk = self.blocks // CHUNKS
        self.piece = self.per_piece * TB
        self.span = self.per_chunk * TB
        self.token = None
        self.pending = []

    def spot(self, row):
        row = jnp.maximum(row, 0)
        part, inside = row // self.per_part, row % self.per_part
        return inside // self.per_piece, part * self.per_piece + inside % self.per_piece

    def block(self, chunk, part, inside):
        return part * self.per_part + chunk * self.per_piece + inside

    def full(self, *shape):
        return pl.BlockSpec(shape, lambda *_: (0,) * len(shape))

    def dense_spec(self):
        return self.full(self.per_chunk, self.slices, TB)

    def slots_spec(self):
        return self.full(self.cap, self.slices, TB)

    def slots(self):
        return jax.ShapeDtypeStruct((self.cap, self.slices, TB), F32)

    def dense(self):
        return jax.ShapeDtypeStruct((self.per_chunk, self.slices, TB), F32)

    def call(self, body, scalars, grid, in_specs, args, out_specs, out_shape, scratch=(), aliases=None, after=(), vmem=VMEM_BYTES):
        given = len(scalars) + len(args)
        waits = list(after) + self.pending + ([] if self.token is None else [self.token])
        self.pending = []

        def ordered(*refs):
            body(*refs[:given], *refs[given + len(waits) :])

        out = pl.pallas_call(
            ordered,
            grid_spec=pltpu.PrefetchScalarGridSpec(
                num_scalar_prefetch=len(scalars),
                grid=grid,
                in_specs=list(in_specs) + [pl.BlockSpec(memory_space=pl.ANY)] * len(waits),
                out_specs=out_specs,
                scratch_shapes=scratch,
            ),
            out_shape=out_shape,
            input_output_aliases=aliases or {},
            compiler_params=pltpu.CompilerParams(vmem_limit_bytes=vmem),
            cost_estimate=pl.CostEstimate(flops=1, bytes_accessed=1, transcendentals=0),
        )(*scalars, *args, *waits)
        self.token = jax.tree.leaves(out)[-1]
        return out

    def relay(self, value, after=()):
        def body(value, out):
            pass

        anywhere = pl.BlockSpec(memory_space=pl.ANY)
        return self.call(
            body, (), (1,), [anywhere], (value,), anywhere, jax.ShapeDtypeStruct(value.shape, value.dtype),
            aliases={0: 0}, after=after,
        )

    def added(self, a, b):
        def body(a, b, out):
            out[...] = a[...] + b[...]

        spec = self.full(*a.shape)
        return self.call(body, (), (1,), [spec] * 2, (a, b), spec, jax.ShapeDtypeStruct(a.shape, F32))

    def added_across(self, place, a, across):
        def body(place, a, across, out):
            out[...] = a[...] + jnp.where(inner_place(place), across[...], 0.0)

        return self.call(body, (place,), (1,), [self.dense_spec()] * 2, (a, across), self.dense_spec(), self.dense())

    def fetched(self, count):
        return [pltpu.VMEM((count, self.cap, TB, TB), F32), pltpu.SemaphoreType.DMA((count,))]

    def fetch(self, tiles, buffer, sems, index, slot):
        return pltpu.make_async_copy(tiles.at[index], buffer.at[slot], sems.at[slot])

    def tiles_spec(self):
        return pl.BlockSpec(memory_space=pl.ANY)

    def first_slots(self, role, place, cols, feats, tiles):
        groups = 4
        per_group = self.cap // groups

        def body(place, cols, feats, tiles, out, done, held, buffer, sems):
            done[...] = jnp.zeros_like(done)
            owned_by = owner(role, place[0]) * 2 + 1 - place[1]
            copies = [pltpu.make_async_copy(feats, held, sems.at[groups])]
            for g in range(groups):
                some = pl.ds(g * per_group, per_group)
                copies.append(pltpu.make_async_copy(tiles.at[owned_by, some], buffer.at[some], sems.at[g]))
            for copy in copies:
                copy.start()
            for g in range(groups):
                if g == 0:
                    copies[0].wait()
                copies[1 + g].wait()
                for c in range(g * per_group, (g + 1) * per_group):
                    out[c] = times_tile_t(held[:, lanes(cols[owned_by, c])], buffer[c])

        return self.call(
            body, (place, cols), (1,), [self.tiles_spec()] * 2, (feats, tiles), [self.slots_spec(), self.full(8, TB)],
            [self.slots(), jax.ShapeDtypeStruct((8, TB), F32)],
            scratch=[
                pltpu.VMEM((self.slices, self.owned), F32),
                pltpu.VMEM((self.cap, TB, TB), F32),
                pltpu.SemaphoreType.DMA((groups + 1,)),
            ],
            vmem=FIRST_VMEM_BYTES,
        )[0]

    def later_slots(self, roles, place, cols, feats, tiles):
        def body(place, cols, feats, tiles, *rest):
            outs, (buffer, sems) = rest[: len(roles)], rest[len(roles) :]
            owners = [owner(role, place[0]) * 2 + 1 - place[1] for role in roles]
            copies = [self.fetch(tiles, buffer, sems, owned_by, i) for i, owned_by in enumerate(owners)]
            for copy in copies:
                copy.start()
            for i, owned_by in enumerate(owners):
                copies[i].wait()
                for c in range(self.cap):
                    outs[i][c] = times_tile_t(feats[:, lanes(cols[owned_by, c])], buffer[i, c])

        return self.call(
            body, (place, cols), (1,), [self.full(self.slices, self.owned), self.tiles_spec()], (feats, tiles),
            [self.slots_spec()] * len(roles), [self.slots()] * len(roles), scratch=self.fetched(len(roles)),
        )

    def dense_sums(self, role, place, cols, rows, feats, tiles, slots):
        def body(place, cols, rows, feats, tiles, slots, *rest):
            outs, (buffer, sems) = rest[:CHUNKS], rest[CHUNKS:]
            z, x = place[0], place[1]
            owned_by = owner(role, z) * 2 + x
            copy = self.fetch(tiles, buffer, sems, owned_by, 0)
            copy.start()
            for out in outs:
                out[...] = jnp.zeros_like(out)

            def add(row, value):
                chunk, spot = self.spot(row)
                for k, out in enumerate(outs):
                    out[spot] += jnp.where((row >= 0) & (chunk == k), value, 0.0)

            for c in range(self.cap):
                add(rows[self.row_index(role, z, 1 - x), c], slots[c])
            copy.wait()
            for c in range(self.cap):
                value = times_tile_t(feats[:, lanes(cols[owned_by, c])], buffer[0, c])
                add(rows[self.row_index(role, z, x), c], value)

        return self.call(
            body, (place, cols, rows), (1,),
            [self.full(self.slices, self.owned), self.tiles_spec(), self.slots_spec()], (feats, tiles, slots),
            [self.dense_spec()] * CHUNKS, [self.dense()] * CHUNKS, scratch=self.fetched(1),
        )

    def stacked_tables(self, first, second):
        def body(first, second, out):
            out[: first.shape[0], :] = first[...]
            out[first.shape[0] :, :] = second[...]

        shape = (2 * first.shape[0], first.shape[1])
        return self.call(
            body, (), (1,), [self.full(*first.shape)] * 2, (first, second), self.full(*shape),
            jax.ShapeDtypeStruct(shape, first.dtype),
        )

    def own_rows(self, place, pair, other_pair):
        half = pair.shape[0] // 2

        def body(place, pair, other, out):
            for distance in range(4):
                table = (pair, other)[distance // 2]
                start = half * (distance % 2) + 2 * place[0]
                out[2 * distance : 2 * distance + 2, :] = table[pl.ds(start, 2), :]

        shape = (half, pair.shape[1])
        return self.call(
            body, (place,), (1,), [self.full(*pair.shape)] * 2, (pair, other_pair), self.full(*shape),
            jax.ShapeDtypeStruct(shape, pair.dtype),
        )

    def row_index(self, role, z, sender_x):
        return (owner(role, z) ^ z) * 2 + sender_x

    def means(self, k, place, pieces, inverse):
        def body(place, own, near, across, inverse, out):
            for part in range(self.parts):
                for j in range(self.per_piece):
                    spot, block = part * self.per_piece + j, self.block(k, part, j)
                    total = own[spot] + near[spot] + jnp.where(inner_place(place), across[spot], 0.0)
                    out[spot] = total * inverse[block : block + 1, :]

        return self.call(
            body, (place,), (1,), [self.dense_spec()] * 3 + [self.full(self.blocks, TB)], (*pieces, inverse),
            self.dense_spec(), self.dense(),
        )

    def loaded(self, feats, tiles, cotangent):
        def body(feats, tiles, cotangent, feats_out, tiles_out, cotangent_out, sems):
            copies = [
                pltpu.make_async_copy(feats, feats_out, sems.at[0]),
                pltpu.make_async_copy(tiles, tiles_out, sems.at[1]),
            ]
            for copy in copies:
                copy.start()
            cotangent_out[...] = cotangent[...].T
            for copy in copies:
                copy.wait()

        rows, cols = cotangent.shape
        anywhere = pl.BlockSpec(memory_space=pl.ANY)
        return self.call(
            body, (), (1,), [anywhere, anywhere, self.full(rows, cols)], (feats, tiles, cotangent),
            [anywhere, anywhere, self.full(cols, rows)],
            [pltpu.VMEM(feats.shape, F32), pltpu.VMEM(tiles.shape, F32), jax.ShapeDtypeStruct((cols, rows), F32)],
            scratch=[pltpu.SemaphoreType.DMA((2,))],
        )

    def copied(self, table):
        def body(table, out):
            out[...] = table[...]

        spec = self.full(*table.shape)
        return self.call(body, (), (1,), [spec], (table,), spec, jax.ShapeDtypeStruct(table.shape, table.dtype))

    def feats_of(self, place):
        y, core = place[2], place[3]
        return (2 * y + core, 2 * (1 - y) + core, 2 * y + 1 - core, 2 * (1 - y) + 1 - core)

    def times_weight(self, weight_t, high, low):
        rows = weight_t.shape[0]
        weight_high, weight_low = split(weight_t)
        out = dot_nn(jnp.concatenate([weight_high, weight_low], 0), high)
        return out[:rows] + out[rows:] + dot_nn(weight_high, low)

    def self_part(self, place, slices, w_self, bias):
        def body(place, own, far, core, both, w_self, bias, out, held):
            for index, piece in zip(self.feats_of(place), (own, far, core, both)):
                held[pl.ds(pl.multiple_of(index * self.slices, self.slices), self.slices), :] = piece[...]
            column = jnp.broadcast_to(bias[...], (TB, self.width)).T
            value = self.times_weight(w_self[...].T, *split(held[...]))
            out[0] = value + jnp.concatenate([column] * self.per_piece, 1)

        columns = pl.BlockSpec((self.slices, self.piece), lambda k, part, *_: (0, part * CHUNKS + k))
        return self.call(
            body, (place,), (CHUNKS, self.parts),
            [columns] * 4 + [self.full(self.width, self.width), self.full(1, self.width)], (*slices, w_self, bias),
            pl.BlockSpec((1, self.width, self.piece), lambda k, part, *_: (k, 0, part)),
            jax.ShapeDtypeStruct((CHUNKS, self.width, self.span), F32),
            scratch=[pltpu.VMEM((self.width, self.piece), F32)],
        )

    def activate(self, k, place, means, w_neigh, self_part, cotangents, inverse, activated):
        rows = pl.BlockSpec((self.piece, self.width), lambda *_: (k, 0))

        def body(place, m0, m1, m2, m3, weight, self_part, c0, c1, c2, c3, inverse, *rest):
            out, grad, back, high, low = rest[-5:]
            feats = self.feats_of(place)
            for index, piece in zip(feats, (m0, m1, m2, m3)):
                at = pl.ds(pl.multiple_of(index * self.slices, self.slices), self.slices)
                for spot in range(self.per_chunk):
                    columns = slice(spot * TB, (spot + 1) * TB)
                    high[at, columns], low[at, columns] = split(piece[spot])
            weight_t = weight[...].T
            own_rows = weight[pl.ds(pl.multiple_of(feats[0] * self.slices, self.slices), self.slices), :]
            for part, cotangent in zip(feats, (c0, c1, c2, c3)):
                at = pl.ds(pl.multiple_of(part * self.piece, self.piece), self.piece)
                pre = self.times_weight(weight_t, high[:, at], low[:, at]) + self_part[0, :, at]
                sigma = jax.nn.sigmoid(pre)
                if cotangent is c0:
                    out[...] = (pre * sigma).T
                slope = cotangent[...] * (sigma * (1.0 + pre * (1.0 - sigma)))
                grad[:, at] = slope
                value = self.times_weight(own_rows, *split(slope))
                for j in range(self.per_piece):
                    scale = inverse[pl.ds(self.block(k, part, j), 1), :]
                    back[part * self.per_piece + j] = value[:, j * TB : (j + 1) * TB] * scale

        in_specs = (
            [self.dense_spec()] * 4
            + [self.full(self.width, self.width)]
            + [pl.BlockSpec((1, self.width, self.span), lambda *_: (k, 0, 0))]
            + [pl.BlockSpec((self.width, self.piece), lambda *_: (0, k))] * 4
            + [self.full(self.blocks, TB)]
        )
        args = [*means, w_neigh, self_part, *cotangents, inverse]
        aliases = {}
        if activated is not None:
            aliases = {1 + len(args): 0}
            in_specs.append(pl.BlockSpec(memory_space=pl.ANY))
            args.append(activated)
        return self.call(
            body, (place,), (1,), in_specs, args,
            [rows, self.full(self.width, self.span), self.dense_spec()],
            [jax.ShapeDtypeStruct((self.per_part * TB, self.width), F32),
             jax.ShapeDtypeStruct((self.width, self.span), F32), self.dense()],
            scratch=[pltpu.VMEM((self.width, self.span), BF16)] * 2, aliases=aliases,
        )

    def weight_grad(self, k, place, w_self, feats, means, grad, before):
        shape = (2 * self.slices + 16, self.width)

        def body(place, w_self, feats, means, grad, *rest):
            self_out, weights_out = rest[-2:]
            total = rest[0][...] if before is not None else jnp.zeros(shape, F32)
            for part in range(self.parts):
                first = part * self.per_piece
                at = slice(part * self.piece, (part + 1) * self.piece)
                high, low = split(grad[:, at])
                value = self.times_weight(w_self[...], high, low)
                for j in range(self.per_piece):
                    self_out[first + j] = value[:, j * TB : (j + 1) * TB]
                start = self.block(k, part, 0) * TB
                rows = jnp.concatenate(
                    [
                        feats[:, start : start + self.piece],
                        jnp.concatenate([means[first + j] for j in range(self.per_piece)], 1),
                        jnp.ones((16, self.piece), F32),
                    ],
                    0,
                )
                rows_high, rows_low = split(rows)
                total += (dot_nt(rows_high, high) + dot_nt(rows_low, high)) + dot_nt(rows_high, low)
            weights_out[...] = total

        weight_rows = pl.BlockSpec((self.slices, self.width), lambda i, place, *_: (2 * place[2] + place[3], 0))
        args = [w_self, feats, means, grad] + ([] if before is None else [before])
        return self.call(
            body, (place,), (1,),
            [weight_rows, self.full(self.slices, self.owned), self.dense_spec(), self.full(self.width, self.span)]
            + [self.full(*shape)] * (before is not None),
            args, [self.dense_spec(), self.full(*shape)], [self.dense(), jax.ShapeDtypeStruct(shape, F32)],
        )

    def both_cores(self, place, mine, other):
        def body(place, mine, other, out):
            out[place[3]] = mine[...]
            out[1 - place[3]] = other[...]

        shape = (2, *mine.shape)
        return self.call(
            body, (place,), (1,), [self.full(*mine.shape)] * 2, (mine, other), self.full(*shape),
            jax.ShapeDtypeStruct(shape, F32),
        )

    def whole_weights(self, place, mine, other):
        def body(place, mine, other, w_self, w_neigh, bias):
            for y, block in ((place[2], mine), (1 - place[2], other)):
                for core in range(2):
                    at = pl.ds(pl.multiple_of((2 * y + core) * self.slices, self.slices), self.slices)
                    w_self[at, :] = block[core, : self.slices, :]
                    w_neigh[at, :] = block[core, self.slices : 2 * self.slices, :]
            bias[...] = mine[0, 2 * self.slices : 2 * self.slices + 1, :]

        square, row = (self.width, self.width), (1, self.width)
        return self.call(
            body, (place,), (1,), [self.full(*mine.shape)] * 2, (mine, other),
            [self.full(*square), self.full(*square), self.full(*row)],
            [jax.ShapeDtypeStruct(shape, F32) for shape in (square, square, row)],
        )

    def gather(self, place, sources, held):
        inner = inner_place(place)
        for k in range(CHUNKS):
            spots = slice(k * self.per_chunk, (k + 1) * self.per_chunk)
            if len(sources) == CHUNKS:
                held[spots] = sources[k][...]
            else:

                @pl.when(jnp.logical_not(inner))
                def _():
                    held[spots] = sources[CHUNKS + k][...]

                @pl.when(inner)
                def _():
                    held[spots] = sources[k][...]

    def held(self):
        return pltpu.VMEM((self.blocks, self.slices, TB), F32)

    def pick(self, row, held):
        chunk, spot = self.spot(row)
        return jnp.where(row >= 0, held[chunk * self.per_chunk + spot], 0.0)

    def picked(self, role, place, rows, sources):
        def body(place, rows, *rest):
            out, held = rest[-2:]
            self.gather(place, rest[:-2], held)
            row_of = self.row_index(role, place[0], 1 - place[1])
            for c in range(self.cap):
                out[c] = self.pick(rows[row_of, c], held)

        return self.call(
            body, (place, rows), (1,), [self.dense_spec()] * len(sources), sources,
            self.slots_spec(), self.slots(), scratch=[self.held()],
        )

    def spread(self, place, cols, rows, tiles, jobs, total=None, self_back=None):
        counts = [len(sources) for _, sources in jobs]
        extra = [total] if self_back is None else list(self_back)

        def body(place, cols, rows, tiles, *rest):
            arrays, more = rest[: sum(counts)], rest[sum(counts) : sum(counts) + len(extra)]
            out, done, held, buffer, sems = rest[sum(counts) + len(extra) :]
            done[...] = jnp.zeros_like(done)
            z, x = place[0], place[1]
            owners = [owner(role, z) * 2 + (1 - x if n == 1 else x) for (role, _), n in zip(jobs, counts)]
            copies = [self.fetch(tiles, buffer, sems, owned_by, i) for i, owned_by in enumerate(owners)]
            for copy in copies:
                copy.start()
            if self_back is None:
                out[...] = more[0][...]
            else:
                for k, back in enumerate(more):
                    for part in range(self.parts):
                        for j in range(self.per_piece):
                            block = self.block(k, part, j)
                            out[:, block * TB : (block + 1) * TB] = back[part * self.per_piece + j]
            for i, (role, _) in enumerate(jobs):
                sources = arrays[sum(counts[:i]) : sum(counts[: i + 1])]
                if counts[i] > 1:
                    self.gather(place, sources, held)
                copies[i].wait()
                for c in range(self.cap):
                    if counts[i] > 1:
                        value = self.pick(rows[self.row_index(role, z, x), c], held)
                    else:
                        value = sources[0][c]
                    out[:, lanes(cols[owners[i], c])] += times_tile(value, buffer[i, c])

        whole = self.full(self.slices, self.owned)
        in_specs, args = [self.tiles_spec()], [tiles]
        for _, sources in jobs:
            in_specs += [self.slots_spec() if len(sources) == 1 else self.dense_spec()] * len(sources)
            args += sources
        in_specs += [whole] if self_back is None else [self.dense_spec()] * CHUNKS
        args += extra
        return self.call(
            body, (place, cols, rows), (1,), in_specs, args, [whole, self.full(8, TB)],
            [jax.ShapeDtypeStruct((self.slices, self.owned), F32), jax.ShapeDtypeStruct((8, TB), F32)],
            scratch=[self.held(), *self.fetched(len(jobs))],
            aliases={3 + len(args) - 1: 0} if self_back is None else {},
        )[0]


def pairs_z(steps):
    return [(2 * a + x, 2 * b + x) for a, b in steps for x in range(2)]


ACROSS = pairs_z([(1, 2), (2, 1), (0, 0), (3, 3)])
OTHER_X = [(n, n ^ 1) for n in range(8)]
OTHER_CORE = [(f, f ^ 1) for f in range(4)]
OTHER_Y = [(f, f ^ 2) for f in range(4)]


def along_z(distance):
    return pairs_z([(z, z ^ distance) for z in range(4)])


def node_swap(value, pairs):
    return lax.ppermute(value, "node", pairs)


def feat_swap(value, pairs):
    return lax.ppermute(value, "feat", pairs)


ORDER = [
    ("slots_first",),
    ("table_out",),
    ("tables_out",),
    ("load",),
    ("slots_later",),
    ("rows_in",),
    ("dense", FAR_OUTER),
    ("slots", FAR_INNER),
    ("send_in", FAR_OUTER, 1),
    ("pass_on", FAR_OUTER, 0),
    ("dense", FAR_INNER),
    ("send_in", FAR_INNER, 1),
    ("slots", NEAR),
    ("pass_on", FAR_OUTER, 1),
    ("dense", NEAR),
    ("pass_on", FAR_INNER, 0),
    ("slots", SELF),
    ("pass_on", NEAR, 0),
    ("pass_on", NEAR, 1),
    ("pass_on", FAR_INNER, 1),
    ("feats_on",),
    ("dense", SELF),
    ("mean", 0),
    ("cotangents_on",),
    ("mean", 1),
    ("means_on", 0),
    ("self_part",),
    ("means_on", 1),
    ("activate", 0),
    ("activate", 1),
    ("weight", 0),
    ("inner_on", 0),
    ("weight", 1),
    ("pick", SELF),
    ("near_on", 0),
    ("inner_on", 1),
    ("near_on", 1),
    ("weight_sum", along_z(1)),
    ("wait", "inner", 0, 1),
    ("wait", "outer", 0, 0),
    ("pick", NEAR),
    ("outer_on", 0),
    ("weight_sum", along_z(3)),
    ("pick", FAR_INNER),
    ("wait", "returned", SELF),
    ("outer_on", 1),
    ("spread", SELF, None),
    ("spread", NEAR, SELF),
    ("wait", "outer", 0, 1),
    ("spread", FAR_INNER, NEAR),
    ("weight_sum", None),
    ("wait", "returned", FAR_INNER),
    ("pick", FAR_OUTER),
    ("weight_cores",),
    ("spread", FAR_OUTER, FAR_INNER),
    ("weight_whole",),
    ("spread", None, FAR_OUTER),
]


class Steps:
    def __init__(self, layer, place, node_feats, tiles, send_col, recv_row, inverse, w_self, w_neigh, bias, cotangent):
        self.layer, self.place, self.feats, self.tiles = layer, place, node_feats, tiles
        self.cols, self.table, self.inverse = send_col, recv_row, inverse
        self.w_self, self.w_neigh, self.bias, self.cotangent = w_self, w_neigh, bias, cotangent
        self.slots_in, self.joined, self.inward, self.returned = {}, {}, {}, {}
        self.across, self.nearby, self.means, self.mean_parts = {}, {}, {}, {}
        self.grads, self.own, self.near, self.inner, self.outer = {}, {}, {}, {}, {}
        self.self_back, self.activated, self.weights, self.total = {}, None, None, None

    def wait(self, name, *key):
        held = getattr(self, name)
        for index in key:
            held = held[index]
        self.layer.pending.append(held)

    def slots_first(self):
        part = self.layer.first_slots(FAR_OUTER, self.place, self.cols, self.feats, self.tiles)
        self.slots_in[FAR_OUTER] = node_swap(part, OTHER_X)

    def slots_later(self):
        self.parts = self.layer.later_slots((FAR_INNER, NEAR, SELF), self.place, self.cols, self.feats, self.tiles)

    def slots(self, role):
        part = self.layer.relay(self.parts[role - 1], after=[self.slots_in[role - 1]])
        self.slots_in[role] = node_swap(part, OTHER_X)

    def table_out(self):
        self.table = self.layer.copied(self.table)
        self.table_in = node_swap(self.table, along_z(1))

    def tables_out(self):
        self.tables = self.layer.stacked_tables(self.table, self.table_in)
        self.tables_in = node_swap(self.tables, along_z(2))

    def rows_in(self):
        self.rows = self.layer.own_rows(self.place, self.tables, self.tables_in)

    def load(self):
        feats, self.tiles, cotangent = self.layer.loaded(self.feats, self.tiles, self.cotangent)
        self.feats = feats
        self.feat_parts = [feats, feat_swap(feats, OTHER_Y), feat_swap(feats, OTHER_CORE)]
        self.cotangents = [cotangent, feat_swap(cotangent, OTHER_Y), feat_swap(cotangent, OTHER_CORE)]

    def on(self, parts):
        parts[1] = self.layer.relay(parts[1])
        parts.append(feat_swap(parts[1], OTHER_CORE))

    def feats_on(self):
        self.on(self.feat_parts)

    def cotangents_on(self):
        self.on(self.cotangents)

    def self_part(self):
        self.self_parts = self.layer.self_part(self.place, self.feat_parts, self.w_self, self.bias)

    def dense(self, role):
        sums = self.layer.dense_sums(
            role, self.place, self.cols, self.rows, self.feats, self.tiles, self.slots_in[role]
        )
        for k in range(CHUNKS):
            self.joined[role, k] = sums[k]
        if role in (FAR_OUTER, FAR_INNER):
            self.inward[role, 0] = node_swap(sums[0], along_z(1))

    def send_in(self, role, k):
        self.joined[role, k] = self.layer.relay(self.joined[role, k])
        self.inward[role, k] = node_swap(self.joined[role, k], along_z(1))

    def pass_on(self, role, k):
        if role == NEAR:
            part = self.layer.added_across(self.place, self.joined[NEAR, k], self.across[FAR_OUTER, k])
            self.nearby[k] = node_swap(part, along_z(1))
        else:
            part = self.layer.added(self.joined[role, k], self.inward[role, k])
            self.across[role, k] = node_swap(part, ACROSS)

    def mean(self, k):
        pieces = (self.joined[SELF, k], self.nearby[k], self.across[FAR_INNER, k])
        means = self.layer.means(k, self.place, pieces, self.inverse)
        self.means[k] = means
        self.mean_parts[k] = [means, feat_swap(means, OTHER_Y), feat_swap(means, OTHER_CORE)]

    def means_on(self, k):
        self.on(self.mean_parts[k])

    def activate(self, k):
        self.activated, self.grads[k], back = self.layer.activate(
            k, self.place, self.mean_parts[k], self.w_neigh, self.self_parts, self.cotangents, self.inverse, self.activated
        )
        self.own[k] = back
        self.near[k] = node_swap(back, along_z(1))
        self.inner[k] = [node_swap(back, ACROSS)]

    def near_on(self, k):
        self.near[k] = self.layer.relay(self.near[k])
        self.outer[k] = [node_swap(self.near[k], ACROSS)]

    def inner_on(self, k):
        self.inner[k][0] = self.layer.relay(self.inner[k][0])
        self.inner[k].append(node_swap(self.inner[k][0], along_z(1)))

    def outer_on(self, k):
        self.outer[k][0] = self.layer.relay(self.outer[k][0])
        self.outer[k].append(node_swap(self.outer[k][0], along_z(1)))

    def weight(self, k):
        back, weights = self.layer.weight_grad(
            k, self.place, self.w_self, self.feats, self.means[k], self.grads[k], self.weights
        )
        self.self_back[k] = back
        self.weights = weights
        if k == CHUNKS - 1:
            self.weights_in = node_swap(weights, OTHER_X)

    def weight_sum(self, pairs):
        self.weights = self.layer.added(self.weights, self.weights_in)
        if pairs is None:
            self.weights_in = feat_swap(self.weights, OTHER_CORE)
        else:
            self.weights_in = node_swap(self.weights, pairs)

    def weight_cores(self):
        self.weights = self.layer.both_cores(self.place, self.weights, self.weights_in)
        self.weights_in = feat_swap(self.weights, OTHER_Y)

    def weight_whole(self):
        self.weights = self.layer.whole_weights(self.place, self.weights, self.weights_in)

    def sources(self, role):
        if role in (SELF, NEAR):
            return [(self.own if role == SELF else self.near)[k] for k in range(CHUNKS)]
        held = self.inner if role == FAR_INNER else self.outer
        return [held[k][0] for k in range(CHUNKS)] + [held[k][1] for k in range(CHUNKS)]

    def pick(self, role):
        self.returned[role] = node_swap(self.layer.picked(role, self.place, self.rows, self.sources(role)), OTHER_X)

    def spread(self, local, slots):
        jobs = [] if local is None else [(local, self.sources(local))]
        jobs += [] if slots is None else [(slots, [self.returned[slots]])]
        first = self.total is None
        back = [self.self_back[k] for k in range(CHUNKS)] if first else None
        self.total = self.layer.spread(self.place, self.cols, self.rows, self.tiles, jobs, self.total, back)


def chain_shards(node_feats, tiles, send_col, recv_row, degree, w_self, w_neigh, bias, cotangent):
    slices, owned = node_feats.shape
    width = w_self.shape[1]
    layer = Layer(slices, owned, tiles.shape[1], 4, width)
    node, feat = lax.axis_index("node"), lax.axis_index("feat")
    place = jnp.stack([node // 2, node % 2, feat // 2, feat % 2]).astype(jnp.int32)
    inverse = (1.0 / degree.astype(F32)).reshape(-1, TB)
    steps = Steps(
        layer, place, node_feats, tiles, send_col, recv_row, inverse, w_self, w_neigh, bias.reshape(1, width), cotangent
    )
    for name, *arguments in ORDER:
        getattr(steps, name)(*arguments)
    grad_self, grad_neigh, grad_bias = steps.weights
    return (steps.activated, steps.total, grad_self, grad_neigh, grad_bias.reshape(width))


def slot_shards(node_feats, tiles, send_col, recv_row, degree, w_self, w_neigh, bias, cotangent):
    slices, owned = node_feats.shape
    blocks = owned // TB
    block_ids = jnp.arange(blocks, dtype=jnp.int32)
    scale = degree.astype(F32)[None, :]
    col_onehot = (send_col[..., None] == block_ids).astype(F32)
    row_onehot = (recv_row[..., None] == block_ids).astype(F32)
    feat_blocks = node_feats.reshape(slices, blocks, TB)
    picked = jnp.einsum("dcb,fbj->dcfj", col_onehot, feat_blocks, precision=HIGH)
    partial_value = jnp.einsum("dcfj,dcij->dcfi", picked, tiles, precision=HIGH)
    arrived = lax.all_to_all(partial_value, "node", split_axis=0, concat_axis=0, tiled=True)
    summed = jnp.einsum("scfi,scb->fbi", arrived, row_onehot, precision=HIGH)
    neighbour = summed.reshape(slices, owned) / scale
    offset = lax.axis_index("feat") * slices
    self_rows = lax.dynamic_slice_in_dim(w_self, offset, slices, 0)
    neigh_rows = lax.dynamic_slice_in_dim(w_neigh, offset, slices, 0)
    dims = (((0,), (0,)), ((), ()))
    first = lax.dot_general(node_feats, self_rows, dims, precision=HIGH)
    second = lax.dot_general(neighbour, neigh_rows, dims, precision=HIGH)
    pre = lax.psum_scatter(first + second, "feat", scatter_dimension=0, tiled=True) + bias
    sigma = jax.nn.sigmoid(pre)
    activated = pre * sigma
    gpre = cotangent * sigma * (1.0 + pre * (1.0 - sigma))
    piece = lax.all_gather(gpre, "feat", axis=0, tiled=True)
    dims = (((1,), (1,)), ((), ()))
    self_back = lax.dot_general(self_rows, piece, dims, precision=HIGH)
    neigh_back = lax.dot_general(neigh_rows, piece, dims, precision=HIGH)
    slice_self = jnp.dot(node_feats, piece, precision=HIGH)
    slice_neigh = jnp.dot(neighbour, piece, precision=HIGH)
    sums = lax.psum((slice_self, slice_neigh, jnp.sum(piece, axis=0)), "node")
    grad_self, grad_neigh = (lax.all_gather(part, "feat", axis=0, tiled=True) for part in sums[:2])
    gneigh = (neigh_back / scale).reshape(slices, blocks, TB)
    outgoing = jnp.einsum("scb,fbi->scfi", row_onehot, gneigh, precision=HIGH)
    returned = lax.all_to_all(outgoing, "node", split_axis=0, concat_axis=0, tiled=True)
    spread = jnp.einsum("dcfi,dcij->dcfj", returned, tiles, precision=HIGH)
    placed = jnp.einsum("dcfj,dcb->fbj", spread, col_onehot, precision=HIGH)
    grad_feats = self_back + placed.reshape(slices, owned)
    return (activated, grad_feats, grad_self, grad_neigh, sums[2])


def solution(mesh):
    chain = mesh.shape["node"] == 8 and mesh.shape["feat"] == 4
    return jax.shard_map(
        chain_shards if chain else slot_shards,
        mesh=mesh,
        in_specs=(
            P("feat", "node"),
            P("node", None, None, None),
            P("node", None),
            P("node", None),
            P("node"),
            P(),
            P(),
            P(),
            P(("node", "feat"), None),
        ),
        out_specs=(P(("node", "feat"), None), P("feat", "node"), P(), P(), P()),
        check_vma=False,
    )
```

```python
import jax
import jax.numpy as jnp
from jax import lax
from jax.experimental import pallas as pl
from jax.experimental.pallas import tpu as pltpu
from jax.sharding import PartitionSpec as P

TB = 128
F32 = jnp.float32
BF16 = jnp.bfloat16
HIGH = lax.Precision.HIGH
CHUNKS = 2
VMEM_BYTES = 28 * 2**20
FIRST_VMEM_BYTES = 57 * 2**20

FAR_OUTER, FAR_INNER, NEAR, SELF = range(4)


def owner(role, z):
    if role == FAR_OUTER:
        return jnp.where(z < 2, 3, 0)
    if role == FAR_INNER:
        return jnp.where(z < 2, 2, 1)
    if role == NEAR:
        return z + 1 - 2 * (z % 2)
    return z


def inner_place(place):
    return (place[0] == 1) | (place[0] == 2)


def split(value):
    high = value.astype(BF16)
    return high, (value - high.astype(F32)).astype(BF16)


def dot_nn(a, b):
    return lax.dot_general(a, b, (((1,), (0,)), ((), ())), preferred_element_type=F32)


def dot_nt(a, b):
    return lax.dot_general(a, b, (((1,), (1,)), ((), ())), preferred_element_type=F32)


def stacked(value):
    high, low = split(value)
    return jnp.concatenate(
        [jnp.concatenate([high, high], 1), jnp.concatenate([low, jnp.zeros_like(low)], 1)], 0
    )


def times_tile_t(value, tile):
    rows = value.shape[0]
    out = dot_nt(stacked(value), jnp.concatenate(split(tile), 1))
    return out[:rows] + out[rows:]


def times_tile(value, tile):
    rows = value.shape[0]
    out = dot_nn(stacked(value), jnp.concatenate(split(tile), 0))
    return out[:rows] + out[rows:]


def lanes(block):
    return pl.ds(pl.multiple_of(block * TB, TB), TB)


class Layer:
    def __init__(self, slices, owned, cap, parts, width):
        self.slices, self.owned, self.cap, self.parts, self.width = slices, owned, cap, parts, width
        self.blocks = owned // TB
        self.per_part = self.blocks // parts
        self.per_piece = self.per_part // CHUNKS
        self.per_chunk = self.blocks // CHUNKS
        self.piece = self.per_piece * TB
        self.span = self.per_chunk * TB
        self.token = None
        self.pending = []

    def spot(self, row):
        row = jnp.maximum(row, 0)
        part, inside = row // self.per_part, row % self.per_part
        return inside // self.per_piece, part * self.per_piece + inside % self.per_piece

    def block(self, chunk, part, inside):
        return part * self.per_part + chunk * self.per_piece + inside

    def full(self, *shape):
        return pl.BlockSpec(shape, lambda *_: (0,) * len(shape))

    def dense_spec(self):
        return self.full(self.per_chunk, self.slices, TB)

    def slots_spec(self):
        return self.full(self.cap, self.slices, TB)

    def slots(self):
        return jax.ShapeDtypeStruct((self.cap, self.slices, TB), F32)

    def dense(self):
        return jax.ShapeDtypeStruct((self.per_chunk, self.slices, TB), F32)

    def call(self, body, scalars, grid, in_specs, args, out_specs, out_shape, scratch=(), aliases=None, after=(), vmem=VMEM_BYTES):
        given = len(scalars) + len(args)
        waits = list(after) + self.pending + ([] if self.token is None else [self.token])
        self.pending = []

        def ordered(*refs):
            body(*refs[:given], *refs[given + len(waits) :])

        out = pl.pallas_call(
            ordered,
            grid_spec=pltpu.PrefetchScalarGridSpec(
                num_scalar_prefetch=len(scalars),
                grid=grid,
                in_specs=list(in_specs) + [pl.BlockSpec(memory_space=pl.ANY)] * len(waits),
                out_specs=out_specs,
                scratch_shapes=scratch,
            ),
            out_shape=out_shape,
            input_output_aliases=aliases or {},
            compiler_params=pltpu.CompilerParams(vmem_limit_bytes=vmem),
            cost_estimate=pl.CostEstimate(flops=1, bytes_accessed=1, transcendentals=0),
        )(*scalars, *args, *waits)
        self.token = jax.tree.leaves(out)[-1]
        return out

    def relay(self, value, after=()):
        def body(value, out):
            pass

        anywhere = pl.BlockSpec(memory_space=pl.ANY)
        return self.call(
            body, (), (1,), [anywhere], (value,), anywhere, jax.ShapeDtypeStruct(value.shape, value.dtype),
            aliases={0: 0}, after=after,
        )

    def added(self, a, b):
        def body(a, b, out):
            out[...] = a[...] + b[...]

        spec = self.full(*a.shape)
        return self.call(body, (), (1,), [spec] * 2, (a, b), spec, jax.ShapeDtypeStruct(a.shape, F32))

    def added_across(self, place, a, across):
        def body(place, a, across, out):
            out[...] = a[...] + jnp.where(inner_place(place), across[...], 0.0)

        return self.call(body, (place,), (1,), [self.dense_spec()] * 2, (a, across), self.dense_spec(), self.dense())

    def fetched(self, count):
        return [pltpu.VMEM((count, self.cap, TB, TB), F32), pltpu.SemaphoreType.DMA((count,))]

    def fetch(self, tiles, buffer, sems, index, slot):
        return pltpu.make_async_copy(tiles.at[index], buffer.at[slot], sems.at[slot])

    def tiles_spec(self):
        return pl.BlockSpec(memory_space=pl.ANY)

    def first_slots(self, role, place, cols, feats, tiles):
        groups = 4
        per_group = self.cap // groups

        def body(place, cols, feats, tiles, out, done, held, buffer, sems):
            done[...] = jnp.zeros_like(done)
            owned_by = owner(role, place[0]) * 2 + 1 - place[1]
            copies = [pltpu.make_async_copy(feats, held, sems.at[groups])]
            for g in range(groups):
                some = pl.ds(g * per_group, per_group)
                copies.append(pltpu.make_async_copy(tiles.at[owned_by, some], buffer.at[some], sems.at[g]))
            for copy in copies:
                copy.start()
            for g in range(groups):
                if g == 0:
                    copies[0].wait()
                copies[1 + g].wait()
                for c in range(g * per_group, (g + 1) * per_group):
                    out[c] = times_tile_t(held[:, lanes(cols[owned_by, c])], buffer[c])

        return self.call(
            body, (place, cols), (1,), [self.tiles_spec()] * 2, (feats, tiles), [self.slots_spec(), self.full(8, TB)],
            [self.slots(), jax.ShapeDtypeStruct((8, TB), F32)],
            scratch=[
                pltpu.VMEM((self.slices, self.owned), F32),
                pltpu.VMEM((self.cap, TB, TB), F32),
                pltpu.SemaphoreType.DMA((groups + 1,)),
            ],
            vmem=FIRST_VMEM_BYTES,
        )[0]

    def later_slots(self, roles, place, cols, feats, tiles):
        def body(place, cols, feats, tiles, *rest):
            outs, (buffer, sems) = rest[: len(roles)], rest[len(roles) :]
            owners = [owner(role, place[0]) * 2 + 1 - place[1] for role in roles]
            copies = [self.fetch(tiles, buffer, sems, owned_by, i) for i, owned_by in enumerate(owners)]
            for copy in copies:
                copy.start()
            for i, owned_by in enumerate(owners):
                copies[i].wait()
                for c in range(self.cap):
                    outs[i][c] = times_tile_t(feats[:, lanes(cols[owned_by, c])], buffer[i, c])

        return self.call(
            body, (place, cols), (1,), [self.full(self.slices, self.owned), self.tiles_spec()], (feats, tiles),
            [self.slots_spec()] * len(roles), [self.slots()] * len(roles), scratch=self.fetched(len(roles)),
        )

    def dense_sums(self, role, place, cols, rows, feats, tiles, slots):
        def body(place, cols, rows, feats, tiles, slots, *rest):
            outs, (buffer, sems) = rest[:CHUNKS], rest[CHUNKS:]
            z, x = place[0], place[1]
            owned_by = owner(role, z) * 2 + x
            copy = self.fetch(tiles, buffer, sems, owned_by, 0)
            copy.start()
            for out in outs:
                out[...] = jnp.zeros_like(out)

            def add(row, value):
                chunk, spot = self.spot(row)
                for k, out in enumerate(outs):
                    out[spot] += jnp.where((row >= 0) & (chunk == k), value, 0.0)

            for c in range(self.cap):
                add(rows[self.row_index(role, z, 1 - x), c], slots[c])
            copy.wait()
            for c in range(self.cap):
                value = times_tile_t(feats[:, lanes(cols[owned_by, c])], buffer[0, c])
                add(rows[self.row_index(role, z, x), c], value)

        return self.call(
            body, (place, cols, rows), (1,),
            [self.full(self.slices, self.owned), self.tiles_spec(), self.slots_spec()], (feats, tiles, slots),
            [self.dense_spec()] * CHUNKS, [self.dense()] * CHUNKS, scratch=self.fetched(1),
        )

    def stacked_tables(self, first, second):
        def body(first, second, out):
            out[: first.shape[0], :] = first[...]
            out[first.shape[0] :, :] = second[...]

        shape = (2 * first.shape[0], first.shape[1])
        return self.call(
            body, (), (1,), [self.full(*first.shape)] * 2, (first, second), self.full(*shape),
            jax.ShapeDtypeStruct(shape, first.dtype),
        )

    def own_rows(self, place, pair, other_pair):
        half = pair.shape[0] // 2

        def body(place, pair, other, out):
            for distance in range(4):
                table = (pair, other)[distance // 2]
                start = half * (distance % 2) + 2 * place[0]
                out[2 * distance : 2 * distance + 2, :] = table[pl.ds(start, 2), :]

        shape = (half, pair.shape[1])
        return self.call(
            body, (place,), (1,), [self.full(*pair.shape)] * 2, (pair, other_pair), self.full(*shape),
            jax.ShapeDtypeStruct(shape, pair.dtype),
        )

    def row_index(self, role, z, sender_x):
        return (owner(role, z) ^ z) * 2 + sender_x

    def means(self, k, place, pieces, inverse):
        def body(place, own, near, across, inverse, out):
            for part in range(self.parts):
                for j in range(self.per_piece):
                    spot, block = part * self.per_piece + j, self.block(k, part, j)
                    total = own[spot] + near[spot] + jnp.where(inner_place(place), across[spot], 0.0)
                    out[spot] = total * inverse[block : block + 1, :]

        return self.call(
            body, (place,), (1,), [self.dense_spec()] * 3 + [self.full(self.blocks, TB)], (*pieces, inverse),
            self.dense_spec(), self.dense(),
        )

    def loaded(self, feats, tiles, cotangent):
        def body(feats, tiles, cotangent, feats_out, tiles_out, cotangent_out, sems):
            copies = [
                pltpu.make_async_copy(feats, feats_out, sems.at[0]),
                pltpu.make_async_copy(tiles, tiles_out, sems.at[1]),
            ]
            for copy in copies:
                copy.start()
            cotangent_out[...] = cotangent[...].T
            for copy in copies:
                copy.wait()

        rows, cols = cotangent.shape
        anywhere = pl.BlockSpec(memory_space=pl.ANY)
        return self.call(
            body, (), (1,), [anywhere, anywhere, self.full(rows, cols)], (feats, tiles, cotangent),
            [anywhere, anywhere, self.full(cols, rows)],
            [pltpu.VMEM(feats.shape, F32), pltpu.VMEM(tiles.shape, F32), jax.ShapeDtypeStruct((cols, rows), F32)],
            scratch=[pltpu.SemaphoreType.DMA((2,))],
        )

    def copied(self, table):
        def body(table, out):
            out[...] = table[...]

        spec = self.full(*table.shape)
        return self.call(body, (), (1,), [spec], (table,), spec, jax.ShapeDtypeStruct(table.shape, table.dtype))

    def feats_of(self, place):
        y, core = place[2], place[3]
        return (2 * y + core, 2 * (1 - y) + core, 2 * y + 1 - core, 2 * (1 - y) + 1 - core)

    def times_weight(self, weight_t, high, low):
        rows = weight_t.shape[0]
        weight_high, weight_low = split(weight_t)
        out = dot_nn(jnp.concatenate([weight_high, weight_low], 0), high)
        return out[:rows] + out[rows:] + dot_nn(weight_high, low)

    def self_part(self, place, slices, w_self, bias):
        def body(place, own, far, core, both, w_self, bias, out, held):
            for index, piece in zip(self.feats_of(place), (own, far, core, both)):
                held[pl.ds(pl.multiple_of(index * self.slices, self.slices), self.slices), :] = piece[...]
            column = jnp.broadcast_to(bias[...], (TB, self.width)).T
            value = self.times_weight(w_self[...].T, *split(held[...]))
            out[0] = value + jnp.concatenate([column] * self.per_piece, 1)

        columns = pl.BlockSpec((self.slices, self.piece), lambda k, part, *_: (0, part * CHUNKS + k))
        return self.call(
            body, (place,), (CHUNKS, self.parts),
            [columns] * 4 + [self.full(self.width, self.width), self.full(1, self.width)], (*slices, w_self, bias),
            pl.BlockSpec((1, self.width, self.piece), lambda k, part, *_: (k, 0, part)),
            jax.ShapeDtypeStruct((CHUNKS, self.width, self.span), F32),
            scratch=[pltpu.VMEM((self.width, self.piece), F32)],
        )

    def activate(self, k, place, means, w_neigh, self_part, cotangents, inverse, activated):
        rows = pl.BlockSpec((self.piece, self.width), lambda *_: (k, 0))

        def body(place, m0, m1, m2, m3, weight, self_part, c0, c1, c2, c3, inverse, *rest):
            out, grad, back, high, low = rest[-5:]
            feats = self.feats_of(place)
            for index, piece in zip(feats, (m0, m1, m2, m3)):
                at = pl.ds(pl.multiple_of(index * self.slices, self.slices), self.slices)
                for spot in range(self.per_chunk):
                    columns = slice(spot * TB, (spot + 1) * TB)
                    high[at, columns], low[at, columns] = split(piece[spot])
            weight_t = weight[...].T
            own_rows = weight[pl.ds(pl.multiple_of(feats[0] * self.slices, self.slices), self.slices), :]
            for part, cotangent in zip(feats, (c0, c1, c2, c3)):
                at = pl.ds(pl.multiple_of(part * self.piece, self.piece), self.piece)
                pre = self.times_weight(weight_t, high[:, at], low[:, at]) + self_part[0, :, at]
                sigma = jax.nn.sigmoid(pre)
                if cotangent is c0:
                    out[...] = (pre * sigma).T
                slope = cotangent[...] * (sigma * (1.0 + pre * (1.0 - sigma)))
                grad[:, at] = slope
                value = self.times_weight(own_rows, *split(slope))
                for j in range(self.per_piece):
                    scale = inverse[pl.ds(self.block(k, part, j), 1), :]
                    back[part * self.per_piece + j] = value[:, j * TB : (j + 1) * TB] * scale

        in_specs = (
            [self.dense_spec()] * 4
            + [self.full(self.width, self.width)]
            + [pl.BlockSpec((1, self.width, self.span), lambda *_: (k, 0, 0))]
            + [pl.BlockSpec((self.width, self.piece), lambda *_: (0, k))] * 4
            + [self.full(self.blocks, TB)]
        )
        args = [*means, w_neigh, self_part, *cotangents, inverse]
        aliases = {}
        if activated is not None:
            aliases = {1 + len(args): 0}
            in_specs.append(pl.BlockSpec(memory_space=pl.ANY))
            args.append(activated)
        return self.call(
            body, (place,), (1,), in_specs, args,
            [rows, self.full(self.width, self.span), self.dense_spec()],
            [jax.ShapeDtypeStruct((self.per_part * TB, self.width), F32),
             jax.ShapeDtypeStruct((self.width, self.span), F32), self.dense()],
            scratch=[pltpu.VMEM((self.width, self.span), BF16)] * 2, aliases=aliases,
        )

    def weight_grad(self, k, place, w_self, feats, means, grad, before):
        shape = (2 * self.slices + 16, self.width)

        def body(place, w_self, feats, means, grad, *rest):
            self_out, weights_out = rest[-2:]
            total = rest[0][...] if before is not None else jnp.zeros(shape, F32)
            for part in range(self.parts):
                first = part * self.per_piece
                at = slice(part * self.piece, (part + 1) * self.piece)
                high, low = split(grad[:, at])
                value = self.times_weight(w_self[...], high, low)
                for j in range(self.per_piece):
                    self_out[first + j] = value[:, j * TB : (j + 1) * TB]
                start = self.block(k, part, 0) * TB
                rows = jnp.concatenate(
                    [
                        feats[:, start : start + self.piece],
                        jnp.concatenate([means[first + j] for j in range(self.per_piece)], 1),
                        jnp.ones((16, self.piece), F32),
                    ],
                    0,
                )
                rows_high, rows_low = split(rows)
                total += (dot_nt(rows_high, high) + dot_nt(rows_low, high)) + dot_nt(rows_high, low)
            weights_out[...] = total

        weight_rows = pl.BlockSpec((self.slices, self.width), lambda i, place, *_: (2 * place[2] + place[3], 0))
        args = [w_self, feats, means, grad] + ([] if before is None else [before])
        return self.call(
            body, (place,), (1,),
            [weight_rows, self.full(self.slices, self.owned), self.dense_spec(), self.full(self.width, self.span)]
            + [self.full(*shape)] * (before is not None),
            args, [self.dense_spec(), self.full(*shape)], [self.dense(), jax.ShapeDtypeStruct(shape, F32)],
        )

    def both_cores(self, place, mine, other):
        def body(place, mine, other, out):
            out[place[3]] = mine[...]
            out[1 - place[3]] = other[...]

        shape = (2, *mine.shape)
        return self.call(
            body, (place,), (1,), [self.full(*mine.shape)] * 2, (mine, other), self.full(*shape),
            jax.ShapeDtypeStruct(shape, F32),
        )

    def whole_weights(self, place, mine, other):
        def body(place, mine, other, w_self, w_neigh, bias):
            for y, block in ((place[2], mine), (1 - place[2], other)):
                for core in range(2):
                    at = pl.ds(pl.multiple_of((2 * y + core) * self.slices, self.slices), self.slices)
                    w_self[at, :] = block[core, : self.slices, :]
                    w_neigh[at, :] = block[core, self.slices : 2 * self.slices, :]
            bias[...] = mine[0, 2 * self.slices : 2 * self.slices + 1, :]

        square, row = (self.width, self.width), (1, self.width)
        return self.call(
            body, (place,), (1,), [self.full(*mine.shape)] * 2, (mine, other),
            [self.full(*square), self.full(*square), self.full(*row)],
            [jax.ShapeDtypeStruct(shape, F32) for shape in (square, square, row)],
        )

    def gather(self, place, sources, held):
        inner = inner_place(place)
        for k in range(CHUNKS):
            spots = slice(k * self.per_chunk, (k + 1) * self.per_chunk)
            if len(sources) == CHUNKS:
                held[spots] = sources[k][...]
            else:

                @pl.when(jnp.logical_not(inner))
                def _():
                    held[spots] = sources[CHUNKS + k][...]

                @pl.when(inner)
                def _():
                    held[spots] = sources[k][...]

    def held(self):
        return pltpu.VMEM((self.blocks, self.slices, TB), F32)

    def pick(self, row, held):
        chunk, spot = self.spot(row)
        return jnp.where(row >= 0, held[chunk * self.per_chunk + spot], 0.0)

    def picked(self, role, place, rows, sources):
        def body(place, rows, *rest):
            out, held = rest[-2:]
            self.gather(place, rest[:-2], held)
            row_of = self.row_index(role, place[0], 1 - place[1])
            for c in range(self.cap):
                out[c] = self.pick(rows[row_of, c], held)

        return self.call(
            body, (place, rows), (1,), [self.dense_spec()] * len(sources), sources,
            self.slots_spec(), self.slots(), scratch=[self.held()],
        )

    def spread(self, place, cols, rows, tiles, jobs, total=None, self_back=None, last=False):
        counts = [len(sources) for _, sources in jobs]
        extra = [total] if self_back is None else list(self_back)

        def body(place, cols, rows, tiles, *rest):
            arrays, more = rest[: sum(counts)], rest[sum(counts) : sum(counts) + len(extra)]
            out, done, held, buffer, sems = rest[sum(counts) + len(extra) :]
            done[...] = jnp.zeros_like(done)
            z, x = place[0], place[1]
            owners = [owner(role, z) * 2 + (1 - x if n == 1 else x) for (role, _), n in zip(jobs, counts)]
            copies = [self.fetch(tiles, buffer, sems, owned_by, i) for i, owned_by in enumerate(owners)]
            for copy in copies:
                copy.start()
            if self_back is None:
                out[...] = more[0][...]
            else:
                for k, back in enumerate(more):
                    for part in range(self.parts):
                        for j in range(self.per_piece):
                            block = self.block(k, part, j)
                            out[:, block * TB : (block + 1) * TB] = back[part * self.per_piece + j]
            for i, (role, _) in enumerate(jobs):
                sources = arrays[sum(counts[:i]) : sum(counts[: i + 1])]
                if counts[i] > 1:
                    self.gather(place, sources, held)
                copies[i].wait()
                for c in range(self.cap):
                    if counts[i] > 1:
                        value = self.pick(rows[self.row_index(role, z, x), c], held)
                    else:
                        value = sources[0][c]
                    out[:, lanes(cols[owners[i], c])] += times_tile(value, buffer[i, c])

        shape = (self.slices, self.owned)
        whole = self.full(*shape)
        in_specs, args = [self.tiles_spec()], [tiles]
        for _, sources in jobs:
            in_specs += [self.slots_spec() if len(sources) == 1 else self.dense_spec()] * len(sources)
            args += sources
        in_specs += [whole] if self_back is None else [self.dense_spec()] * CHUNKS
        args += extra
        return self.call(
            body, (place, cols, rows), (1,), in_specs, args, [whole, self.full(8, TB)],
            [
                jax.ShapeDtypeStruct(shape, F32) if last else pltpu.VMEM(shape, F32),
                jax.ShapeDtypeStruct((8, TB), F32),
            ],
            scratch=[self.held(), *self.fetched(len(jobs))],
            aliases={} if last or self_back is not None else {3 + len(args) - 1: 0},
        )[0]


def pairs_z(steps):
    return [(2 * a + x, 2 * b + x) for a, b in steps for x in range(2)]


ACROSS = pairs_z([(1, 2), (2, 1), (0, 0), (3, 3)])
OUTWARD = pairs_z([(1, 0), (2, 3)])
OTHER_X = [(n, n ^ 1) for n in range(8)]
OTHER_CORE = [(f, f ^ 1) for f in range(4)]
OTHER_Y = [(f, f ^ 2) for f in range(4)]


def along_z(distance):
    return pairs_z([(z, z ^ distance) for z in range(4)])


def node_swap(value, pairs):
    return lax.ppermute(value, "node", pairs)


def feat_swap(value, pairs):
    return lax.ppermute(value, "feat", pairs)


ORDER = [
    ("slots_first",),
    ("table_out",),
    ("load",),
    ("tables_out",),
    ("slots_later",),
    ("rows_in",),
    ("dense", FAR_OUTER),
    ("slots", FAR_INNER),
    ("send_in", FAR_OUTER, 1),
    ("pass_on", FAR_OUTER, 0),
    ("slots", NEAR),
    ("dense", FAR_INNER),
    ("pass_on", FAR_OUTER, 1),
    ("send_in", FAR_INNER, 1),
    ("dense", NEAR),
    ("feats_on",),
    ("pass_on", FAR_INNER, 0),
    ("pass_on", NEAR, 0),
    ("slots", SELF),
    ("pass_on", FAR_INNER, 1),
    ("pass_on", NEAR, 1),
    ("cotangents_on",),
    ("dense", SELF),
    ("mean", 0),
    ("wait", "nearby", 1),
    ("mean", 1),
    ("means_on", 0),
    ("self_part",),
    ("means_on", 1),
    ("activate", 0),
    ("activate", 1),
    ("pick", SELF),
    ("weight", 0),
    ("weight", 1),
    ("inner_on", 0),
    ("near_on", 0),
    ("inner_on", 1),
    ("weight_sum", along_z(1)),
    ("near_on", 1),
    ("wait", "inner", 0, 1),
    ("outer_on", 0),
    ("spread", SELF, None),
    ("pick", NEAR),
    ("spread", NEAR, SELF),
    ("weight_sum", along_z(3)),
    ("outer_on", 1),
    ("pick", FAR_INNER),
    ("wait", "returned", NEAR),
    ("wait", "weights_in"),
    ("wait", "outer", 0, 1),
    ("weight_sum", None),
    ("spread", FAR_INNER, NEAR),
    ("wait", "returned", FAR_INNER),
    ("pick", FAR_OUTER),
    ("weight_cores",),
    ("spread", FAR_OUTER, FAR_INNER),
    ("weight_whole",),
    ("spread", None, FAR_OUTER),
]


class Steps:
    def __init__(self, layer, place, node_feats, tiles, send_col, recv_row, inverse, w_self, w_neigh, bias, cotangent):
        self.layer, self.place, self.feats, self.tiles = layer, place, node_feats, tiles
        self.cols, self.table, self.inverse = send_col, recv_row, inverse
        self.w_self, self.w_neigh, self.bias, self.cotangent = w_self, w_neigh, bias, cotangent
        self.slots_in, self.joined, self.inward, self.returned = {}, {}, {}, {}
        self.across, self.nearby, self.means, self.mean_parts = {}, {}, {}, {}
        self.grads, self.own, self.near, self.inner, self.outer = {}, {}, {}, {}, {}
        self.self_back, self.activated, self.weights, self.total = {}, None, None, None

    def wait(self, name, *key):
        held = getattr(self, name)
        for index in key:
            held = held[index]
        self.layer.pending.append(held)

    def slots_first(self):
        part = self.layer.first_slots(FAR_OUTER, self.place, self.cols, self.feats, self.tiles)
        self.slots_in[FAR_OUTER] = node_swap(part, OTHER_X)

    def slots_later(self):
        self.parts = self.layer.later_slots((FAR_INNER, NEAR, SELF), self.place, self.cols, self.feats, self.tiles)

    def slots(self, role):
        part = self.layer.relay(self.parts[role - 1], after=[self.slots_in[role - 1]])
        self.slots_in[role] = node_swap(part, OTHER_X)

    def table_out(self):
        self.table = self.layer.copied(self.table)
        self.table_in = node_swap(self.table, along_z(1))

    def tables_out(self):
        self.tables = self.layer.stacked_tables(self.table, self.table_in)
        self.tables_in = node_swap(self.tables, along_z(2))

    def rows_in(self):
        self.rows = self.layer.own_rows(self.place, self.tables, self.tables_in)

    def load(self):
        feats, self.tiles, cotangent = self.layer.loaded(self.feats, self.tiles, self.cotangent)
        self.feats = feats
        self.feat_parts = [feats, feat_swap(feats, OTHER_Y), feat_swap(feats, OTHER_CORE)]
        self.cotangents = [cotangent, feat_swap(cotangent, OTHER_Y), feat_swap(cotangent, OTHER_CORE)]

    def on(self, parts):
        parts[1] = self.layer.relay(parts[1])
        parts.append(feat_swap(parts[1], OTHER_CORE))

    def feats_on(self):
        self.on(self.feat_parts)

    def cotangents_on(self):
        self.on(self.cotangents)

    def self_part(self):
        self.self_parts = self.layer.self_part(self.place, self.feat_parts, self.w_self, self.bias)

    def dense(self, role):
        sums = self.layer.dense_sums(
            role, self.place, self.cols, self.rows, self.feats, self.tiles, self.slots_in[role]
        )
        for k in range(CHUNKS):
            self.joined[role, k] = sums[k]
        if role in (FAR_OUTER, FAR_INNER):
            self.inward[role, 0] = node_swap(sums[0], along_z(1))

    def send_in(self, role, k):
        self.joined[role, k] = self.layer.relay(self.joined[role, k])
        self.inward[role, k] = node_swap(self.joined[role, k], along_z(1))

    def pass_on(self, role, k):
        if role == NEAR:
            part = self.layer.added_across(self.place, self.joined[NEAR, k], self.across[FAR_OUTER, k])
            self.nearby[k] = node_swap(part, along_z(1))
        else:
            part = self.layer.added(self.joined[role, k], self.inward[role, k])
            self.across[role, k] = node_swap(part, ACROSS)

    def mean(self, k):
        pieces = (self.joined[SELF, k], self.nearby[k], self.across[FAR_INNER, k])
        means = self.layer.means(k, self.place, pieces, self.inverse)
        self.means[k] = means
        self.mean_parts[k] = [means, feat_swap(means, OTHER_Y), feat_swap(means, OTHER_CORE)]

    def means_on(self, k):
        self.on(self.mean_parts[k])

    def activate(self, k):
        self.activated, self.grads[k], back = self.layer.activate(
            k, self.place, self.mean_parts[k], self.w_neigh, self.self_parts, self.cotangents, self.inverse, self.activated
        )
        self.own[k] = back
        self.near[k] = node_swap(back, along_z(1))
        self.inner[k] = [node_swap(back, ACROSS)]

    def near_on(self, k):
        self.near[k] = self.layer.relay(self.near[k])
        self.outer[k] = [node_swap(self.near[k], ACROSS)]

    def inner_on(self, k):
        self.inner[k][0] = self.layer.relay(self.inner[k][0])
        self.inner[k].append(node_swap(self.inner[k][0], OUTWARD))

    def outer_on(self, k):
        self.outer[k][0] = self.layer.relay(self.outer[k][0])
        self.outer[k].append(node_swap(self.outer[k][0], OUTWARD))

    def weight(self, k):
        back, weights = self.layer.weight_grad(
            k, self.place, self.w_self, self.feats, self.means[k], self.grads[k], self.weights
        )
        self.self_back[k] = back
        self.weights = weights
        if k == CHUNKS - 1:
            self.weights_in = node_swap(weights, OTHER_X)

    def weight_sum(self, pairs):
        self.weights = self.layer.added(self.weights, self.weights_in)
        if pairs is None:
            self.weights_in = feat_swap(self.weights, OTHER_CORE)
        else:
            self.weights_in = node_swap(self.weights, pairs)

    def weight_cores(self):
        self.weights = self.layer.both_cores(self.place, self.weights, self.weights_in)
        self.weights_in = feat_swap(self.weights, OTHER_Y)

    def weight_whole(self):
        self.weights = self.layer.whole_weights(self.place, self.weights, self.weights_in)

    def sources(self, role):
        if role in (SELF, NEAR):
            return [(self.own if role == SELF else self.near)[k] for k in range(CHUNKS)]
        held = self.inner if role == FAR_INNER else self.outer
        return [held[k][0] for k in range(CHUNKS)] + [held[k][1] for k in range(CHUNKS)]

    def pick(self, role):
        self.returned[role] = node_swap(self.layer.picked(role, self.place, self.rows, self.sources(role)), OTHER_X)

    def spread(self, local, slots):
        jobs = [] if local is None else [(local, self.sources(local))]
        jobs += [] if slots is None else [(slots, [self.returned[slots]])]
        first = self.total is None
        back = [self.self_back[k] for k in range(CHUNKS)] if first else None
        self.total = self.layer.spread(
            self.place, self.cols, self.rows, self.tiles, jobs, self.total, back, last=local is None
        )


def chain_shards(node_feats, tiles, send_col, recv_row, degree, w_self, w_neigh, bias, cotangent):
    slices, owned = node_feats.shape
    width = w_self.shape[1]
    layer = Layer(slices, owned, tiles.shape[1], 4, width)
    node, feat = lax.axis_index("node"), lax.axis_index("feat")
    place = jnp.stack([node // 2, node % 2, feat // 2, feat % 2]).astype(jnp.int32)
    inverse = (1.0 / degree.astype(F32)).reshape(-1, TB)
    steps = Steps(
        layer, place, node_feats, tiles, send_col, recv_row, inverse, w_self, w_neigh, bias.reshape(1, width), cotangent
    )
    for name, *arguments in ORDER:
        getattr(steps, name)(*arguments)
    grad_self, grad_neigh, grad_bias = steps.weights
    return (steps.activated, steps.total, grad_self, grad_neigh, grad_bias.reshape(width))


def slot_shards(node_feats, tiles, send_col, recv_row, degree, w_self, w_neigh, bias, cotangent):
    slices, owned = node_feats.shape
    blocks = owned // TB
    block_ids = jnp.arange(blocks, dtype=jnp.int32)
    scale = degree.astype(F32)[None, :]
    col_onehot = (send_col[..., None] == block_ids).astype(F32)
    row_onehot = (recv_row[..., None] == block_ids).astype(F32)
    feat_blocks = node_feats.reshape(slices, blocks, TB)
    picked = jnp.einsum("dcb,fbj->dcfj", col_onehot, feat_blocks, precision=HIGH)
    partial_value = jnp.einsum("dcfj,dcij->dcfi", picked, tiles, precision=HIGH)
    arrived = lax.all_to_all(partial_value, "node", split_axis=0, concat_axis=0, tiled=True)
    summed = jnp.einsum("scfi,scb->fbi", arrived, row_onehot, precision=HIGH)
    neighbour = summed.reshape(slices, owned) / scale
    offset = lax.axis_index("feat") * slices
    self_rows = lax.dynamic_slice_in_dim(w_self, offset, slices, 0)
    neigh_rows = lax.dynamic_slice_in_dim(w_neigh, offset, slices, 0)
    dims = (((0,), (0,)), ((), ()))
    first = lax.dot_general(node_feats, self_rows, dims, precision=HIGH)
    second = lax.dot_general(neighbour, neigh_rows, dims, precision=HIGH)
    pre = lax.psum_scatter(first + second, "feat", scatter_dimension=0, tiled=True) + bias
    sigma = jax.nn.sigmoid(pre)
    activated = pre * sigma
    gpre = cotangent * sigma * (1.0 + pre * (1.0 - sigma))
    piece = lax.all_gather(gpre, "feat", axis=0, tiled=True)
    dims = (((1,), (1,)), ((), ()))
    self_back = lax.dot_general(self_rows, piece, dims, precision=HIGH)
    neigh_back = lax.dot_general(neigh_rows, piece, dims, precision=HIGH)
    slice_self = jnp.dot(node_feats, piece, precision=HIGH)
    slice_neigh = jnp.dot(neighbour, piece, precision=HIGH)
    sums = lax.psum((slice_self, slice_neigh, jnp.sum(piece, axis=0)), "node")
    grad_self, grad_neigh = (lax.all_gather(part, "feat", axis=0, tiled=True) for part in sums[:2])
    gneigh = (neigh_back / scale).reshape(slices, blocks, TB)
    outgoing = jnp.einsum("scb,fbi->scfi", row_onehot, gneigh, precision=HIGH)
    returned = lax.all_to_all(outgoing, "node", split_axis=0, concat_axis=0, tiled=True)
    spread = jnp.einsum("dcfi,dcij->dcfj", returned, tiles, precision=HIGH)
    placed = jnp.einsum("dcfj,dcb->fbj", spread, col_onehot, precision=HIGH)
    grad_feats = self_back + placed.reshape(slices, owned)
    return (activated, grad_feats, grad_self, grad_neigh, sums[2])


def solution(mesh):
    chain = mesh.shape["node"] == 8 and mesh.shape["feat"] == 4
    return jax.shard_map(
        chain_shards if chain else slot_shards,
        mesh=mesh,
        in_specs=(
            P("feat", "node"),
            P("node", None, None, None),
            P("node", None),
            P("node", None),
            P("node"),
            P(),
            P(),
            P(),
            P(("node", "feat"), None),
        ),
        out_specs=(P(("node", "feat"), None), P("feat", "node"), P(), P(), P()),
        check_vma=False,
    )
```

```python
import jax
import jax.numpy as jnp
from jax import lax
from jax.experimental import pallas as pl
from jax.experimental.pallas import tpu as pltpu
from jax.sharding import PartitionSpec as P

TB = 128
F32 = jnp.float32
BF16 = jnp.bfloat16
HIGH = lax.Precision.HIGH
CHUNKS = 2
VMEM_BYTES = 28 * 2**20
FIRST_VMEM_BYTES = 57 * 2**20

FAR_OUTER, FAR_INNER, NEAR, SELF = range(4)


def owner(role, z):
    if role == FAR_OUTER:
        return jnp.where(z < 2, 3, 0)
    if role == FAR_INNER:
        return jnp.where(z < 2, 2, 1)
    if role == NEAR:
        return z + 1 - 2 * (z % 2)
    return z


def inner_place(place):
    return (place[0] == 1) | (place[0] == 2)


def split(value):
    high = value.astype(BF16)
    return high, (value - high.astype(F32)).astype(BF16)


def dot_nn(a, b):
    return lax.dot_general(a, b, (((1,), (0,)), ((), ())), preferred_element_type=F32)


def dot_nt(a, b):
    return lax.dot_general(a, b, (((1,), (1,)), ((), ())), preferred_element_type=F32)


def stacked(value):
    high, low = split(value)
    return jnp.concatenate(
        [jnp.concatenate([high, high], 1), jnp.concatenate([low, jnp.zeros_like(low)], 1)], 0
    )


def times_tile_t(value, tile):
    rows = value.shape[0]
    out = dot_nt(stacked(value), jnp.concatenate(split(tile), 1))
    return out[:rows] + out[rows:]


def times_tile(value, tile):
    rows = value.shape[0]
    out = dot_nn(stacked(value), jnp.concatenate(split(tile), 0))
    return out[:rows] + out[rows:]


def lanes(block):
    return pl.ds(pl.multiple_of(block * TB, TB), TB)


class Layer:
    def __init__(self, slices, owned, cap, parts, width):
        self.slices, self.owned, self.cap, self.parts, self.width = slices, owned, cap, parts, width
        self.blocks = owned // TB
        self.per_part = self.blocks // parts
        self.per_piece = self.per_part // CHUNKS
        self.per_chunk = self.blocks // CHUNKS
        self.piece = self.per_piece * TB
        self.span = self.per_chunk * TB
        self.token = None
        self.pending = []

    def spot(self, row):
        row = jnp.maximum(row, 0)
        part, inside = row // self.per_part, row % self.per_part
        return inside // self.per_piece, part * self.per_piece + inside % self.per_piece

    def block(self, chunk, part, inside):
        return part * self.per_part + chunk * self.per_piece + inside

    def full(self, *shape):
        return pl.BlockSpec(shape, lambda *_: (0,) * len(shape))

    def dense_spec(self):
        return self.full(self.per_chunk, self.slices, TB)

    def slots_spec(self):
        return self.full(self.cap, self.slices, TB)

    def slots(self):
        return jax.ShapeDtypeStruct((self.cap, self.slices, TB), F32)

    def dense(self):
        return jax.ShapeDtypeStruct((self.per_chunk, self.slices, TB), F32)

    def call(self, body, scalars, grid, in_specs, args, out_specs, out_shape, scratch=(), aliases=None, after=(), vmem=VMEM_BYTES):
        given = len(scalars) + len(args)
        waits = list(after) + self.pending + ([] if self.token is None else [self.token])
        self.pending = []

        def ordered(*refs):
            body(*refs[:given], *refs[given + len(waits) :])

        out = pl.pallas_call(
            ordered,
            grid_spec=pltpu.PrefetchScalarGridSpec(
                num_scalar_prefetch=len(scalars),
                grid=grid,
                in_specs=list(in_specs) + [pl.BlockSpec(memory_space=pl.ANY)] * len(waits),
                out_specs=out_specs,
                scratch_shapes=scratch,
            ),
            out_shape=out_shape,
            input_output_aliases=aliases or {},
            compiler_params=pltpu.CompilerParams(vmem_limit_bytes=vmem),
            cost_estimate=pl.CostEstimate(flops=1, bytes_accessed=1, transcendentals=0),
        )(*scalars, *args, *waits)
        self.token = jax.tree.leaves(out)[-1]
        return out

    def relay(self, value, after=()):
        def body(value, out):
            pass

        anywhere = pl.BlockSpec(memory_space=pl.ANY)
        return self.call(
            body, (), (1,), [anywhere], (value,), anywhere, jax.ShapeDtypeStruct(value.shape, value.dtype),
            aliases={0: 0}, after=after,
        )

    def added(self, a, b):
        def body(a, b, out):
            out[...] = a[...] + b[...]

        spec = self.full(*a.shape)
        return self.call(body, (), (1,), [spec] * 2, (a, b), spec, jax.ShapeDtypeStruct(a.shape, F32))

    def added_across(self, place, a, across):
        def body(place, a, across, out):
            out[...] = a[...] + jnp.where(inner_place(place), across[...], 0.0)

        return self.call(body, (place,), (1,), [self.dense_spec()] * 2, (a, across), self.dense_spec(), self.dense())

    def fetched(self, count):
        return [pltpu.VMEM((count, self.cap, TB, TB), F32), pltpu.SemaphoreType.DMA((count,))]

    def fetch(self, tiles, buffer, sems, index, slot):
        return pltpu.make_async_copy(tiles.at[index], buffer.at[slot], sems.at[slot])

    def tiles_spec(self):
        return pl.BlockSpec(memory_space=pl.ANY)

    def first_slots(self, role, place, cols, feats, tiles):
        groups = 4
        per_group = self.cap // groups

        def body(place, cols, feats, tiles, out, done, held, buffer, sems):
            done[...] = jnp.zeros_like(done)
            owned_by = owner(role, place[0]) * 2 + 1 - place[1]
            copies = [pltpu.make_async_copy(feats, held, sems.at[groups])]
            for g in range(groups):
                some = pl.ds(g * per_group, per_group)
                copies.append(pltpu.make_async_copy(tiles.at[owned_by, some], buffer.at[some], sems.at[g]))
            for copy in copies:
                copy.start()
            for g in range(groups):
                if g == 0:
                    copies[0].wait()
                copies[1 + g].wait()
                for c in range(g * per_group, (g + 1) * per_group):
                    out[c] = times_tile_t(held[:, lanes(cols[owned_by, c])], buffer[c])

        return self.call(
            body, (place, cols), (1,), [self.tiles_spec()] * 2, (feats, tiles), [self.slots_spec(), self.full(8, TB)],
            [self.slots(), jax.ShapeDtypeStruct((8, TB), F32)],
            scratch=[
                pltpu.VMEM((self.slices, self.owned), F32),
                pltpu.VMEM((self.cap, TB, TB), F32),
                pltpu.SemaphoreType.DMA((groups + 1,)),
            ],
            vmem=FIRST_VMEM_BYTES,
        )[0]

    def later_slots(self, roles, place, cols, feats, tiles):
        def body(place, cols, feats, tiles, *rest):
            outs, (buffer, sems) = rest[: len(roles)], rest[len(roles) :]
            owners = [owner(role, place[0]) * 2 + 1 - place[1] for role in roles]
            copies = [self.fetch(tiles, buffer, sems, owned_by, i) for i, owned_by in enumerate(owners)]
            for copy in copies:
                copy.start()
            for i, owned_by in enumerate(owners):
                copies[i].wait()
                for c in range(self.cap):
                    outs[i][c] = times_tile_t(feats[:, lanes(cols[owned_by, c])], buffer[i, c])

        return self.call(
            body, (place, cols), (1,), [self.full(self.slices, self.owned), self.tiles_spec()], (feats, tiles),
            [self.slots_spec()] * len(roles), [self.slots()] * len(roles), scratch=self.fetched(len(roles)),
        )

    def dense_sums(self, role, place, cols, rows, feats, tiles, slots):
        def body(place, cols, rows, feats, tiles, slots, *rest):
            outs, (buffer, sems) = rest[:CHUNKS], rest[CHUNKS:]
            z, x = place[0], place[1]
            owned_by = owner(role, z) * 2 + x
            copy = self.fetch(tiles, buffer, sems, owned_by, 0)
            copy.start()
            for out in outs:
                out[...] = jnp.zeros_like(out)

            def add(row, value):
                chunk, spot = self.spot(row)
                for k, out in enumerate(outs):
                    out[spot] += jnp.where((row >= 0) & (chunk == k), value, 0.0)

            for c in range(self.cap):
                add(rows[self.row_index(role, z, 1 - x), c], slots[c])
            copy.wait()
            for c in range(self.cap):
                value = times_tile_t(feats[:, lanes(cols[owned_by, c])], buffer[0, c])
                add(rows[self.row_index(role, z, x), c], value)

        return self.call(
            body, (place, cols, rows), (1,),
            [self.full(self.slices, self.owned), self.tiles_spec(), self.slots_spec()], (feats, tiles, slots),
            [self.dense_spec()] * CHUNKS, [self.dense()] * CHUNKS, scratch=self.fetched(1),
        )

    def stacked_tables(self, first, second):
        def body(first, second, out):
            out[: first.shape[0], :] = first[...]
            out[first.shape[0] :, :] = second[...]

        shape = (2 * first.shape[0], first.shape[1])
        return self.call(
            body, (), (1,), [self.full(*first.shape)] * 2, (first, second), self.full(*shape),
            jax.ShapeDtypeStruct(shape, first.dtype),
        )

    def own_rows(self, place, pair, other_pair):
        half = pair.shape[0] // 2

        def body(place, pair, other, out):
            for distance in range(4):
                table = (pair, other)[distance // 2]
                start = half * (distance % 2) + 2 * place[0]
                out[2 * distance : 2 * distance + 2, :] = table[pl.ds(start, 2), :]

        shape = (half, pair.shape[1])
        return self.call(
            body, (place,), (1,), [self.full(*pair.shape)] * 2, (pair, other_pair), self.full(*shape),
            jax.ShapeDtypeStruct(shape, pair.dtype),
        )

    def row_index(self, role, z, sender_x):
        return (owner(role, z) ^ z) * 2 + sender_x

    def means(self, k, place, pieces, inverse):
        def body(place, own, near, across, inverse, out):
            for part in range(self.parts):
                for j in range(self.per_piece):
                    spot, block = part * self.per_piece + j, self.block(k, part, j)
                    total = own[spot] + near[spot] + jnp.where(inner_place(place), across[spot], 0.0)
                    out[spot] = total * inverse[block : block + 1, :]

        return self.call(
            body, (place,), (1,), [self.dense_spec()] * 3 + [self.full(self.blocks, TB)], (*pieces, inverse),
            self.dense_spec(), self.dense(),
        )

    def loaded(self, feats, tiles, cotangent):
        def body(feats, tiles, cotangent, feats_out, tiles_out, cotangent_out, sems):
            copies = [
                pltpu.make_async_copy(feats, feats_out, sems.at[0]),
                pltpu.make_async_copy(tiles, tiles_out, sems.at[1]),
            ]
            for copy in copies:
                copy.start()
            cotangent_out[...] = cotangent[...].T
            for copy in copies:
                copy.wait()

        rows, cols = cotangent.shape
        anywhere = pl.BlockSpec(memory_space=pl.ANY)
        return self.call(
            body, (), (1,), [anywhere, anywhere, self.full(rows, cols)], (feats, tiles, cotangent),
            [anywhere, anywhere, self.full(cols, rows)],
            [pltpu.VMEM(feats.shape, F32), pltpu.VMEM(tiles.shape, F32), jax.ShapeDtypeStruct((cols, rows), F32)],
            scratch=[pltpu.SemaphoreType.DMA((2,))],
        )

    def copied(self, table):
        def body(table, out):
            out[...] = table[...]

        spec = self.full(*table.shape)
        return self.call(body, (), (1,), [spec], (table,), spec, jax.ShapeDtypeStruct(table.shape, table.dtype))

    def feats_of(self, place):
        y, core = place[2], place[3]
        return (2 * y + core, 2 * (1 - y) + core, 2 * y + 1 - core, 2 * (1 - y) + 1 - core)

    def times_weight(self, weight_t, high, low):
        rows = weight_t.shape[0]
        weight_high, weight_low = split(weight_t)
        out = dot_nn(jnp.concatenate([weight_high, weight_low], 0), high)
        return out[:rows] + out[rows:] + dot_nn(weight_high, low)

    def self_part(self, place, slices, w_self, bias):
        def body(place, own, far, core, both, w_self, bias, out, held):
            for index, piece in zip(self.feats_of(place), (own, far, core, both)):
                held[pl.ds(pl.multiple_of(index * self.slices, self.slices), self.slices), :] = piece[...]
            column = jnp.broadcast_to(bias[...], (TB, self.width)).T
            value = self.times_weight(w_self[...].T, *split(held[...]))
            out[0] = value + jnp.concatenate([column] * self.per_piece, 1)

        columns = pl.BlockSpec((self.slices, self.piece), lambda k, part, *_: (0, part * CHUNKS + k))
        return self.call(
            body, (place,), (CHUNKS, self.parts),
            [columns] * 4 + [self.full(self.width, self.width), self.full(1, self.width)], (*slices, w_self, bias),
            pl.BlockSpec((1, self.width, self.piece), lambda k, part, *_: (k, 0, part)),
            jax.ShapeDtypeStruct((CHUNKS, self.width, self.span), F32),
            scratch=[pltpu.VMEM((self.width, self.piece), F32)],
        )

    def activate(self, k, place, means, w_neigh, self_part, cotangents, inverse, activated):
        rows = pl.BlockSpec((self.piece, self.width), lambda *_: (k, 0))

        def body(place, m0, m1, m2, m3, weight, self_part, c0, c1, c2, c3, inverse, *rest):
            out, grad, back, high, low = rest[-5:]
            feats = self.feats_of(place)
            for index, piece in zip(feats, (m0, m1, m2, m3)):
                at = pl.ds(pl.multiple_of(index * self.slices, self.slices), self.slices)
                for spot in range(self.per_chunk):
                    columns = slice(spot * TB, (spot + 1) * TB)
                    high[at, columns], low[at, columns] = split(piece[spot])
            weight_t = weight[...].T
            own_rows = weight[pl.ds(pl.multiple_of(feats[0] * self.slices, self.slices), self.slices), :]
            for part, cotangent in zip(feats, (c0, c1, c2, c3)):
                at = pl.ds(pl.multiple_of(part * self.piece, self.piece), self.piece)
                pre = self.times_weight(weight_t, high[:, at], low[:, at]) + self_part[0, :, at]
                sigma = jax.nn.sigmoid(pre)
                if cotangent is c0:
                    out[...] = (pre * sigma).T
                slope = cotangent[...] * (sigma * (1.0 + pre * (1.0 - sigma)))
                grad[:, at] = slope
                value = self.times_weight(own_rows, *split(slope))
                for j in range(self.per_piece):
                    scale = inverse[pl.ds(self.block(k, part, j), 1), :]
                    back[part * self.per_piece + j] = value[:, j * TB : (j + 1) * TB] * scale

        in_specs = (
            [self.dense_spec()] * 4
            + [self.full(self.width, self.width)]
            + [pl.BlockSpec((1, self.width, self.span), lambda *_: (k, 0, 0))]
            + [pl.BlockSpec((self.width, self.piece), lambda *_: (0, k))] * 4
            + [self.full(self.blocks, TB)]
        )
        args = [*means, w_neigh, self_part, *cotangents, inverse]
        aliases = {}
        if activated is not None:
            aliases = {1 + len(args): 0}
            in_specs.append(pl.BlockSpec(memory_space=pl.ANY))
            args.append(activated)
        return self.call(
            body, (place,), (1,), in_specs, args,
            [rows, self.full(self.width, self.span), self.dense_spec()],
            [jax.ShapeDtypeStruct((self.per_part * TB, self.width), F32),
             jax.ShapeDtypeStruct((self.width, self.span), F32), self.dense()],
            scratch=[pltpu.VMEM((self.width, self.span), BF16)] * 2, aliases=aliases,
        )

    def weight_grad(self, k, place, w_self, feats, means, grad, before):
        shape = (2 * self.slices + 16, self.width)

        def body(place, w_self, feats, means, grad, *rest):
            self_out, weights_out = rest[-2:]
            total = rest[0][...] if before is not None else jnp.zeros(shape, F32)
            for part in range(self.parts):
                first = part * self.per_piece
                at = slice(part * self.piece, (part + 1) * self.piece)
                high, low = split(grad[:, at])
                value = self.times_weight(w_self[...], high, low)
                for j in range(self.per_piece):
                    self_out[first + j] = value[:, j * TB : (j + 1) * TB]
                start = self.block(k, part, 0) * TB
                rows = jnp.concatenate(
                    [
                        feats[:, start : start + self.piece],
                        jnp.concatenate([means[first + j] for j in range(self.per_piece)], 1),
                        jnp.ones((16, self.piece), F32),
                    ],
                    0,
                )
                rows_high, rows_low = split(rows)
                total += (dot_nt(rows_high, high) + dot_nt(rows_low, high)) + dot_nt(rows_high, low)
            weights_out[...] = total

        weight_rows = pl.BlockSpec((self.slices, self.width), lambda i, place, *_: (2 * place[2] + place[3], 0))
        args = [w_self, feats, means, grad] + ([] if before is None else [before])
        return self.call(
            body, (place,), (1,),
            [weight_rows, self.full(self.slices, self.owned), self.dense_spec(), self.full(self.width, self.span)]
            + [self.full(*shape)] * (before is not None),
            args, [self.dense_spec(), self.full(*shape)], [self.dense(), jax.ShapeDtypeStruct(shape, F32)],
        )

    def both_cores(self, place, mine, other):
        def body(place, mine, other, out):
            out[place[3]] = mine[...]
            out[1 - place[3]] = other[...]

        shape = (2, *mine.shape)
        return self.call(
            body, (place,), (1,), [self.full(*mine.shape)] * 2, (mine, other), self.full(*shape),
            jax.ShapeDtypeStruct(shape, F32),
        )

    def whole_weights(self, place, mine, other):
        def body(place, mine, other, w_self, w_neigh, bias):
            for y, block in ((place[2], mine), (1 - place[2], other)):
                for core in range(2):
                    at = pl.ds(pl.multiple_of((2 * y + core) * self.slices, self.slices), self.slices)
                    w_self[at, :] = block[core, : self.slices, :]
                    w_neigh[at, :] = block[core, self.slices : 2 * self.slices, :]
            bias[...] = mine[0, 2 * self.slices : 2 * self.slices + 1, :]

        square, row = (self.width, self.width), (1, self.width)
        return self.call(
            body, (place,), (1,), [self.full(*mine.shape)] * 2, (mine, other),
            [self.full(*square), self.full(*square), self.full(*row)],
            [jax.ShapeDtypeStruct(shape, F32) for shape in (square, square, row)],
        )

    def gather(self, place, sources, held):
        inner = inner_place(place)
        for k in range(CHUNKS):
            spots = slice(k * self.per_chunk, (k + 1) * self.per_chunk)
            if len(sources) == CHUNKS:
                held[spots] = sources[k][...]
            else:

                @pl.when(jnp.logical_not(inner))
                def _():
                    held[spots] = sources[CHUNKS + k][...]

                @pl.when(inner)
                def _():
                    held[spots] = sources[k][...]

    def held(self):
        return pltpu.VMEM((self.blocks, self.slices, TB), F32)

    def pick(self, row, held):
        chunk, spot = self.spot(row)
        return jnp.where(row >= 0, held[chunk * self.per_chunk + spot], 0.0)

    def picked(self, role, place, rows, sources):
        def body(place, rows, *rest):
            out, held = rest[-2:]
            self.gather(place, rest[:-2], held)
            row_of = self.row_index(role, place[0], 1 - place[1])
            for c in range(self.cap):
                out[c] = self.pick(rows[row_of, c], held)

        return self.call(
            body, (place, rows), (1,), [self.dense_spec()] * len(sources), sources,
            self.slots_spec(), self.slots(), scratch=[self.held()],
        )

    def spread(self, place, cols, rows, tiles, jobs, total=None, self_back=None, last=False):
        counts = [len(sources) for _, sources in jobs]
        extra = [total] if self_back is None else list(self_back)

        def body(place, cols, rows, tiles, *rest):
            arrays, more = rest[: sum(counts)], rest[sum(counts) : sum(counts) + len(extra)]
            out, done, held, buffer, sems = rest[sum(counts) + len(extra) :]
            done[...] = jnp.zeros_like(done)
            z, x = place[0], place[1]
            owners = [owner(role, z) * 2 + (1 - x if n == 1 else x) for (role, _), n in zip(jobs, counts)]
            copies = [self.fetch(tiles, buffer, sems, owned_by, i) for i, owned_by in enumerate(owners)]
            for copy in copies:
                copy.start()
            if self_back is None:
                out[...] = more[0][...]
            else:
                for k, back in enumerate(more):
                    for part in range(self.parts):
                        for j in range(self.per_piece):
                            block = self.block(k, part, j)
                            out[:, block * TB : (block + 1) * TB] = back[part * self.per_piece + j]
            for i, (role, _) in enumerate(jobs):
                sources = arrays[sum(counts[:i]) : sum(counts[: i + 1])]
                if counts[i] > 1:
                    self.gather(place, sources, held)
                copies[i].wait()
                for c in range(self.cap):
                    if counts[i] > 1:
                        value = self.pick(rows[self.row_index(role, z, x), c], held)
                    else:
                        value = sources[0][c]
                    out[:, lanes(cols[owners[i], c])] += times_tile(value, buffer[i, c])

        shape = (self.slices, self.owned)
        whole = self.full(*shape)
        in_specs, args = [self.tiles_spec()], [tiles]
        for _, sources in jobs:
            in_specs += [self.slots_spec() if len(sources) == 1 else self.dense_spec()] * len(sources)
            args += sources
        in_specs += [whole] if self_back is None else [self.dense_spec()] * CHUNKS
        args += extra
        return self.call(
            body, (place, cols, rows), (1,), in_specs, args, [whole, self.full(8, TB)],
            [
                jax.ShapeDtypeStruct(shape, F32) if last else pltpu.VMEM(shape, F32),
                jax.ShapeDtypeStruct((8, TB), F32),
            ],
            scratch=[self.held(), *self.fetched(len(jobs))],
            aliases={} if last or self_back is not None else {3 + len(args) - 1: 0},
        )[0]


def pairs_z(steps):
    return [(2 * a + x, 2 * b + x) for a, b in steps for x in range(2)]


ACROSS = pairs_z([(1, 2), (2, 1), (0, 0), (3, 3)])
OUTWARD = pairs_z([(1, 0), (2, 3)])
OTHER_X = [(n, n ^ 1) for n in range(8)]
OTHER_CORE = [(f, f ^ 1) for f in range(4)]
OTHER_Y = [(f, f ^ 2) for f in range(4)]


def along_z(distance):
    return pairs_z([(z, z ^ distance) for z in range(4)])


def node_swap(value, pairs):
    return lax.ppermute(value, "node", pairs)


def feat_swap(value, pairs):
    return lax.ppermute(value, "feat", pairs)


ORDER = [
    ("slots_first",),
    ("table_out",),
    ("load",),
    ("slots_later",),
    ("tables_out",),
    ("rows_in",),
    ("dense", FAR_OUTER),
    ("slots", FAR_INNER),
    ("send_in", FAR_OUTER, 1),
    ("pass_on", FAR_OUTER, 0),
    ("dense", FAR_INNER),
    ("slots", NEAR),
    ("pass_on", FAR_OUTER, 1),
    ("send_in", FAR_INNER, 1),
    ("dense", NEAR),
    ("feats_on",),
    ("slots", SELF),
    ("pass_on", NEAR, 0),
    ("pass_on", FAR_INNER, 0),
    ("pass_on", NEAR, 1),
    ("cotangents_on",),
    ("pass_on", FAR_INNER, 1),
    ("dense", SELF),
    ("mean", 0),
    ("mean", 1),
    ("means_on", 0),
    ("self_part",),
    ("means_on", 1),
    ("activate", 0),
    ("activate", 1),
    ("inner_on", 0),
    ("weight", 0),
    ("near_on", 0),
    ("weight", 1),
    ("pick", SELF),
    ("wait", "inner", 1, 0),
    ("wait", "near", 1),
    ("inner_on", 1),
    ("near_on", 1),
    ("pick", NEAR),
    ("weight_sum", along_z(1)),
    ("wait", "inner", 0, 1),
    ("outer_on", 0),
    ("wait", "inner", 1, 1),
    ("spread", SELF, None),
    ("wait", "returned", SELF),
    ("wait", "outer", 1, 0),
    ("weight_sum", along_z(3)),
    ("pick", FAR_INNER),
    ("outer_on", 1),
    ("spread", NEAR, SELF),
    ("wait", "returned", NEAR),
    ("wait", "outer", 0, 1),
    ("weight_sum", None),
    ("spread", FAR_INNER, NEAR),
    ("wait", "returned", FAR_INNER),
    ("weight_cores",),
    ("pick", FAR_OUTER),
    ("spread", FAR_OUTER, FAR_INNER),
    ("wait", "weights_in"),
    ("weight_whole",),
    ("spread", None, FAR_OUTER),
]


class Steps:
    def __init__(self, layer, place, node_feats, tiles, send_col, recv_row, inverse, w_self, w_neigh, bias, cotangent):
        self.layer, self.place, self.feats, self.tiles = layer, place, node_feats, tiles
        self.cols, self.table, self.inverse = send_col, recv_row, inverse
        self.w_self, self.w_neigh, self.bias, self.cotangent = w_self, w_neigh, bias, cotangent
        self.slots_in, self.joined, self.inward, self.returned = {}, {}, {}, {}
        self.across, self.nearby, self.means, self.mean_parts = {}, {}, {}, {}
        self.grads, self.own, self.near, self.inner, self.outer = {}, {}, {}, {}, {}
        self.self_back, self.activated, self.weights, self.total = {}, None, None, None

    def wait(self, name, *key):
        held = getattr(self, name)
        for index in key:
            held = held[index]
        self.layer.pending.append(held)

    def slots_first(self):
        part = self.layer.first_slots(FAR_OUTER, self.place, self.cols, self.feats, self.tiles)
        self.slots_in[FAR_OUTER] = node_swap(part, OTHER_X)

    def slots_later(self):
        self.parts = self.layer.later_slots((FAR_INNER, NEAR, SELF), self.place, self.cols, self.feats, self.tiles)

    def slots(self, role):
        part = self.layer.relay(self.parts[role - 1], after=[self.slots_in[role - 1]])
        self.slots_in[role] = node_swap(part, OTHER_X)

    def table_out(self):
        self.table = self.layer.copied(self.table)
        self.table_in = node_swap(self.table, along_z(1))

    def tables_out(self):
        self.tables = self.layer.stacked_tables(self.table, self.table_in)
        self.tables_in = node_swap(self.tables, along_z(2))

    def rows_in(self):
        self.rows = self.layer.own_rows(self.place, self.tables, self.tables_in)

    def load(self):
        feats, self.tiles, cotangent = self.layer.loaded(self.feats, self.tiles, self.cotangent)
        self.feats = feats
        self.feat_parts = [feats, feat_swap(feats, OTHER_Y), feat_swap(feats, OTHER_CORE)]
        self.cotangents = [cotangent, feat_swap(cotangent, OTHER_Y), feat_swap(cotangent, OTHER_CORE)]

    def on(self, parts):
        parts[1] = self.layer.relay(parts[1])
        parts.append(feat_swap(parts[1], OTHER_CORE))

    def feats_on(self):
        self.on(self.feat_parts)

    def cotangents_on(self):
        self.on(self.cotangents)

    def self_part(self):
        self.self_parts = self.layer.self_part(self.place, self.feat_parts, self.w_self, self.bias)

    def dense(self, role):
        sums = self.layer.dense_sums(
            role, self.place, self.cols, self.rows, self.feats, self.tiles, self.slots_in[role]
        )
        for k in range(CHUNKS):
            self.joined[role, k] = sums[k]
        if role in (FAR_OUTER, FAR_INNER):
            self.inward[role, 0] = node_swap(sums[0], along_z(1))

    def send_in(self, role, k):
        self.joined[role, k] = self.layer.relay(self.joined[role, k])
        self.inward[role, k] = node_swap(self.joined[role, k], along_z(1))

    def pass_on(self, role, k):
        if role == NEAR:
            part = self.layer.added_across(self.place, self.joined[NEAR, k], self.across[FAR_OUTER, k])
            self.nearby[k] = node_swap(part, along_z(1))
        else:
            part = self.layer.added(self.joined[role, k], self.inward[role, k])
            self.across[role, k] = node_swap(part, ACROSS)

    def mean(self, k):
        pieces = (self.joined[SELF, k], self.nearby[k], self.across[FAR_INNER, k])
        means = self.layer.means(k, self.place, pieces, self.inverse)
        self.means[k] = means
        self.mean_parts[k] = [means, feat_swap(means, OTHER_Y), feat_swap(means, OTHER_CORE)]

    def means_on(self, k):
        self.on(self.mean_parts[k])

    def activate(self, k):
        self.activated, self.grads[k], back = self.layer.activate(
            k, self.place, self.mean_parts[k], self.w_neigh, self.self_parts, self.cotangents, self.inverse, self.activated
        )
        self.own[k] = back
        self.near[k] = node_swap(back, along_z(1))
        self.inner[k] = [node_swap(back, ACROSS)]

    def near_on(self, k):
        self.near[k] = self.layer.relay(self.near[k])
        self.outer[k] = [node_swap(self.near[k], ACROSS)]

    def inner_on(self, k):
        self.inner[k][0] = self.layer.relay(self.inner[k][0])
        self.inner[k].append(node_swap(self.inner[k][0], OUTWARD))

    def outer_on(self, k):
        self.outer[k][0] = self.layer.relay(self.outer[k][0])
        self.outer[k].append(node_swap(self.outer[k][0], OUTWARD))

    def weight(self, k):
        back, weights = self.layer.weight_grad(
            k, self.place, self.w_self, self.feats, self.means[k], self.grads[k], self.weights
        )
        self.self_back[k] = back
        self.weights = weights
        if k == CHUNKS - 1:
            self.weights_in = node_swap(weights, OTHER_X)

    def weight_sum(self, pairs):
        self.weights = self.layer.added(self.weights, self.weights_in)
        if pairs is None:
            self.weights_in = feat_swap(self.weights, OTHER_CORE)
        else:
            self.weights_in = node_swap(self.weights, pairs)

    def weight_cores(self):
        self.weights = self.layer.both_cores(self.place, self.weights, self.weights_in)
        self.weights_in = feat_swap(self.weights, OTHER_Y)

    def weight_whole(self):
        self.weights = self.layer.whole_weights(self.place, self.weights, self.weights_in)

    def sources(self, role):
        if role in (SELF, NEAR):
            return [(self.own if role == SELF else self.near)[k] for k in range(CHUNKS)]
        held = self.inner if role == FAR_INNER else self.outer
        return [held[k][0] for k in range(CHUNKS)] + [held[k][1] for k in range(CHUNKS)]

    def pick(self, role):
        self.returned[role] = node_swap(self.layer.picked(role, self.place, self.rows, self.sources(role)), OTHER_X)

    def spread(self, local, slots):
        jobs = [] if local is None else [(local, self.sources(local))]
        jobs += [] if slots is None else [(slots, [self.returned[slots]])]
        first = self.total is None
        back = [self.self_back[k] for k in range(CHUNKS)] if first else None
        self.total = self.layer.spread(
            self.place, self.cols, self.rows, self.tiles, jobs, self.total, back, last=local is None
        )


def chain_shards(node_feats, tiles, send_col, recv_row, degree, w_self, w_neigh, bias, cotangent):
    slices, owned = node_feats.shape
    width = w_self.shape[1]
    layer = Layer(slices, owned, tiles.shape[1], 4, width)
    node, feat = lax.axis_index("node"), lax.axis_index("feat")
    place = jnp.stack([node // 2, node % 2, feat // 2, feat % 2]).astype(jnp.int32)
    inverse = (1.0 / degree.astype(F32)).reshape(-1, TB)
    steps = Steps(
        layer, place, node_feats, tiles, send_col, recv_row, inverse, w_self, w_neigh, bias.reshape(1, width), cotangent
    )
    for name, *arguments in ORDER:
        getattr(steps, name)(*arguments)
    grad_self, grad_neigh, grad_bias = steps.weights
    return (steps.activated, steps.total, grad_self, grad_neigh, grad_bias.reshape(width))


def slot_shards(node_feats, tiles, send_col, recv_row, degree, w_self, w_neigh, bias, cotangent):
    slices, owned = node_feats.shape
    blocks = owned // TB
    block_ids = jnp.arange(blocks, dtype=jnp.int32)
    scale = degree.astype(F32)[None, :]
    col_onehot = (send_col[..., None] == block_ids).astype(F32)
    row_onehot = (recv_row[..., None] == block_ids).astype(F32)
    feat_blocks = node_feats.reshape(slices, blocks, TB)
    picked = jnp.einsum("dcb,fbj->dcfj", col_onehot, feat_blocks, precision=HIGH)
    partial_value = jnp.einsum("dcfj,dcij->dcfi", picked, tiles, precision=HIGH)
    arrived = lax.all_to_all(partial_value, "node", split_axis=0, concat_axis=0, tiled=True)
    summed = jnp.einsum("scfi,scb->fbi", arrived, row_onehot, precision=HIGH)
    neighbour = summed.reshape(slices, owned) / scale
    offset = lax.axis_index("feat") * slices
    self_rows = lax.dynamic_slice_in_dim(w_self, offset, slices, 0)
    neigh_rows = lax.dynamic_slice_in_dim(w_neigh, offset, slices, 0)
    dims = (((0,), (0,)), ((), ()))
    first = lax.dot_general(node_feats, self_rows, dims, precision=HIGH)
    second = lax.dot_general(neighbour, neigh_rows, dims, precision=HIGH)
    pre = lax.psum_scatter(first + second, "feat", scatter_dimension=0, tiled=True) + bias
    sigma = jax.nn.sigmoid(pre)
    activated = pre * sigma
    gpre = cotangent * sigma * (1.0 + pre * (1.0 - sigma))
    piece = lax.all_gather(gpre, "feat", axis=0, tiled=True)
    dims = (((1,), (1,)), ((), ()))
    self_back = lax.dot_general(self_rows, piece, dims, precision=HIGH)
    neigh_back = lax.dot_general(neigh_rows, piece, dims, precision=HIGH)
    slice_self = jnp.dot(node_feats, piece, precision=HIGH)
    slice_neigh = jnp.dot(neighbour, piece, precision=HIGH)
    sums = lax.psum((slice_self, slice_neigh, jnp.sum(piece, axis=0)), "node")
    grad_self, grad_neigh = (lax.all_gather(part, "feat", axis=0, tiled=True) for part in sums[:2])
    gneigh = (neigh_back / scale).reshape(slices, blocks, TB)
    outgoing = jnp.einsum("scb,fbi->scfi", row_onehot, gneigh, precision=HIGH)
    returned = lax.all_to_all(outgoing, "node", split_axis=0, concat_axis=0, tiled=True)
    spread = jnp.einsum("dcfi,dcij->dcfj", returned, tiles, precision=HIGH)
    placed = jnp.einsum("dcfj,dcb->fbj", spread, col_onehot, precision=HIGH)
    grad_feats = self_back + placed.reshape(slices, owned)
    return (activated, grad_feats, grad_self, grad_neigh, sums[2])


def solution(mesh):
    chain = mesh.shape["node"] == 8 and mesh.shape["feat"] == 4
    return jax.shard_map(
        chain_shards if chain else slot_shards,
        mesh=mesh,
        in_specs=(
            P("feat", "node"),
            P("node", None, None, None),
            P("node", None),
            P("node", None),
            P("node"),
            P(),
            P(),
            P(),
            P(("node", "feat"), None),
        ),
        out_specs=(P(("node", "feat"), None), P("feat", "node"), P(), P(), P()),
        check_vma=False,
    )
```

```python
import jax
import jax.numpy as jnp
from jax import lax
from jax.experimental import pallas as pl
from jax.experimental.pallas import tpu as pltpu
from jax.sharding import PartitionSpec as P

TB = 128
F32 = jnp.float32
BF16 = jnp.bfloat16
HIGH = lax.Precision.HIGH
CHUNKS = 2
VMEM_BYTES = 28 * 2**20
FIRST_VMEM_BYTES = 57 * 2**20

FAR_OUTER, FAR_INNER, NEAR, SELF = range(4)


def owner(role, z):
    if role == FAR_OUTER:
        return jnp.where(z < 2, 3, 0)
    if role == FAR_INNER:
        return jnp.where(z < 2, 2, 1)
    if role == NEAR:
        return z + 1 - 2 * (z % 2)
    return z


def inner_place(place):
    return (place[0] == 1) | (place[0] == 2)


def split(value):
    high = value.astype(BF16)
    return high, (value - high.astype(F32)).astype(BF16)


def dot_nn(a, b):
    return lax.dot_general(a, b, (((1,), (0,)), ((), ())), preferred_element_type=F32)


def dot_nt(a, b):
    return lax.dot_general(a, b, (((1,), (1,)), ((), ())), preferred_element_type=F32)


def stacked(value):
    high, low = split(value)
    return jnp.concatenate(
        [jnp.concatenate([high, high], 1), jnp.concatenate([low, jnp.zeros_like(low)], 1)], 0
    )


def times_tile_t(value, tile):
    rows = value.shape[0]
    out = dot_nt(stacked(value), jnp.concatenate(split(tile), 1))
    return out[:rows] + out[rows:]


def times_tile(value, tile):
    rows = value.shape[0]
    out = dot_nn(stacked(value), jnp.concatenate(split(tile), 0))
    return out[:rows] + out[rows:]


def lanes(block):
    return pl.ds(pl.multiple_of(block * TB, TB), TB)


class Layer:
    def __init__(self, slices, owned, cap, parts, width):
        self.slices, self.owned, self.cap, self.parts, self.width = slices, owned, cap, parts, width
        self.blocks = owned // TB
        self.per_part = self.blocks // parts
        self.per_piece = self.per_part // CHUNKS
        self.per_chunk = self.blocks // CHUNKS
        self.piece = self.per_piece * TB
        self.span = self.per_chunk * TB
        self.token = None
        self.pending = []

    def spot(self, row):
        row = jnp.maximum(row, 0)
        part, inside = row // self.per_part, row % self.per_part
        return inside // self.per_piece, part * self.per_piece + inside % self.per_piece

    def block(self, chunk, part, inside):
        return part * self.per_part + chunk * self.per_piece + inside

    def full(self, *shape):
        return pl.BlockSpec(shape, lambda *_: (0,) * len(shape))

    def dense_spec(self):
        return self.full(self.per_chunk, self.slices, TB)

    def slots_spec(self):
        return self.full(self.cap, self.slices, TB)

    def slots(self):
        return jax.ShapeDtypeStruct((self.cap, self.slices, TB), F32)

    def dense(self):
        return jax.ShapeDtypeStruct((self.per_chunk, self.slices, TB), F32)

    def call(self, body, scalars, grid, in_specs, args, out_specs, out_shape, scratch=(), aliases=None, after=(), vmem=VMEM_BYTES):
        given = len(scalars) + len(args)
        waits = list(after) + self.pending + ([] if self.token is None else [self.token])
        self.pending = []

        def ordered(*refs):
            body(*refs[:given], *refs[given + len(waits) :])

        out = pl.pallas_call(
            ordered,
            grid_spec=pltpu.PrefetchScalarGridSpec(
                num_scalar_prefetch=len(scalars),
                grid=grid,
                in_specs=list(in_specs) + [pl.BlockSpec(memory_space=pl.ANY)] * len(waits),
                out_specs=out_specs,
                scratch_shapes=scratch,
            ),
            out_shape=out_shape,
            input_output_aliases=aliases or {},
            compiler_params=pltpu.CompilerParams(vmem_limit_bytes=vmem),
            cost_estimate=pl.CostEstimate(flops=1, bytes_accessed=1, transcendentals=0),
        )(*scalars, *args, *waits)
        self.token = jax.tree.leaves(out)[-1]
        return out

    def relay(self, value, after=()):
        def body(value, out):
            pass

        anywhere = pl.BlockSpec(memory_space=pl.ANY)
        return self.call(
            body, (), (1,), [anywhere], (value,), anywhere, jax.ShapeDtypeStruct(value.shape, value.dtype),
            aliases={0: 0}, after=after,
        )

    def added(self, a, b):
        def body(a, b, out):
            out[...] = a[...] + b[...]

        spec = self.full(*a.shape)
        return self.call(body, (), (1,), [spec] * 2, (a, b), spec, jax.ShapeDtypeStruct(a.shape, F32))

    def added_across(self, place, a, across):
        def body(place, a, across, out):
            out[...] = a[...] + jnp.where(inner_place(place), across[...], 0.0)

        return self.call(body, (place,), (1,), [self.dense_spec()] * 2, (a, across), self.dense_spec(), self.dense())

    def fetched(self, count):
        return [pltpu.VMEM((count, self.cap, TB, TB), F32), pltpu.SemaphoreType.DMA((count,))]

    def fetch(self, tiles, buffer, sems, index, slot):
        return pltpu.make_async_copy(tiles.at[index], buffer.at[slot], sems.at[slot])

    def tiles_spec(self):
        return pl.BlockSpec(memory_space=pl.ANY)

    def first_slots(self, role, place, cols, feats, tiles):
        groups = 4
        per_group = self.cap // groups

        def body(place, cols, feats, tiles, out, done, held, buffer, sems):
            done[...] = jnp.zeros_like(done)
            owned_by = owner(role, place[0]) * 2 + 1 - place[1]
            copies = [pltpu.make_async_copy(feats, held, sems.at[groups])]
            for g in range(groups):
                some = pl.ds(g * per_group, per_group)
                copies.append(pltpu.make_async_copy(tiles.at[owned_by, some], buffer.at[some], sems.at[g]))
            for copy in copies:
                copy.start()
            for g in range(groups):
                if g == 0:
                    copies[0].wait()
                copies[1 + g].wait()
                for c in range(g * per_group, (g + 1) * per_group):
                    out[c] = times_tile_t(held[:, lanes(cols[owned_by, c])], buffer[c])

        return self.call(
            body, (place, cols), (1,), [self.tiles_spec()] * 2, (feats, tiles), [self.slots_spec(), self.full(8, TB)],
            [self.slots(), jax.ShapeDtypeStruct((8, TB), F32)],
            scratch=[
                pltpu.VMEM((self.slices, self.owned), F32),
                pltpu.VMEM((self.cap, TB, TB), F32),
                pltpu.SemaphoreType.DMA((groups + 1,)),
            ],
            vmem=FIRST_VMEM_BYTES,
        )[0]

    def later_slots(self, roles, place, cols, feats, tiles):
        def body(place, cols, feats, tiles, *rest):
            outs, (buffer, sems) = rest[: len(roles)], rest[len(roles) :]
            owners = [owner(role, place[0]) * 2 + 1 - place[1] for role in roles]
            copies = [self.fetch(tiles, buffer, sems, owned_by, i) for i, owned_by in enumerate(owners)]
            for copy in copies:
                copy.start()
            for i, owned_by in enumerate(owners):
                copies[i].wait()
                for c in range(self.cap):
                    outs[i][c] = times_tile_t(feats[:, lanes(cols[owned_by, c])], buffer[i, c])

        return self.call(
            body, (place, cols), (1,), [self.full(self.slices, self.owned), self.tiles_spec()], (feats, tiles),
            [self.slots_spec()] * len(roles), [self.slots()] * len(roles), scratch=self.fetched(len(roles)),
        )

    def dense_sums(self, role, place, cols, rows, feats, tiles, slots):
        def body(place, cols, rows, feats, tiles, slots, *rest):
            outs, (buffer, sems) = rest[:CHUNKS], rest[CHUNKS:]
            z, x = place[0], place[1]
            owned_by = owner(role, z) * 2 + x
            copy = self.fetch(tiles, buffer, sems, owned_by, 0)
            copy.start()
            for out in outs:
                out[...] = jnp.zeros_like(out)

            def add(row, value):
                chunk, spot = self.spot(row)
                for k, out in enumerate(outs):
                    out[spot] += jnp.where((row >= 0) & (chunk == k), value, 0.0)

            for c in range(self.cap):
                add(rows[self.row_index(role, z, 1 - x), c], slots[c])
            copy.wait()
            for c in range(self.cap):
                value = times_tile_t(feats[:, lanes(cols[owned_by, c])], buffer[0, c])
                add(rows[self.row_index(role, z, x), c], value)

        return self.call(
            body, (place, cols, rows), (1,),
            [self.full(self.slices, self.owned), self.tiles_spec(), self.slots_spec()], (feats, tiles, slots),
            [self.dense_spec()] * CHUNKS, [self.dense()] * CHUNKS, scratch=self.fetched(1),
        )

    def stacked_tables(self, first, second):
        def body(first, second, out):
            out[: first.shape[0], :] = first[...]
            out[first.shape[0] :, :] = second[...]

        shape = (2 * first.shape[0], first.shape[1])
        return self.call(
            body, (), (1,), [self.full(*first.shape)] * 2, (first, second), self.full(*shape),
            jax.ShapeDtypeStruct(shape, first.dtype),
        )

    def own_rows(self, place, pair, other_pair):
        half = pair.shape[0] // 2

        def body(place, pair, other, out):
            for distance in range(4):
                table = (pair, other)[distance // 2]
                start = half * (distance % 2) + 2 * place[0]
                out[2 * distance : 2 * distance + 2, :] = table[pl.ds(start, 2), :]

        shape = (half, pair.shape[1])
        return self.call(
            body, (place,), (1,), [self.full(*pair.shape)] * 2, (pair, other_pair), self.full(*shape),
            jax.ShapeDtypeStruct(shape, pair.dtype),
        )

    def row_index(self, role, z, sender_x):
        return (owner(role, z) ^ z) * 2 + sender_x

    def means(self, k, place, pieces, inverse):
        def body(place, own, near, across, inverse, out):
            for part in range(self.parts):
                for j in range(self.per_piece):
                    spot, block = part * self.per_piece + j, self.block(k, part, j)
                    total = own[spot] + near[spot] + jnp.where(inner_place(place), across[spot], 0.0)
                    out[spot] = total * inverse[block : block + 1, :]

        return self.call(
            body, (place,), (1,), [self.dense_spec()] * 3 + [self.full(self.blocks, TB)], (*pieces, inverse),
            self.dense_spec(), self.dense(),
        )

    def loaded(self, feats, tiles, cotangent):
        def body(feats, tiles, cotangent, feats_out, tiles_out, cotangent_out, sems):
            copies = [
                pltpu.make_async_copy(feats, feats_out, sems.at[0]),
                pltpu.make_async_copy(tiles, tiles_out, sems.at[1]),
            ]
            for copy in copies:
                copy.start()
            cotangent_out[...] = cotangent[...].T
            for copy in copies:
                copy.wait()

        rows, cols = cotangent.shape
        anywhere = pl.BlockSpec(memory_space=pl.ANY)
        return self.call(
            body, (), (1,), [anywhere, anywhere, self.full(rows, cols)], (feats, tiles, cotangent),
            [anywhere, anywhere, self.full(cols, rows)],
            [pltpu.VMEM(feats.shape, F32), pltpu.VMEM(tiles.shape, F32), jax.ShapeDtypeStruct((cols, rows), F32)],
            scratch=[pltpu.SemaphoreType.DMA((2,))],
        )

    def copied(self, table):
        def body(table, out):
            out[...] = table[...]

        spec = self.full(*table.shape)
        return self.call(body, (), (1,), [spec], (table,), spec, jax.ShapeDtypeStruct(table.shape, table.dtype))

    def feats_of(self, place):
        y, core = place[2], place[3]
        return (2 * y + core, 2 * (1 - y) + core, 2 * y + 1 - core, 2 * (1 - y) + 1 - core)

    def times_weight(self, weight_t, high, low):
        rows = weight_t.shape[0]
        weight_high, weight_low = split(weight_t)
        out = dot_nn(jnp.concatenate([weight_high, weight_low], 0), high)
        return out[:rows] + out[rows:] + dot_nn(weight_high, low)

    def self_part(self, place, slices, w_self, bias):
        def body(place, own, far, core, both, w_self, bias, out, held):
            for index, piece in zip(self.feats_of(place), (own, far, core, both)):
                held[pl.ds(pl.multiple_of(index * self.slices, self.slices), self.slices), :] = piece[...]
            column = jnp.broadcast_to(bias[...], (TB, self.width)).T
            value = self.times_weight(w_self[...].T, *split(held[...]))
            out[0] = value + jnp.concatenate([column] * self.per_piece, 1)

        columns = pl.BlockSpec((self.slices, self.piece), lambda k, part, *_: (0, part * CHUNKS + k))
        return self.call(
            body, (place,), (CHUNKS, self.parts),
            [columns] * 4 + [self.full(self.width, self.width), self.full(1, self.width)], (*slices, w_self, bias),
            pl.BlockSpec((1, self.width, self.piece), lambda k, part, *_: (k, 0, part)),
            jax.ShapeDtypeStruct((CHUNKS, self.width, self.span), F32),
            scratch=[pltpu.VMEM((self.width, self.piece), F32)],
        )

    def activate(self, k, place, means, w_neigh, self_part, cotangents, inverse, activated):
        rows = pl.BlockSpec((self.piece, self.width), lambda *_: (k, 0))

        def body(place, m0, m1, m2, m3, weight, self_part, c0, c1, c2, c3, inverse, *rest):
            out, grad, back, high, low = rest[-5:]
            feats = self.feats_of(place)
            for index, piece in zip(feats, (m0, m1, m2, m3)):
                at = pl.ds(pl.multiple_of(index * self.slices, self.slices), self.slices)
                for spot in range(self.per_chunk):
                    columns = slice(spot * TB, (spot + 1) * TB)
                    high[at, columns], low[at, columns] = split(piece[spot])
            weight_t = weight[...].T
            own_rows = weight[pl.ds(pl.multiple_of(feats[0] * self.slices, self.slices), self.slices), :]
            for part, cotangent in zip(feats, (c0, c1, c2, c3)):
                at = pl.ds(pl.multiple_of(part * self.piece, self.piece), self.piece)
                pre = self.times_weight(weight_t, high[:, at], low[:, at]) + self_part[0, :, at]
                sigma = jax.nn.sigmoid(pre)
                if cotangent is c0:
                    out[...] = (pre * sigma).T
                slope = cotangent[...] * (sigma * (1.0 + pre * (1.0 - sigma)))
                grad[:, at] = slope
                value = self.times_weight(own_rows, *split(slope))
                for j in range(self.per_piece):
                    scale = inverse[pl.ds(self.block(k, part, j), 1), :]
                    back[part * self.per_piece + j] = value[:, j * TB : (j + 1) * TB] * scale

        in_specs = (
            [self.dense_spec()] * 4
            + [self.full(self.width, self.width)]
            + [pl.BlockSpec((1, self.width, self.span), lambda *_: (k, 0, 0))]
            + [pl.BlockSpec((self.width, self.piece), lambda *_: (0, k))] * 4
            + [self.full(self.blocks, TB)]
        )
        args = [*means, w_neigh, self_part, *cotangents, inverse]
        aliases = {}
        if activated is not None:
            aliases = {1 + len(args): 0}
            in_specs.append(pl.BlockSpec(memory_space=pl.ANY))
            args.append(activated)
        return self.call(
            body, (place,), (1,), in_specs, args,
            [rows, self.full(self.width, self.span), self.dense_spec()],
            [jax.ShapeDtypeStruct((self.per_part * TB, self.width), F32),
             jax.ShapeDtypeStruct((self.width, self.span), F32), self.dense()],
            scratch=[pltpu.VMEM((self.width, self.span), BF16)] * 2, aliases=aliases,
        )

    def weight_grad(self, k, place, w_self, feats, means, grad, before):
        shape = (2 * self.slices + 16, self.width)

        def body(place, w_self, feats, means, grad, *rest):
            self_out, weights_out = rest[-2:]
            total = rest[0][...] if before is not None else jnp.zeros(shape, F32)
            for part in range(self.parts):
                first = part * self.per_piece
                at = slice(part * self.piece, (part + 1) * self.piece)
                high, low = split(grad[:, at])
                value = self.times_weight(w_self[...], high, low)
                for j in range(self.per_piece):
                    self_out[first + j] = value[:, j * TB : (j + 1) * TB]
                start = self.block(k, part, 0) * TB
                rows = jnp.concatenate(
                    [
                        feats[:, start : start + self.piece],
                        jnp.concatenate([means[first + j] for j in range(self.per_piece)], 1),
                        jnp.ones((16, self.piece), F32),
                    ],
                    0,
                )
                rows_high, rows_low = split(rows)
                total += (dot_nt(rows_high, high) + dot_nt(rows_low, high)) + dot_nt(rows_high, low)
            weights_out[...] = total

        weight_rows = pl.BlockSpec((self.slices, self.width), lambda i, place, *_: (2 * place[2] + place[3], 0))
        args = [w_self, feats, means, grad] + ([] if before is None else [before])
        return self.call(
            body, (place,), (1,),
            [weight_rows, self.full(self.slices, self.owned), self.dense_spec(), self.full(self.width, self.span)]
            + [self.full(*shape)] * (before is not None),
            args, [self.dense_spec(), self.full(*shape)], [self.dense(), jax.ShapeDtypeStruct(shape, F32)],
        )

    def both_cores(self, place, mine, other):
        def body(place, mine, other, out):
            out[place[3]] = mine[...]
            out[1 - place[3]] = other[...]

        shape = (2, *mine.shape)
        return self.call(
            body, (place,), (1,), [self.full(*mine.shape)] * 2, (mine, other), self.full(*shape),
            jax.ShapeDtypeStruct(shape, F32),
        )

    def whole_weights(self, place, mine, other):
        def body(place, mine, other, w_self, w_neigh, bias):
            for y, block in ((place[2], mine), (1 - place[2], other)):
                for core in range(2):
                    at = pl.ds(pl.multiple_of((2 * y + core) * self.slices, self.slices), self.slices)
                    w_self[at, :] = block[core, : self.slices, :]
                    w_neigh[at, :] = block[core, self.slices : 2 * self.slices, :]
            bias[...] = mine[0, 2 * self.slices : 2 * self.slices + 1, :]

        square, row = (self.width, self.width), (1, self.width)
        return self.call(
            body, (place,), (1,), [self.full(*mine.shape)] * 2, (mine, other),
            [self.full(*square), self.full(*square), self.full(*row)],
            [jax.ShapeDtypeStruct(shape, F32) for shape in (square, square, row)],
        )

    def gather(self, place, sources, held):
        inner = inner_place(place)
        for k in range(CHUNKS):
            spots = slice(k * self.per_chunk, (k + 1) * self.per_chunk)
            if len(sources) == CHUNKS:
                held[spots] = sources[k][...]
            else:

                @pl.when(jnp.logical_not(inner))
                def _():
                    held[spots] = sources[CHUNKS + k][...]

                @pl.when(inner)
                def _():
                    held[spots] = sources[k][...]

    def held(self):
        return pltpu.VMEM((self.blocks, self.slices, TB), F32)

    def pick(self, row, held):
        chunk, spot = self.spot(row)
        return jnp.where(row >= 0, held[chunk * self.per_chunk + spot], 0.0)

    def picked(self, role, place, rows, sources):
        def body(place, rows, *rest):
            out, held = rest[-2:]
            self.gather(place, rest[:-2], held)
            row_of = self.row_index(role, place[0], 1 - place[1])
            for c in range(self.cap):
                out[c] = self.pick(rows[row_of, c], held)

        return self.call(
            body, (place, rows), (1,), [self.dense_spec()] * len(sources), sources,
            self.slots_spec(), self.slots(), scratch=[self.held()],
        )

    def spread(self, place, cols, rows, tiles, jobs, total=None, self_back=None, last=False):
        counts = [len(sources) for _, sources in jobs]
        extra = [total] if self_back is None else list(self_back)

        def body(place, cols, rows, tiles, *rest):
            arrays, more = rest[: sum(counts)], rest[sum(counts) : sum(counts) + len(extra)]
            out, done, held, buffer, sems = rest[sum(counts) + len(extra) :]
            done[...] = jnp.zeros_like(done)
            z, x = place[0], place[1]
            owners = [owner(role, z) * 2 + (1 - x if n == 1 else x) for (role, _), n in zip(jobs, counts)]
            copies = [self.fetch(tiles, buffer, sems, owned_by, i) for i, owned_by in enumerate(owners)]
            for copy in copies:
                copy.start()
            if self_back is None:
                out[...] = more[0][...]
            else:
                for k, back in enumerate(more):
                    for part in range(self.parts):
                        for j in range(self.per_piece):
                            block = self.block(k, part, j)
                            out[:, block * TB : (block + 1) * TB] = back[part * self.per_piece + j]
            for i, (role, _) in enumerate(jobs):
                sources = arrays[sum(counts[:i]) : sum(counts[: i + 1])]
                if counts[i] > 1:
                    self.gather(place, sources, held)
                copies[i].wait()
                for c in range(self.cap):
                    if counts[i] > 1:
                        value = self.pick(rows[self.row_index(role, z, x), c], held)
                    else:
                        value = sources[0][c]
                    out[:, lanes(cols[owners[i], c])] += times_tile(value, buffer[i, c])

        shape = (self.slices, self.owned)
        whole = self.full(*shape)
        in_specs, args = [self.tiles_spec()], [tiles]
        for _, sources in jobs:
            in_specs += [self.slots_spec() if len(sources) == 1 else self.dense_spec()] * len(sources)
            args += sources
        in_specs += [whole] if self_back is None else [self.dense_spec()] * CHUNKS
        args += extra
        return self.call(
            body, (place, cols, rows), (1,), in_specs, args, [whole, self.full(8, TB)],
            [
                jax.ShapeDtypeStruct(shape, F32) if last else pltpu.VMEM(shape, F32),
                jax.ShapeDtypeStruct((8, TB), F32),
            ],
            scratch=[self.held(), *self.fetched(len(jobs))],
            aliases={} if last or self_back is not None else {3 + len(args) - 1: 0},
        )[0]


def pairs_z(steps):
    return [(2 * a + x, 2 * b + x) for a, b in steps for x in range(2)]


ACROSS = pairs_z([(1, 2), (2, 1), (0, 0), (3, 3)])
OUTWARD = pairs_z([(1, 0), (2, 3)])
OTHER_X = [(n, n ^ 1) for n in range(8)]
OTHER_CORE = [(f, f ^ 1) for f in range(4)]
OTHER_Y = [(f, f ^ 2) for f in range(4)]


def along_z(distance):
    return pairs_z([(z, z ^ distance) for z in range(4)])


def node_swap(value, pairs):
    return lax.ppermute(value, "node", pairs)


def feat_swap(value, pairs):
    return lax.ppermute(value, "feat", pairs)


ORDER = [
    ("slots_first",),
    ("table_out",),
    ("load",),
    ("tables_out",),
    ("slots_later",),
    ("rows_in",),
    ("dense", FAR_OUTER),
    ("slots", FAR_INNER),
    ("send_in", FAR_OUTER, 1),
    ("pass_on", FAR_OUTER, 0),
    ("slots", NEAR),
    ("dense", FAR_INNER),
    ("pass_on", FAR_OUTER, 1),
    ("send_in", FAR_INNER, 1),
    ("dense", NEAR),
    ("pass_on", NEAR, 0),
    ("slots", SELF),
    ("pass_on", FAR_INNER, 0),
    ("pass_on", NEAR, 1),
    ("cotangents_on",),
    ("feats_on",),
    ("pass_on", FAR_INNER, 1),
    ("dense", SELF),
    ("mean", 0),
    ("mean", 1),
    ("means_on", 0),
    ("self_part",),
    ("means_on", 1),
    ("activate", 0),
    ("activate", 1),
    ("weight", 0),
    ("near_on", 0),
    ("weight", 1),
    ("inner_on", 0),
    ("pick", SELF),
    ("wait", "near", 1),
    ("wait", "inner", 1, 0),
    ("inner_on", 1),
    ("near_on", 1),
    ("pick", NEAR),
    ("weight_sum", along_z(1)),
    ("wait", "inner", 0, 1),
    ("outer_on", 0),
    ("wait", "inner", 1, 1),
    ("spread", SELF, None),
    ("wait", "outer", 1, 0),
    ("wait", "returned", SELF),
    ("weight_sum", along_z(3)),
    ("pick", FAR_INNER),
    ("outer_on", 1),
    ("spread", NEAR, SELF),
    ("wait", "returned", NEAR),
    ("wait", "outer", 0, 1),
    ("weight_sum", None),
    ("spread", FAR_INNER, NEAR),
    ("wait", "returned", FAR_INNER),
    ("weight_cores",),
    ("pick", FAR_OUTER),
    ("spread", FAR_OUTER, FAR_INNER),
    ("wait", "weights_in"),
    ("weight_whole",),
    ("spread", None, FAR_OUTER),
]


class Steps:
    def __init__(self, layer, place, node_feats, tiles, send_col, recv_row, inverse, w_self, w_neigh, bias, cotangent):
        self.layer, self.place, self.feats, self.tiles = layer, place, node_feats, tiles
        self.cols, self.table, self.inverse = send_col, recv_row, inverse
        self.w_self, self.w_neigh, self.bias, self.cotangent = w_self, w_neigh, bias, cotangent
        self.slots_in, self.joined, self.inward, self.returned = {}, {}, {}, {}
        self.across, self.nearby, self.means, self.mean_parts = {}, {}, {}, {}
        self.grads, self.own, self.near, self.inner, self.outer = {}, {}, {}, {}, {}
        self.self_back, self.activated, self.weights, self.total = {}, None, None, None

    def wait(self, name, *key):
        held = getattr(self, name)
        for index in key:
            held = held[index]
        self.layer.pending.append(held)

    def slots_first(self):
        part = self.layer.first_slots(FAR_OUTER, self.place, self.cols, self.feats, self.tiles)
        self.slots_in[FAR_OUTER] = node_swap(part, OTHER_X)

    def slots_later(self):
        self.parts = self.layer.later_slots((FAR_INNER, NEAR, SELF), self.place, self.cols, self.feats, self.tiles)

    def slots(self, role):
        part = self.layer.relay(self.parts[role - 1], after=[self.slots_in[role - 1]])
        self.slots_in[role] = node_swap(part, OTHER_X)

    def table_out(self):
        self.table = self.layer.copied(self.table)
        self.table_in = node_swap(self.table, along_z(1))

    def tables_out(self):
        self.tables = self.layer.stacked_tables(self.table, self.table_in)
        self.tables_in = node_swap(self.tables, along_z(2))

    def rows_in(self):
        self.rows = self.layer.own_rows(self.place, self.tables, self.tables_in)

    def load(self):
        feats, self.tiles, cotangent = self.layer.loaded(self.feats, self.tiles, self.cotangent)
        self.feats = feats
        self.feat_parts = [feats, feat_swap(feats, OTHER_Y), feat_swap(feats, OTHER_CORE)]
        self.cotangents = [cotangent, feat_swap(cotangent, OTHER_Y), feat_swap(cotangent, OTHER_CORE)]

    def on(self, parts):
        parts[1] = self.layer.relay(parts[1])
        parts.append(feat_swap(parts[1], OTHER_CORE))

    def feats_on(self):
        self.on(self.feat_parts)

    def cotangents_on(self):
        self.on(self.cotangents)

    def self_part(self):
        self.self_parts = self.layer.self_part(self.place, self.feat_parts, self.w_self, self.bias)

    def dense(self, role):
        sums = self.layer.dense_sums(
            role, self.place, self.cols, self.rows, self.feats, self.tiles, self.slots_in[role]
        )
        for k in range(CHUNKS):
            self.joined[role, k] = sums[k]
        if role in (FAR_OUTER, FAR_INNER):
            self.inward[role, 0] = node_swap(sums[0], along_z(1))

    def send_in(self, role, k):
        self.joined[role, k] = self.layer.relay(self.joined[role, k])
        self.inward[role, k] = node_swap(self.joined[role, k], along_z(1))

    def pass_on(self, role, k):
        if role == NEAR:
            part = self.layer.added_across(self.place, self.joined[NEAR, k], self.across[FAR_OUTER, k])
            self.nearby[k] = node_swap(part, along_z(1))
        else:
            part = self.layer.added(self.joined[role, k], self.inward[role, k])
            self.across[role, k] = node_swap(part, ACROSS)

    def mean(self, k):
        pieces = (self.joined[SELF, k], self.nearby[k], self.across[FAR_INNER, k])
        means = self.layer.means(k, self.place, pieces, self.inverse)
        self.means[k] = means
        self.mean_parts[k] = [means, feat_swap(means, OTHER_Y), feat_swap(means, OTHER_CORE)]

    def means_on(self, k):
        self.on(self.mean_parts[k])

    def activate(self, k):
        self.activated, self.grads[k], back = self.layer.activate(
            k, self.place, self.mean_parts[k], self.w_neigh, self.self_parts, self.cotangents, self.inverse, self.activated
        )
        self.own[k] = back
        self.near[k] = node_swap(back, along_z(1))
        self.inner[k] = [node_swap(back, ACROSS)]

    def near_on(self, k):
        self.near[k] = self.layer.relay(self.near[k])
        self.outer[k] = [node_swap(self.near[k], ACROSS)]

    def inner_on(self, k):
        self.inner[k][0] = self.layer.relay(self.inner[k][0])
        self.inner[k].append(node_swap(self.inner[k][0], OUTWARD))

    def outer_on(self, k):
        self.outer[k][0] = self.layer.relay(self.outer[k][0])
        self.outer[k].append(node_swap(self.outer[k][0], OUTWARD))

    def weight(self, k):
        back, weights = self.layer.weight_grad(
            k, self.place, self.w_self, self.feats, self.means[k], self.grads[k], self.weights
        )
        self.self_back[k] = back
        self.weights = weights
        if k == CHUNKS - 1:
            self.weights_in = node_swap(weights, OTHER_X)

    def weight_sum(self, pairs):
        self.weights = self.layer.added(self.weights, self.weights_in)
        if pairs is None:
            self.weights_in = feat_swap(self.weights, OTHER_CORE)
        else:
            self.weights_in = node_swap(self.weights, pairs)

    def weight_cores(self):
        self.weights = self.layer.both_cores(self.place, self.weights, self.weights_in)
        self.weights_in = feat_swap(self.weights, OTHER_Y)

    def weight_whole(self):
        self.weights = self.layer.whole_weights(self.place, self.weights, self.weights_in)

    def sources(self, role):
        if role in (SELF, NEAR):
            return [(self.own if role == SELF else self.near)[k] for k in range(CHUNKS)]
        held = self.inner if role == FAR_INNER else self.outer
        return [held[k][0] for k in range(CHUNKS)] + [held[k][1] for k in range(CHUNKS)]

    def pick(self, role):
        self.returned[role] = node_swap(self.layer.picked(role, self.place, self.rows, self.sources(role)), OTHER_X)

    def spread(self, local, slots):
        jobs = [] if local is None else [(local, self.sources(local))]
        jobs += [] if slots is None else [(slots, [self.returned[slots]])]
        first = self.total is None
        back = [self.self_back[k] for k in range(CHUNKS)] if first else None
        self.total = self.layer.spread(
            self.place, self.cols, self.rows, self.tiles, jobs, self.total, back, last=local is None
        )


def chain_shards(node_feats, tiles, send_col, recv_row, degree, w_self, w_neigh, bias, cotangent):
    slices, owned = node_feats.shape
    width = w_self.shape[1]
    layer = Layer(slices, owned, tiles.shape[1], 4, width)
    node, feat = lax.axis_index("node"), lax.axis_index("feat")
    place = jnp.stack([node // 2, node % 2, feat // 2, feat % 2]).astype(jnp.int32)
    inverse = (1.0 / degree.astype(F32)).reshape(-1, TB)
    steps = Steps(
        layer, place, node_feats, tiles, send_col, recv_row, inverse, w_self, w_neigh, bias.reshape(1, width), cotangent
    )
    for name, *arguments in ORDER:
        getattr(steps, name)(*arguments)
    grad_self, grad_neigh, grad_bias = steps.weights
    return (steps.activated, steps.total, grad_self, grad_neigh, grad_bias.reshape(width))


def slot_shards(node_feats, tiles, send_col, recv_row, degree, w_self, w_neigh, bias, cotangent):
    slices, owned = node_feats.shape
    blocks = owned // TB
    block_ids = jnp.arange(blocks, dtype=jnp.int32)
    scale = degree.astype(F32)[None, :]
    col_onehot = (send_col[..., None] == block_ids).astype(F32)
    row_onehot = (recv_row[..., None] == block_ids).astype(F32)
    feat_blocks = node_feats.reshape(slices, blocks, TB)
    picked = jnp.einsum("dcb,fbj->dcfj", col_onehot, feat_blocks, precision=HIGH)
    partial_value = jnp.einsum("dcfj,dcij->dcfi", picked, tiles, precision=HIGH)
    arrived = lax.all_to_all(partial_value, "node", split_axis=0, concat_axis=0, tiled=True)
    summed = jnp.einsum("scfi,scb->fbi", arrived, row_onehot, precision=HIGH)
    neighbour = summed.reshape(slices, owned) / scale
    offset = lax.axis_index("feat") * slices
    self_rows = lax.dynamic_slice_in_dim(w_self, offset, slices, 0)
    neigh_rows = lax.dynamic_slice_in_dim(w_neigh, offset, slices, 0)
    dims = (((0,), (0,)), ((), ()))
    first = lax.dot_general(node_feats, self_rows, dims, precision=HIGH)
    second = lax.dot_general(neighbour, neigh_rows, dims, precision=HIGH)
    pre = lax.psum_scatter(first + second, "feat", scatter_dimension=0, tiled=True) + bias
    sigma = jax.nn.sigmoid(pre)
    activated = pre * sigma
    gpre = cotangent * sigma * (1.0 + pre * (1.0 - sigma))
    piece = lax.all_gather(gpre, "feat", axis=0, tiled=True)
    dims = (((1,), (1,)), ((), ()))
    self_back = lax.dot_general(self_rows, piece, dims, precision=HIGH)
    neigh_back = lax.dot_general(neigh_rows, piece, dims, precision=HIGH)
    slice_self = jnp.dot(node_feats, piece, precision=HIGH)
    slice_neigh = jnp.dot(neighbour, piece, precision=HIGH)
    sums = lax.psum((slice_self, slice_neigh, jnp.sum(piece, axis=0)), "node")
    grad_self, grad_neigh = (lax.all_gather(part, "feat", axis=0, tiled=True) for part in sums[:2])
    gneigh = (neigh_back / scale).reshape(slices, blocks, TB)
    outgoing = jnp.einsum("scb,fbi->scfi", row_onehot, gneigh, precision=HIGH)
    returned = lax.all_to_all(outgoing, "node", split_axis=0, concat_axis=0, tiled=True)
    spread = jnp.einsum("dcfi,dcij->dcfj", returned, tiles, precision=HIGH)
    placed = jnp.einsum("dcfj,dcb->fbj", spread, col_onehot, precision=HIGH)
    grad_feats = self_back + placed.reshape(slices, owned)
    return (activated, grad_feats, grad_self, grad_neigh, sums[2])


def solution(mesh):
    chain = mesh.shape["node"] == 8 and mesh.shape["feat"] == 4
    return jax.shard_map(
        chain_shards if chain else slot_shards,
        mesh=mesh,
        in_specs=(
            P("feat", "node"),
            P("node", None, None, None),
            P("node", None),
            P("node", None),
            P("node"),
            P(),
            P(),
            P(),
            P(("node", "feat"), None),
        ),
        out_specs=(P(("node", "feat"), None), P("feat", "node"), P(), P(), P()),
        check_vma=False,
    )
```
